128 devices in a mesh: group: 64 (over z, y, x), local: 2 (over core).
Axes of the slice: x: 4, y: 4, z: 4, core: 2. Of those that a mesh axis runs over, the one named last changes fastest.
Arguments:
- tokens: bfloat16 [65536, 2048], P(('group', 'local')), may hold values from -6 to 6
- cotangent: bfloat16 [65536, 2048], P(('group', 'local')), may hold values from -6 to 6
- row_slot: int32 [65536], P(('group', 'local')), may hold values from 0 to 1
- placement: int32 [64, 2], replicated, may hold values from 0 to 7, as said below
- master: float32 [8, 3, 384, 2048], P(None, None, 'group', 'local'), may hold values from -0.125 to 0.125
- first_moment: float32 [8, 3, 384, 2048], P(None, None, 'group', 'local'), may hold values from -2 to 2
- second_moment: float32 [8, 3, 384, 2048], P(None, None, 'group', 'local'), may hold values from 1 to 1000
Outputs:
- layer_out: bfloat16 [65536, 2048], P(('group', 'local'))
- input_grad: bfloat16 [65536, 2048], P(('group', 'local'))
- new_master: float32 [8, 3, 384, 2048], P(None, None, 'group', 'local')
- new_first: float32 [8, 3, 384, 2048], P(None, None, 'group', 'local')
- new_second: float32 [8, 3, 384, 2048], P(None, None, 'group', 'local')
The draws below stay inside these ranges and needn't reach their ends.
Inputs may be any that keep to these rules, and one draw needn't show every extreme that they name: `placement`: the 2 slots of a group name different experts; every expert is named by at least one slot.
All inputs are finite; a program needn't handle non-finite values.
Results may differ from the reference program's by a relative error of at most 0.0071.
Values may be sent and summed in bfloat16 or wider, within the bound.
No kernel may reach another device: no remote copies, remote signals or barrier semaphores. Data moves between devices by JAX's collectives and lax.ppermute only.
A program may use at most 128 MiB of HBM per device.

```python
import math
import jax
import jax.numpy as jnp
from jax import lax

D = 2048
H = 384
E = 8
SLOTS = 2
ROWS = 512
TOKENS = 65536
N_GROUP = 64
N_LOCAL = 2


def draw_placement(key, part):
    key = jax.random.fold_in(key, 11)
    keys = jax.random.split(key, 6)
    cover = jax.random.permutation(keys[0], E)
    pick = jnp.minimum(jax.random.randint(keys[1], (N_GROUP - E,), 0, E), jax.random.randint(keys[2], (N_GROUP - E,), 0, E))
    relabel = jax.random.permutation(keys[3], E)
    extra = relabel[pick]
    first = jax.random.permutation(keys[4], jnp.concatenate([cover, extra]))
    offset = jax.random.randint(keys[5], (N_GROUP,), 1, E)
    second = (first + offset) % E
    return jnp.stack([first, second], 1).astype(jnp.int32)


def with_ends(values, own_key, low, top_value):
    index_at = [jax.random.randint(jax.random.fold_in(own_key, axis), (), 0, length) for axis, length in enumerate(values.shape)]
    widest = values.shape.index(max(values.shape))
    beside = index_at[:widest] + [(index_at[widest] + 1) % values.shape[widest]] + index_at[widest + 1:]
    return values.at[tuple(index_at)].set(low).at[tuple(beside)].set(top_value)


def shard_levels(rng, extent, pieces, least, high):
    gain, own = 1.0, jax.random.fold_in(rng, 6)
    for dim, blocks in pieces:
        draws = jnp.exp(jax.random.uniform(jax.random.fold_in(own, dim), (blocks,), jnp.float32, least / len(pieces), high / len(pieces)))
        gain = gain * jnp.repeat(draws, extent[dim] // blocks).reshape([-1 if axis == dim else 1 for axis in range(len(extent))])
    return gain


def noise(rng, dims, scale, limit, pieces=(), kind=jnp.bfloat16):
    loudness = shard_levels(rng, dims, pieces, -0.22, 0.18) if pieces else 1.0
    drawn = jax.random.normal(rng, dims, jnp.float32) * scale * loudness
    return jnp.minimum(jnp.maximum(drawn, -limit), limit).astype(kind)


def setup_inputs(seed: int = 0) -> dict:
    key_list = jax.random.split(jax.random.key(seed), 8)
    return {
        "tokens": noise(key_list[0], (TOKENS, D), 1.0, 6.0, ((0, 128),)),
        "cotangent": noise(key_list[1], (TOKENS, D), 1.0, 6.0, ((0, 128),)),
        "row_slot": with_ends(jax.random.randint(key_list[2], (TOKENS,), 0, SLOTS), jax.random.fold_in(key_list[2], 1), 0, SLOTS - 1).astype(jnp.int32),
        "placement": draw_placement(jax.random.fold_in(key_list[7], 71), 0),
        "master": noise(key_list[4], (E, 3, H, D), D ** -0.5, 0.125, ((2, 64), (3, 2)), jnp.float32),
        "first_moment": noise(key_list[5], (E, 3, H, D), 0.3, 2.0, ((2, 64), (3, 2)), jnp.float32),
        "second_moment": jnp.clip(jnp.exp(math.log(1000.0) - 6.9077553 * jax.random.uniform(key_list[6], (E, 3, H, D), jnp.float32) ** shard_levels(key_list[6], (E, 3, H, D), ((2, 64), (3, 2)), -0.2, 0.2)), 1.0, 1000.0),
    }


loss_scale = 4.0
beta_first = 0.9
beta_second = 0.95
learn_rate = 0.001
adam_epsilon = 1e-08
bias_first = 1.0 - 0.9 ** 10
bias_second = 1.0 - 0.95 ** 10

def reference(tokens, cotangent, row_slot, placement, master, first_moment, second_moment):
    rows_group = ROWS * N_LOCAL
    tok_groups = tokens.reshape(N_GROUP, rows_group, D)
    cot_groups = cotangent.reshape(N_GROUP, rows_group, D)
    slot_groups = row_slot.reshape(N_GROUP, rows_group)

    def group_step(grads, inputs):
        tok_rows, cot_rows, slot_rows, places = inputs
        out_sum = jnp.zeros((rows_group, D), jnp.float32)
        in_sum = jnp.zeros((rows_group, D), jnp.float32)
        for slot_index in range(SLOTS):
            expert = places[slot_index]
            weights = master[expert].astype(jnp.bfloat16)
            chosen = (slot_rows == slot_index)[:, None]
            gate_pre = jnp.dot(tok_rows, weights[0].T, preferred_element_type=jnp.float32)
            up_pre = jnp.dot(tok_rows, weights[1].T, preferred_element_type=jnp.float32)
            hidden = (jax.nn.silu(gate_pre) * up_pre).astype(jnp.bfloat16)
            masked = jnp.where(chosen, hidden, jnp.zeros_like(hidden))
            out_sum = out_sum + jnp.dot(masked, weights[2], preferred_element_type=jnp.float32)
            masked_cot = jnp.where(chosen, cot_rows, jnp.zeros_like(cot_rows))
            d_hidden = jnp.dot(masked_cot, weights[2].T, preferred_element_type=jnp.float32)
            sigmoid_gate = jax.nn.sigmoid(gate_pre)
            d_gate = (d_hidden * up_pre * sigmoid_gate * (1.0 + gate_pre * (1.0 - sigmoid_gate))).astype(jnp.bfloat16)
            d_up = (d_hidden * gate_pre * sigmoid_gate).astype(jnp.bfloat16)
            in_sum = in_sum + jnp.dot(d_gate, weights[0], preferred_element_type=jnp.float32)
            in_sum = in_sum + jnp.dot(d_up, weights[1], preferred_element_type=jnp.float32)
            term_gate = jnp.dot(d_gate.T, tok_rows, preferred_element_type=jnp.float32)
            term_up = jnp.dot(d_up.T, tok_rows, preferred_element_type=jnp.float32)
            term_down = jnp.dot(masked.T, cot_rows, preferred_element_type=jnp.float32)
            grads = grads.at[expert].add(jnp.stack([term_gate, term_up, term_down], 0))
        return (grads, (out_sum.astype(jnp.bfloat16), in_sum.astype(jnp.bfloat16)))
    start_grads = jnp.zeros(master.shape, jnp.float32)
    grads, (outs, ins) = lax.scan(group_step, start_grads, (tok_groups, cot_groups, slot_groups, placement))
    scaled = grads / loss_scale
    new_first = beta_first * first_moment + (1.0 - beta_first) * scaled
    new_second = beta_second * second_moment + (1.0 - beta_second) * scaled * scaled
    new_master = master - learn_rate * (new_first / bias_first) / (jnp.sqrt(new_second / bias_second) + adam_epsilon)
    return (outs.reshape(TOKENS, D), ins.reshape(TOKENS, D), new_master, new_first, new_second)
```

```python
import jax
import jax.numpy as jnp
from jax import lax
from jax.sharding import PartitionSpec as P

loss_scale = 4.0
beta_first = 0.9
beta_second = 0.95
learn_rate = 0.001
adam_epsilon = 1e-08
bias_first = 1.0 - 0.9**10
bias_second = 1.0 - 0.95**10

SIDE = 4
CHAINS = 3
OFFSETS = (0, 1, 3, 2)
BOTH = ("group", "local")
AXES = ((2, 1, 0), (1, 0, 2), (0, 2, 1))


def place(coords, core):
    return ((coords[0] * SIDE + coords[1]) * SIDE + coords[2]) * 2 + core


def step_pairs(axis, offset):
    pairs = []
    for group in range(SIDE**3):
        coords = [group // 16, group // 4 % 4, group % 4]
        other = list(coords)
        other[axis] ^= offset
        for core in range(2):
            pairs.append((place(coords, core), place(other, core)))
    return pairs


CORE_PAIRS = [(i, i ^ 1) for i in range(2 * SIDE**3)]


def hop(value, axis, offset):
    return lax.ppermute(value, BOTH, step_pairs(axis, offset))


def swap(value):
    return lax.ppermute(value, BOTH, CORE_PAIRS)


def contract_last(left, right):
    return lax.dot_general(
        left, right, (((1,), (1,)), ((), ())), preferred_element_type=jnp.float32
    )


def contract_first(left, right):
    return lax.dot_general(
        left, right, (((0,), (0,)), ((), ())), preferred_element_type=jnp.float32
    )


def matmul(left, right):
    return jnp.dot(left, right, preferred_element_type=jnp.float32)


def shards(tokens, cotangent, row_slot, placement, master, first_moment, second_moment):
    group = lax.axis_index("group")
    core = lax.axis_index("local")
    coords = (group // 16, group // 4 % 4, group % 4)
    strides = (16, 4, 1)
    experts = master.shape[0]
    columns = master.shape[3]
    rows = tokens.shape[0]

    def placed(axis, offset):
        there = group + ((coords[axis] ^ offset) - coords[axis]) * strides[axis]
        pair = lax.dynamic_index_in_dim(placement, there, 0, keepdims=False)
        return pair[core], pair[1 - core]

    narrow = master.astype(jnp.bfloat16).transpose(1, 2, 0, 3)
    mine_w = []
    other_w = []
    for chain in range(CHAINS):
        axis1, axis2, axis3 = AXES[chain]
        block = narrow[:, 2 * chain : 2 * chain + 2]
        line = [block] + [hop(block, axis1, o) for o in OFFSETS[1:]]
        line = jnp.stack(line, 0)
        line = line.transpose(1, 3, 0, 2, 4).reshape(3, experts, 8, columns)
        plane = [line] + [hop(line, axis2, o) for o in OFFSETS[1:]]
        arrived = []
        for o in OFFSETS:
            picked = []
            for e in placed(axis3, o):
                picked.append(
                    jnp.stack([lax.dynamic_index_in_dim(p, e, 1, keepdims=False) for p in plane], 1)
                )
            packed = jnp.stack(picked, 0)
            arrived.append(packed if o == 0 else hop(packed, axis3, o))
        keep = jnp.stack([a[0] for a in arrived], 1).reshape(3, 128, columns)
        give = jnp.stack([a[1] for a in arrived], 1).reshape(3, 128, columns)
        mine_w.append(keep)
        other_w.append(swap(give))

    def halves(own):
        got = swap(own)
        whole = jnp.concatenate([own, got], 0).reshape(2 * rows, 2, columns)
        near = lax.dynamic_index_in_dim(whole, core, 1, keepdims=False)
        far = lax.dynamic_index_in_dim(whole, 1 - core, 1, keepdims=False)
        return near, far

    tok_near, tok_far = halves(tokens)
    cot_near, cot_far = halves(cotangent)
    slots = jnp.concatenate([row_slot, swap(row_slot)], 0)
    chosen = (slots == core)[:, None]

    hidden_list = []
    d_list = []
    sums = []
    for chain in range(CHAINS):
        wn = mine_w[chain]
        wf = other_w[chain]
        pre = contract_last(tok_near, wn[:2].reshape(256, columns)) + contract_last(
            tok_far, wf[:2].reshape(256, columns)
        )
        gate_pre = pre[:, :128]
        up_pre = pre[:, 128:]
        sigmoid_gate = jax.nn.sigmoid(gate_pre)
        hidden = jnp.where(chosen, gate_pre * sigmoid_gate * up_pre, 0.0).astype(jnp.bfloat16)
        d_hidden = contract_last(cot_near, wn[2]) + contract_last(cot_far, wf[2])
        d_hidden = jnp.where(chosen, d_hidden, 0.0)
        d_gate = d_hidden * up_pre * sigmoid_gate * (1.0 + gate_pre * (1.0 - sigmoid_gate))
        d_up = d_hidden * gate_pre * sigmoid_gate
        d_pair = jnp.concatenate([d_gate, d_up], 1).astype(jnp.bfloat16)
        hidden_list.append(hidden)
        d_list.append(d_pair)

        def term(tok, cot):
            pair = contract_first(d_pair, tok).astype(jnp.bfloat16).reshape(2, 128, columns)
            down = contract_first(hidden, cot).astype(jnp.bfloat16)[None]
            return jnp.concatenate([pair, down], 0)

        got = swap(term(tok_far, cot_far))
        own = term(tok_near, cot_near)

        axis1, axis2, axis3 = AXES[chain]
        total = jnp.zeros((3, experts, 32, columns), jnp.float32)
        names = jnp.arange(experts, dtype=jnp.int32)[None, :, None, None]
        for index, o in enumerate(OFFSETS):
            part = slice(32 * index, 32 * index + 32)
            packed = jnp.stack([own[:, part], got[:, part]], 0)
            came = packed if o == 0 else hop(packed, axis3, o)
            for k, e in enumerate(placed(axis3, o)):
                total = total + jnp.where(names == e, came[k][:, None].astype(jnp.float32), 0.0)
        total = total.astype(jnp.bfloat16)
        added = jnp.zeros((3, experts, 8, columns), jnp.float32)
        for index, o in enumerate(OFFSETS):
            part = total[:, :, 8 * index : 8 * index + 8]
            came = part if o == 0 else hop(part, axis2, o)
            added = added + came.astype(jnp.float32)
        added = added.astype(jnp.bfloat16).reshape(3, experts, 4, 2, columns).transpose(2, 0, 3, 1, 4)
        grad = jnp.zeros((3, 2, experts, columns), jnp.float32)
        for index, o in enumerate(OFFSETS):
            came = added[index] if o == 0 else hop(added[index], axis1, o)
            grad = grad + came.astype(jnp.float32)
        sums.append(grad)

    grads = jnp.concatenate(sums, 1).transpose(2, 0, 1, 3)
    scaled = grads / loss_scale
    new_first = beta_first * first_moment + (1.0 - beta_first) * scaled
    new_second = beta_second * second_moment + (1.0 - beta_second) * scaled * scaled
    new_master = master - learn_rate * (new_first / bias_first) / (
        jnp.sqrt(new_second / bias_second) + adam_epsilon
    )

    hidden = jnp.concatenate(hidden_list, 1)
    d_all = jnp.concatenate(d_list, 1)

    def weight_rows(parts, lo, hi):
        return jnp.concatenate([p[lo:hi].reshape(-1, columns) for p in parts], 0)

    def settle(near, far):
        both = jnp.stack([near, far], 1).astype(jnp.bfloat16)
        got = swap(both[rows:])
        low = jnp.where(core == 0, both[:rows, 0], both[:rows, 1])
        high = jnp.where(core == 0, both[:rows, 1], both[:rows, 0])
        got_low = jnp.where(core == 0, got[:, 1], got[:, 0])
        got_high = jnp.where(core == 0, got[:, 0], got[:, 1])
        pick = (row_slot == core)[:, None]
        return jnp.concatenate([jnp.where(pick, low, got_low), jnp.where(pick, high, got_high)], 1)

    layer_out = settle(
        matmul(hidden, weight_rows(mine_w, 2, 3)), matmul(hidden, weight_rows(other_w, 2, 3))
    )
    input_grad = settle(
        matmul(d_all, weight_rows(mine_w, 0, 2)), matmul(d_all, weight_rows(other_w, 0, 2))
    )
    return layer_out, input_grad, new_master, new_first, new_second


def solution(mesh):
    state = P(None, None, "group", "local")
    rows = P(("group", "local"), None)
    return jax.shard_map(
        shards,
        mesh=mesh,
        in_specs=(rows, rows, P(("group", "local")), P(), state, state, state),
        out_specs=(rows, rows, state, state, state),
        check_vma=False,
    )
```

```python
import jax
import jax.numpy as jnp
import numpy as np
from jax import lax
from jax.experimental import pallas as pl
from jax.experimental.pallas import tpu as pltpu
from jax.sharding import PartitionSpec as P

loss_scale = 4.0
beta_first = 0.9
beta_second = 0.95
learn_rate = 0.001
adam_epsilon = 1e-08
bias_first = 1.0 - 0.9**10
bias_second = 1.0 - 0.95**10

SIDE = 4
CHAINS = 3
OFFSETS = (0, 1, 3, 2)
BOTH = ("group", "local")
SHIFTS = (4, 2, 0)
AXES = ((2, 1, 0), (1, 0, 2), (0, 2, 1))


def place(coords, core):
    return ((coords[0] * SIDE + coords[1]) * SIDE + coords[2]) * 2 + core


def step_pairs(axis, offset):
    pairs = []
    for group in range(SIDE**3):
        coords = [group // 16, group // 4 % 4, group % 4]
        other = list(coords)
        other[axis] ^= offset
        for core in range(2):
            pairs.append((place(coords, core), place(other, core)))
    return pairs


CORE_PAIRS = [(i, i ^ 1) for i in range(2 * SIDE**3)]


def hop(value, axis, offset):
    return lax.ppermute(value, BOTH, step_pairs(axis, offset))


def swap(value):
    return lax.ppermute(value, BOTH, CORE_PAIRS)


VMEM = pl.BlockSpec(memory_space=pltpu.VMEM)
SMEM = pl.BlockSpec(memory_space=pltpu.SMEM)
LIMIT = pltpu.CompilerParams(vmem_limit_bytes=48 * 1024 * 1024)


def shape_of(*dims):
    return jax.ShapeDtypeStruct(dims, jnp.bfloat16)


def pick_kernel(table_ref, p0, p1, p2, p3, *outs):
    for index, out in enumerate(outs):
        for k in range(2):
            e = table_ref[2 * index + k]
            for b, p in enumerate((p0, p1, p2, p3)):
                out[k, :, b] = p[:, e]


def pick(table, plane):
    columns = plane[0].shape[-1]
    return pl.pallas_call(
        pick_kernel,
        out_shape=[shape_of(2, 3, 4, 8, columns)] * 4,
        in_specs=[SMEM] + [VMEM] * 4,
        out_specs=[VMEM] * 4,
        compiler_params=LIMIT,
        name="pick",
    )(table, *plane)


def join_kernel(a0, a1, a2, a3, keep, give):
    for o, a in enumerate((a0, a1, a2, a3)):
        keep[:, 32 * o : 32 * o + 32] = a[0]
        give[:, 32 * o : 32 * o + 32] = a[1]


def join(arrived):
    columns = arrived[0].shape[-1]
    return pl.pallas_call(
        join_kernel,
        out_shape=[shape_of(3, 128, columns)] * 2,
        in_specs=[VMEM] * 4,
        out_specs=[VMEM] * 2,
        compiler_params=LIMIT,
        name="join",
    )(*arrived)


def cut_kernel(own, got, *outs):
    for o, out in enumerate(outs):
        out[0] = own[:, 32 * o : 32 * o + 32]
        out[1] = got[:, 32 * o : 32 * o + 32]


def cut(own, got):
    columns = own.shape[-1]
    return pl.pallas_call(
        cut_kernel,
        out_shape=[shape_of(2, 3, 32, columns)] * 4,
        in_specs=[VMEM] * 2,
        out_specs=[VMEM] * 4,
        compiler_params=LIMIT,
        name="cut",
    )(own, got)


def merge_kernel(table_ref, c0, c1, c2, c3, o0, o1, o2, o3, total):
    total[...] = jnp.zeros_like(total)
    for index, came in enumerate((c0, c1, c2, c3)):
        for k in range(2):
            e = table_ref[2 * index + k]
            total[:, e] += came[k].astype(jnp.float32)
    for index, out in enumerate((o0, o1, o2, o3)):
        out[...] = total[:, :, 8 * index : 8 * index + 8].astype(jnp.bfloat16)


def merge(table, came, experts):
    columns = came[0].shape[-1]
    return pl.pallas_call(
        merge_kernel,
        out_shape=[shape_of(3, experts, 8, columns)] * 4,
        in_specs=[SMEM] + [VMEM] * 4,
        out_specs=[VMEM] * 4,
        scratch_shapes=[pltpu.VMEM((3, experts, 32, columns), jnp.float32)],
        compiler_params=LIMIT,
        name="merge",
    )(table, *came)


def contract_last(left, right):
    return lax.dot_general(
        left, right, (((1,), (1,)), ((), ())), preferred_element_type=jnp.float32
    )


def contract_first(left, right):
    return lax.dot_general(
        left, right, (((0,), (0,)), ((), ())), preferred_element_type=jnp.float32
    )


def matmul(left, right):
    return jnp.dot(left, right, preferred_element_type=jnp.float32)


def shards(tokens, cotangent, row_slot, placement, master, first_moment, second_moment):
    group = lax.axis_index("group")
    core = lax.axis_index("local")
    experts = master.shape[0]
    columns = master.shape[3]
    rows = tokens.shape[0]

    steps = np.array([[o << SHIFTS[axes[2]] for o in OFFSETS] for axes in AXES], np.int32)
    seen = (group ^ jnp.asarray(steps.reshape(-1)))[:, None] == jnp.arange(SIDE**3)[None]
    pairs = jnp.sum(jnp.where(seen[:, :, None], placement[None], 0), 1)
    table = jnp.where(core == 0, pairs, pairs[:, ::-1]).reshape(CHAINS, 2 * SIDE)

    narrow = master.astype(jnp.bfloat16).transpose(1, 2, 0, 3)
    mine_w = []
    other_w = []
    for chain in range(CHAINS):
        axis1, axis2, axis3 = AXES[chain]
        block = narrow[:, 2 * chain : 2 * chain + 2]
        line = [block] + [hop(block, axis1, o) for o in OFFSETS[1:]]
        line = jnp.stack(line, 0)
        line = line.transpose(1, 3, 0, 2, 4).reshape(3, experts, 8, columns)
        plane = [line] + [hop(line, axis2, o) for o in OFFSETS[1:]]
        packed = pick(table[chain], plane)
        arrived = [
            (p if o == 0 else hop(p, axis3, o)).reshape(2, 3, 32, columns)
            for p, o in zip(packed, OFFSETS)
        ]
        keep, give = join(arrived)
        mine_w.append(keep)
        other_w.append(swap(give))

    def halves(own):
        got = swap(own)
        near = [lax.dynamic_slice_in_dim(v, core * columns, columns, 1) for v in (own, got)]
        far = [lax.dynamic_slice_in_dim(v, (1 - core) * columns, columns, 1) for v in (own, got)]
        return jnp.concatenate(near, 0), jnp.concatenate(far, 0)

    tok_near, tok_far = halves(tokens)
    cot_near, cot_far = halves(cotangent)
    slots = jnp.concatenate([row_slot, swap(row_slot)], 0)
    chosen = jnp.broadcast_to((slots == core)[:, None], (2 * rows, 128)).astype(jnp.float32)
    chosen = lax.optimization_barrier(chosen)

    hidden_list = []
    d_list = []
    sums = []
    for chain in range(CHAINS):
        wn = mine_w[chain]
        wf = other_w[chain]
        pre = contract_last(tok_near, wn[:2].reshape(256, columns)) + contract_last(
            tok_far, wf[:2].reshape(256, columns)
        )
        gate_pre = pre[:, :128]
        up_pre = pre[:, 128:]
        sigmoid_gate = jax.nn.sigmoid(gate_pre)
        hidden = (chosen * (gate_pre * sigmoid_gate * up_pre)).astype(jnp.bfloat16)
        d_hidden = contract_last(cot_near, wn[2]) + contract_last(cot_far, wf[2])
        d_hidden = chosen * d_hidden
        d_gate = d_hidden * up_pre * sigmoid_gate * (1.0 + gate_pre * (1.0 - sigmoid_gate))
        d_up = d_hidden * gate_pre * sigmoid_gate
        d_pair = jnp.concatenate([d_gate, d_up], 1).astype(jnp.bfloat16)
        hidden_list.append(hidden)
        d_list.append(d_pair)

        def term(tok, cot):
            pair = contract_first(d_pair, tok).astype(jnp.bfloat16).reshape(2, 128, columns)
            down = contract_first(hidden, cot).astype(jnp.bfloat16)[None]
            return jnp.concatenate([pair, down], 0)

        got = swap(term(tok_far, cot_far))
        own = term(tok_near, cot_near)

        axis1, axis2, axis3 = AXES[chain]
        packed = cut(own, got)
        came = [p if o == 0 else hop(p, axis3, o) for p, o in zip(packed, OFFSETS)]
        parts = merge(table[chain], came, experts)
        added = jnp.zeros((3, experts, 8, columns), jnp.float32)
        for index, o in enumerate(OFFSETS):
            came = parts[index] if o == 0 else hop(parts[index], axis2, o)
            added = added + came.astype(jnp.float32)
        added = added.astype(jnp.bfloat16).reshape(3, experts, 4, 2, columns).transpose(2, 0, 3, 1, 4)
        grad = jnp.zeros((3, 2, experts, columns), jnp.float32)
        for index, o in enumerate(OFFSETS):
            came = added[index] if o == 0 else hop(added[index], axis1, o)
            grad = grad + came.astype(jnp.float32)
        sums.append(grad)

    grads = jnp.concatenate(sums, 1).transpose(2, 0, 1, 3)
    scaled = grads / loss_scale
    new_first = beta_first * first_moment + (1.0 - beta_first) * scaled
    new_second = beta_second * second_moment + (1.0 - beta_second) * scaled * scaled
    new_master = master - learn_rate * (new_first / bias_first) / (
        jnp.sqrt(new_second / bias_second) + adam_epsilon
    )

    hidden = jnp.concatenate(hidden_list, 1)
    d_all = jnp.concatenate(d_list, 1)

    def weight_rows(parts, lo, hi):
        return jnp.concatenate([p[lo:hi].reshape(-1, columns) for p in parts], 0)

    def settle(near, far):
        both = jnp.stack([near, far], 1).astype(jnp.bfloat16)
        got = swap(both[rows:])
        low = jnp.where(core == 0, both[:rows, 0], both[:rows, 1])
        high = jnp.where(core == 0, both[:rows, 1], both[:rows, 0])
        got_low = jnp.where(core == 0, got[:, 1], got[:, 0])
        got_high = jnp.where(core == 0, got[:, 0], got[:, 1])
        pick = (row_slot == core)[:, None]
        return jnp.concatenate([jnp.where(pick, low, got_low), jnp.where(pick, high, got_high)], 1)

    layer_out = settle(
        matmul(hidden, weight_rows(mine_w, 2, 3)), matmul(hidden, weight_rows(other_w, 2, 3))
    )
    input_grad = settle(
        matmul(d_all, weight_rows(mine_w, 0, 2)), matmul(d_all, weight_rows(other_w, 0, 2))
    )
    return layer_out, input_grad, new_master, new_first, new_second


def solution(mesh):
    state = P(None, None, "group", "local")
    rows = P(("group", "local"), None)
    return jax.shard_map(
        shards,
        mesh=mesh,
        in_specs=(rows, rows, P(("group", "local")), P(), state, state, state),
        out_specs=(rows, rows, state, state, state),
        check_vma=False,
    )
```

```python
import jax
import jax.numpy as jnp
import numpy as np
from jax import lax
from jax.experimental import pallas as pl
from jax.experimental.pallas import tpu as pltpu
from jax.sharding import PartitionSpec as P

loss_scale = 4.0
beta_first = 0.9
beta_second = 0.95
learn_rate = 0.001
adam_epsilon = 1e-08
bias_first = 1.0 - 0.9**10
bias_second = 1.0 - 0.95**10

SIDE = 4
CHAINS = 3
BOTH = ("group", "local")
SHIFTS = (4, 2, 0)
AXES = ((2, 1, 0), (1, 0, 2), (0, 2, 1))


def place(coords, core):
    return ((coords[0] * SIDE + coords[1]) * SIDE + coords[2]) * 2 + core


def step_pairs(axis, offsets):
    pairs = []
    for group in range(SIDE**3):
        for core in range(2):
            coords = [group // 16, group // 4 % 4, group % 4]
            here = place(coords, core)
            coords[axis] ^= offsets[core]
            pairs.append((here, place(coords, core)))
    return pairs


CORE_PAIRS = [(i, i ^ 1) for i in range(2 * SIDE**3)]
ONE, BACK, ACROSS = (1, 3), (3, 1), (2, 2)
STEPS = ((0, 0), ONE, BACK, ACROSS)


def hop(value, axis, offsets):
    return lax.ppermute(value, BOTH, step_pairs(axis, offsets))


def swap(value):
    return lax.ppermute(value, BOTH, CORE_PAIRS)


def gather(block, axis):
    one = hop(block, axis, ONE)
    back = hop(block, axis, BACK)
    return [block, one, back, hop(one, axis, BACK)]


def scatter(parts, axis):
    own, one, back, across = parts
    passed = hop(across, axis, BACK)
    back = hop(back, axis, BACK)
    one = hop((one.astype(jnp.float32) + passed).astype(jnp.bfloat16), axis, ONE)
    return own.astype(jnp.float32) + one.astype(jnp.float32) + back.astype(jnp.float32)


VMEM = pl.BlockSpec(memory_space=pltpu.VMEM)
SMEM = pl.BlockSpec(memory_space=pltpu.SMEM)
LIMIT = pltpu.CompilerParams(vmem_limit_bytes=48 * 1024 * 1024)


def shape_of(*dims):
    return jax.ShapeDtypeStruct(dims, jnp.bfloat16)


def spots(core):
    return (0, 1 + core, 2 - core, 3)


def pick_kernel(table_ref, p0, p1, p2, p3, *outs):
    spot = spots(table_ref[8])
    for index, out in enumerate(outs):
        for k in range(2):
            e = table_ref[2 * index + k]
            for b, p in enumerate((p0, p1, p2, p3)):
                out[k, :, spot[b]] = p[:, e]


def pick(table, plane):
    columns = plane[0].shape[-1]
    return pl.pallas_call(
        pick_kernel,
        out_shape=[shape_of(2, 3, 4, 8, columns)] * 4,
        in_specs=[SMEM] + [VMEM] * 4,
        out_specs=[VMEM] * 4,
        compiler_params=LIMIT,
        name="pick",
    )(table, *plane)


def join_kernel(table_ref, a0, a1, a2, a3, keep, give):
    spot = spots(table_ref[8])
    for o, a in enumerate((a0, a1, a2, a3)):
        keep[:, spot[o]] = a[0]
        give[:, spot[o]] = a[1]


def join(table, arrived):
    columns = arrived[0].shape[-1]
    return pl.pallas_call(
        join_kernel,
        out_shape=[shape_of(3, 4, 32, columns)] * 2,
        in_specs=[SMEM] + [VMEM] * 4,
        out_specs=[VMEM] * 2,
        compiler_params=LIMIT,
        name="join",
    )(table, *arrived)


def lay_kernel(table_ref, keep, got, pair, down):
    core = table_ref[8]
    columns = keep.shape[-1]
    for side, half in ((core, keep), (1 - core, got)):
        where = pl.ds(pl.multiple_of(side * columns, columns), columns)
        for m in range(2):
            pair[128 * m : 128 * m + 128, where] = half[m]
        down[:, where] = half[2]


def lay(table, keep, got):
    columns = keep.shape[-1]
    return pl.pallas_call(
        lay_kernel,
        out_shape=[shape_of(256, 2 * columns), shape_of(128, 2 * columns)],
        in_specs=[SMEM] + [VMEM] * 2,
        out_specs=[VMEM] * 2,
        compiler_params=LIMIT,
        name="lay",
    )(table, keep.reshape(3, 128, columns), got.reshape(3, 128, columns))


def cut_kernel(table_ref, pair, down, got, *outs):
    spot = spots(table_ref[8])
    columns = got.shape[-1]
    half = pl.ds(pl.multiple_of(table_ref[8] * columns, columns), columns)
    for o, out in enumerate(outs):
        for m in range(2):
            out[0, m] = pair[m, spot[o], :, half]
        out[0, 2] = down[spot[o], :, half]
        out[1] = got[:, spot[o]]


def cut(table, pair, down, got):
    columns = got.shape[-1]
    return pl.pallas_call(
        cut_kernel,
        out_shape=[shape_of(2, 3, 32, columns)] * 4,
        in_specs=[SMEM] + [VMEM] * 3,
        out_specs=[VMEM] * 4,
        compiler_params=LIMIT,
        name="cut",
    )(
        table,
        pair.reshape(2, 4, 32, 2 * columns),
        down.reshape(4, 32, 2 * columns),
        got.reshape(3, 4, 32, columns),
    )


def merge_kernel(table_ref, c0, c1, c2, c3, o0, o1, o2, o3, total):
    spot = spots(table_ref[8])
    total[...] = jnp.zeros_like(total)
    for index, came in enumerate((c0, c1, c2, c3)):
        for k in range(2):
            e = table_ref[2 * index + k]
            for p in range(4):
                total[p, :, e] += came[k, :, p].astype(jnp.float32)
    for index, out in enumerate((o0, o1, o2, o3)):
        out[...] = total[spot[index]].astype(jnp.bfloat16)


def merge(table, came, experts):
    columns = came[0].shape[-1]
    return pl.pallas_call(
        merge_kernel,
        out_shape=[shape_of(3, experts, 8, columns)] * 4,
        in_specs=[SMEM] + [VMEM] * 4,
        out_specs=[VMEM] * 4,
        scratch_shapes=[pltpu.VMEM((4, 3, experts, 8, columns), jnp.float32)],
        compiler_params=LIMIT,
        name="merge",
    )(table, *[c.reshape(2, 3, 4, 8, columns) for c in came])


def contract_last(left, right):
    return lax.dot_general(
        left, right, (((1,), (1,)), ((), ())), preferred_element_type=jnp.float32
    )


def contract_first(left, right):
    return lax.dot_general(
        left, right, (((0,), (0,)), ((), ())), preferred_element_type=jnp.float32
    )


def matmul(left, right):
    return jnp.dot(left, right, preferred_element_type=jnp.float32)


def shards(tokens, cotangent, row_slot, placement, master, first_moment, second_moment):
    group = lax.axis_index("group")
    core = lax.axis_index("local")
    experts = master.shape[0]
    columns = master.shape[3]
    rows = tokens.shape[0]

    steps = np.array(
        [[[step[c] << SHIFTS[axes[2]] for step in STEPS] for axes in AXES] for c in range(2)], np.int32
    ).reshape(2, -1)
    there = group ^ jnp.where(core == 0, jnp.asarray(steps[0]), jnp.asarray(steps[1]))
    seen = there[:, None] == jnp.arange(SIDE**3)[None]
    pairs = jnp.sum(jnp.where(seen[:, :, None], placement[None], 0), 1)
    pairs = jnp.where(core == 0, pairs, pairs[:, ::-1]).reshape(CHAINS, 2 * SIDE)
    table = jnp.concatenate([pairs, jnp.full((CHAINS, 1), core)], 1)

    narrow = master.astype(jnp.bfloat16).transpose(1, 2, 0, 3)
    lines = []
    for chain in range(CHAINS):
        own, one, back, across = gather(narrow[:, 2 * chain : 2 * chain + 2], AXES[chain][0])
        line = [own, jnp.where(core == 0, one, back), jnp.where(core == 0, back, one), across]
        line = jnp.stack(line, 0).transpose(1, 3, 0, 2, 4)
        lines.append(line.reshape(3, experts, 8, columns))
    lines = lax.optimization_barrier(lines)
    planes = [gather(line, axes[1]) for line, axes in zip(lines, AXES)]

    tok = lax.all_gather(tokens, "local", axis=0, tiled=True)
    cot = lax.all_gather(cotangent, "local", axis=0, tiled=True)
    got_slot = swap(row_slot)
    slots = jnp.stack([jnp.where(core == 0, row_slot, got_slot), jnp.where(core == 0, got_slot, row_slot)])
    chosen = jnp.broadcast_to((slots.reshape(-1) == core)[:, None], (2 * rows, 128)).astype(jnp.float32)
    planes[2], tok, cot, chosen = lax.optimization_barrier((planes[2], tok, cot, chosen))

    weights = []
    for chain in range(CHAINS):
        packed = pick(table[chain], planes[chain])
        arrived = [packed[0]] + [hop(p, AXES[chain][2], s) for p, s in zip(packed[1:], STEPS[1:])]
        keep, give = join(table[chain], [a.reshape(2, 3, 32, columns) for a in arrived])
        weights.append(lay(table[chain], keep, swap(give)))

    hidden_list = []
    d_list = []
    sums = []
    for chain in range(CHAINS):
        w_pair, w_down = weights[chain]
        pre = contract_last(tok, w_pair)
        gate_pre = pre[:, :128]
        up_pre = pre[:, 128:]
        sigmoid_gate = jax.nn.sigmoid(gate_pre)
        hidden = (chosen * (gate_pre * sigmoid_gate * up_pre)).astype(jnp.bfloat16)
        d_hidden = contract_last(cot, w_down)
        d_hidden = chosen * d_hidden
        d_gate = d_hidden * up_pre * sigmoid_gate * (1.0 + gate_pre * (1.0 - sigmoid_gate))
        d_up = d_hidden * gate_pre * sigmoid_gate
        d_pair = jnp.concatenate([d_gate, d_up], 1).astype(jnp.bfloat16)
        hidden_list.append(hidden)
        d_list.append(d_pair)

        pair = contract_first(d_pair, tok).astype(jnp.bfloat16)
        down = contract_first(hidden, cot).astype(jnp.bfloat16)
        far = (1 - core) * columns
        give_pair = lax.dynamic_slice_in_dim(pair, far, columns, 1).reshape(2, 128, columns)
        give_down = lax.dynamic_slice_in_dim(down, far, columns, 1)[None]
        got = swap(jnp.concatenate([give_pair, give_down], 0))
        packed = cut(table[chain], pair, down, got)
        came = [packed[0]] + [hop(p, AXES[chain][2], s) for p, s in zip(packed[1:], STEPS[1:])]
        sums.append(scatter(merge(table[chain], came, experts), AXES[chain][1]))

    hidden = jnp.concatenate(hidden_list, 1)
    d_all = jnp.concatenate(d_list, 1)

    def rows_out(left, right):
        out = matmul(left, jnp.concatenate(right, 0)).astype(jnp.bfloat16)
        got = swap(lax.dynamic_slice_in_dim(out, (1 - core) * rows, rows, 0))
        return lax.dynamic_slice_in_dim(out, core * rows, rows, 0) + got

    layer_out = rows_out(hidden, [w[1] for w in weights])
    input_grad = rows_out(d_all, [w[0] for w in weights])
    sums[2], layer_out, input_grad = lax.optimization_barrier((sums[2], layer_out, input_grad))

    parts = []
    for chain in range(CHAINS):
        line = sums[chain].astype(jnp.bfloat16).reshape(3, experts, 4, 2, columns)
        own, first, second, across = line.transpose(2, 0, 3, 1, 4)
        one = jnp.where(core == 0, first, second)
        back = jnp.where(core == 0, second, first)
        parts.append(scatter([own, one, back, across], AXES[chain][0]))

    grads = jnp.concatenate(parts, 1).transpose(2, 0, 1, 3)
    scaled = grads / loss_scale
    new_first = beta_first * first_moment + (1.0 - beta_first) * scaled
    new_second = beta_second * second_moment + (1.0 - beta_second) * scaled * scaled
    new_master = master - learn_rate * (new_first / bias_first) / (
        jnp.sqrt(new_second / bias_second) + adam_epsilon
    )

    return layer_out, input_grad, new_master, new_first, new_second


def solution(mesh):
    state = P(None, None, "group", "local")
    rows = P(("group", "local"), None)
    return jax.shard_map(
        shards,
        mesh=mesh,
        in_specs=(rows, rows, P(("group", "local")), P(), state, state, state),
        out_specs=(rows, rows, state, state, state),
        check_vma=False,
    )
```

```python
import jax
import jax.numpy as jnp
import numpy as np
from jax import lax
from jax.experimental import pallas as pl
from jax.experimental.pallas import tpu as pltpu
from jax.sharding import PartitionSpec as P

loss_scale = 4.0
beta_first = 0.9
beta_second = 0.95
learn_rate = 0.001
adam_epsilon = 1e-08
bias_first = 1.0 - 0.9**10
bias_second = 1.0 - 0.95**10

SIDE = 4
CHAINS = 3
BOTH = ("group", "local")
SHIFTS = (4, 2, 0)
AXES = ((2, 1, 0), (1, 0, 2), (0, 2, 1))


def place(coords, core):
    return ((coords[0] * SIDE + coords[1]) * SIDE + coords[2]) * 2 + core


def step_pairs(axis, offsets):
    pairs = []
    for group in range(SIDE**3):
        for core in range(2):
            coords = [group // 16, group // 4 % 4, group % 4]
            here = place(coords, core)
            coords[axis] ^= offsets[core]
            pairs.append((here, place(coords, core)))
    return pairs


CORE_PAIRS = [(i, i ^ 1) for i in range(2 * SIDE**3)]
ONE, BACK, ACROSS = (1, 3), (3, 1), (2, 2)
STEPS = ((0, 0), ONE, BACK, ACROSS)


def hop(value, axis, offsets):
    return lax.ppermute(value, BOTH, step_pairs(axis, offsets))


def swap(value):
    return lax.ppermute(value, BOTH, CORE_PAIRS)


def gather(block, axis):
    one = hop(block, axis, ONE)
    back = hop(block, axis, BACK)
    return [block, one, back, hop(one, axis, BACK)]


def scatter(parts, axis):
    own, one, back, across = parts
    passed = hop(across, axis, BACK)
    back = hop(back, axis, BACK)
    one = hop((one.astype(jnp.float32) + passed).astype(jnp.bfloat16), axis, ONE)
    return own.astype(jnp.float32) + one.astype(jnp.float32) + back.astype(jnp.float32)


def contract_last(left, right):
    return lax.dot_general(
        left, right, (((1,), (1,)), ((), ())), preferred_element_type=jnp.float32
    )


def contract_first(left, right):
    return lax.dot_general(
        left, right, (((0,), (0,)), ((), ())), preferred_element_type=jnp.float32
    )


def matmul(left, right):
    return jnp.dot(left, right, preferred_element_type=jnp.float32)


VMEM = pl.BlockSpec(memory_space=pltpu.VMEM)
SMEM = pl.BlockSpec(memory_space=pltpu.SMEM)
LIMIT = pltpu.CompilerParams(vmem_limit_bytes=16 * 1024 * 1024)


def shape_of(*dims):
    return jax.ShapeDtypeStruct(dims, jnp.bfloat16)


def spots(core):
    return (0, 1 + core, 2 - core, 3)


def pick_kernel(table_ref, p0, p1, p2, p3, *outs):
    spot = spots(table_ref[8])
    for index, out in enumerate(outs):
        for k in range(2):
            e = table_ref[2 * index + k]
            for b, p in enumerate((p0, p1, p2, p3)):
                out[k, :, spot[b]] = p[:, e]


def pick(table, plane):
    columns = plane[0].shape[-1]
    return pl.pallas_call(
        pick_kernel,
        out_shape=[shape_of(2, 3, 4, 8, columns)] * 4,
        in_specs=[SMEM] + [VMEM] * 4,
        out_specs=[VMEM] * 4,
        compiler_params=LIMIT,
        name="pick",
    )(table, *plane)


def join_kernel(table_ref, a0, a1, a2, a3, keep, give):
    spot = spots(table_ref[8])
    for o, a in enumerate((a0, a1, a2, a3)):
        keep[:, spot[o]] = a[0]
        give[:, spot[o]] = a[1]


def join(table, arrived):
    columns = arrived[0].shape[-1]
    return pl.pallas_call(
        join_kernel,
        out_shape=[shape_of(3, 4, 32, columns)] * 2,
        in_specs=[SMEM] + [VMEM] * 4,
        out_specs=[VMEM] * 2,
        compiler_params=LIMIT,
        name="join",
    )(table, *arrived)


def work_kernel(
    table_ref, tok0, tok1, cot0, cot1, mask, keep, got, hidden, pair, own_term, far_term
):
    core = table_ref[8]
    columns = keep.shape[-1]
    rows = tok0.shape[0]
    step = 256
    near = pl.multiple_of(core * columns, columns)
    far = pl.multiple_of((1 - core) * columns, columns)
    sides = ((pl.ds(near, columns), keep), (pl.ds(far, columns), got))
    for b, (tok, cot) in enumerate(((tok0, cot0), (tok1, cot1))):
        for r in range(0, rows, step):
            here = slice(r, r + step)
            gate_pre = up_pre = d_hidden = 0.0
            for cols, w in sides:
                tok_part = tok[here, cols]
                gate_pre = gate_pre + contract_last(tok_part, w[0])
                up_pre = up_pre + contract_last(tok_part, w[1])
                d_hidden = d_hidden + contract_last(cot[here, cols], w[2])
            there = slice(rows * b + r, rows * b + r + step)
            chosen = mask[there]
            sigmoid_gate = jax.nn.sigmoid(gate_pre)
            hidden[there] = (chosen * (gate_pre * sigmoid_gate * up_pre)).astype(jnp.bfloat16)
            d_hidden = chosen * d_hidden
            d_gate = d_hidden * up_pre * sigmoid_gate * (1.0 + gate_pre * (1.0 - sigmoid_gate))
            pair[there, :128] = d_gate.astype(jnp.bfloat16)
            pair[there, 128:] = (d_hidden * gate_pre * sigmoid_gate).astype(jnp.bfloat16)
    for start, out in ((near, own_term), (far, far_term)):
        for c in range(0, columns, step):
            cols = pl.ds(start + c, step)
            both = 0.0
            down = 0.0
            for b, (tok, cot) in enumerate(((tok0, cot0), (tok1, cot1))):
                there = slice(rows * b, rows * b + rows)
                both = both + contract_first(pair[there], tok[:, cols])
                down = down + contract_first(hidden[there], cot[:, cols])
            out[0, :, c : c + step] = both[:128].astype(jnp.bfloat16)
            out[1, :, c : c + step] = both[128:].astype(jnp.bfloat16)
            out[2, :, c : c + step] = down.astype(jnp.bfloat16)


def work(table, rows_in, mask, keep, got):
    columns = keep.shape[-1]
    rows = mask.shape[0]
    return pl.pallas_call(
        work_kernel,
        out_shape=[
            shape_of(rows, 128),
            shape_of(rows, 256),
            shape_of(3, 128, columns),
            shape_of(3, 128, columns),
        ],
        in_specs=[SMEM] + [VMEM] * 7,
        out_specs=[VMEM] * 4,
        compiler_params=pltpu.CompilerParams(vmem_limit_bytes=32 * 1024 * 1024),
        name="work",
    )(table, *rows_in, mask, keep.reshape(3, 128, columns), got.reshape(3, 128, columns))


def rows_kernel(table_ref, *refs):
    core = table_ref[8]
    hidden, pair, keep, got = refs[0:3], refs[3:6], refs[6:9], refs[9:12]
    outs = refs[12:]
    columns = keep[0].shape[-1]
    step = 512
    for side, w in ((core, keep), (1 - core, got)):
        start = pl.multiple_of(side * columns, columns)
        for c in range(0, columns, step):
            cols = pl.ds(start + c, step)
            part = slice(c, c + step)
            for half in range(2):
                rows = slice(512 * half, 512 * half + 512)
                layer = 0.0
                grad = 0.0
                for chain in range(CHAINS):
                    layer = layer + matmul(hidden[chain][rows], w[chain][2, :, part])
                    for m in range(2):
                        d = pair[chain][rows, 128 * m : 128 * m + 128]
                        grad = grad + matmul(d, w[chain][m, :, part])
                outs[half][:, cols] = layer.astype(jnp.bfloat16)
                outs[2 + half][:, cols] = grad.astype(jnp.bfloat16)


def rows_out(table, hidden, pair, keep, got):
    columns = keep[0].shape[-1]
    keep = [k.reshape(3, 128, columns) for k in keep]
    got = [g.reshape(3, 128, columns) for g in got]
    return pl.pallas_call(
        rows_kernel,
        out_shape=[shape_of(512, 2 * columns)] * 4,
        in_specs=[SMEM] + [VMEM] * 12,
        out_specs=[VMEM] * 4,
        compiler_params=pltpu.CompilerParams(vmem_limit_bytes=40 * 1024 * 1024),
        name="rows_out",
    )(table, *hidden, *pair, *keep, *got)


def cut_kernel(table_ref, own, got, *outs):
    spot = spots(table_ref[8])
    for o, out in enumerate(outs):
        out[0] = own[:, spot[o]]
        out[1] = got[:, spot[o]]


def cut(table, own, got):
    columns = own.shape[-1]
    return pl.pallas_call(
        cut_kernel,
        out_shape=[shape_of(2, 3, 32, columns)] * 4,
        in_specs=[SMEM] + [VMEM] * 2,
        out_specs=[VMEM] * 4,
        compiler_params=LIMIT,
        name="cut",
    )(table, own.reshape(3, 4, 32, columns), got.reshape(3, 4, 32, columns))


def merge_kernel(table_ref, c0, c1, c2, c3, o0, o1, o2, o3, total):
    spot = spots(table_ref[8])
    total[...] = jnp.zeros_like(total)
    for index, came in enumerate((c0, c1, c2, c3)):
        for k in range(2):
            e = table_ref[2 * index + k]
            for p in range(4):
                total[p, :, e] += came[k, :, p].astype(jnp.float32)
    for index, out in enumerate((o0, o1, o2, o3)):
        out[...] = total[spot[index]].astype(jnp.bfloat16)


def merge(table, came, experts):
    columns = came[0].shape[-1]
    return pl.pallas_call(
        merge_kernel,
        out_shape=[shape_of(3, experts, 8, columns)] * 4,
        in_specs=[SMEM] + [VMEM] * 4,
        out_specs=[VMEM] * 4,
        scratch_shapes=[pltpu.VMEM((4, 3, experts, 8, columns), jnp.float32)],
        compiler_params=LIMIT,
        name="merge",
    )(table, *[c.reshape(2, 3, 4, 8, columns) for c in came])


def shards(tokens, cotangent, row_slot, placement, master, first_moment, second_moment):
    group = lax.axis_index("group")
    core = lax.axis_index("local")
    experts = master.shape[0]
    columns = master.shape[3]
    rows = tokens.shape[0]

    steps = np.array(
        [[[step[c] << SHIFTS[axes[2]] for step in STEPS] for axes in AXES] for c in range(2)], np.int32
    ).reshape(2, -1)
    there = group ^ jnp.where(core == 0, jnp.asarray(steps[0]), jnp.asarray(steps[1]))
    seen = there[:, None] == jnp.arange(SIDE**3)[None]
    pairs = jnp.sum(jnp.where(seen[:, :, None], placement[None], 0), 1)
    pairs = jnp.where(core == 0, pairs, pairs[:, ::-1]).reshape(CHAINS, 2 * SIDE)
    table = jnp.concatenate([pairs, jnp.full((CHAINS, 1), core)], 1)

    narrow = master.astype(jnp.bfloat16).transpose(1, 2, 0, 3)
    lines = []
    for chain in range(CHAINS):
        own, one, back, across = gather(narrow[:, 2 * chain : 2 * chain + 2], AXES[chain][0])
        line = [own, jnp.where(core == 0, one, back), jnp.where(core == 0, back, one), across]
        line = jnp.stack(line, 0).transpose(1, 3, 0, 2, 4)
        lines.append(line.reshape(3, experts, 8, columns))
    rows_in = [tokens, swap(tokens), cotangent, swap(cotangent)]
    slots = jnp.concatenate([row_slot, swap(row_slot)], 0)
    chosen = jnp.broadcast_to((slots == core)[:, None], (2 * rows, 128)).astype(jnp.float32)
    lines, rows_in, chosen = lax.optimization_barrier((lines, rows_in, chosen))
    planes = [gather(line, axes[1]) for line, axes in zip(lines, AXES)]

    mine_w = []
    other_w = []
    hidden = []
    pair = []
    sums = []
    for chain in range(CHAINS):
        packed = pick(table[chain], planes[chain])
        arrived = [packed[0]] + [hop(p, AXES[chain][2], s) for p, s in zip(packed[1:], STEPS[1:])]
        keep, give = join(table[chain], [a.reshape(2, 3, 32, columns) for a in arrived])
        got = swap(give)
        mine_w.append(keep)
        other_w.append(got)
        one_hidden, one_pair, own, far = work(table[chain], rows_in, chosen, keep, got)
        hidden.append(one_hidden)
        pair.append(one_pair)
        packed = cut(table[chain], own, swap(far))
        came = [packed[0]] + [hop(p, AXES[chain][2], s) for p, s in zip(packed[1:], STEPS[1:])]
        sums.append(scatter(merge(table[chain], came, experts), AXES[chain][1]))

    layer_own, layer_far, grad_own, grad_far = rows_out(table[0], hidden, pair, mine_w, other_w)
    layer_out = layer_own + swap(layer_far)
    input_grad = grad_own + swap(grad_far)
    sums[2], layer_out, input_grad = lax.optimization_barrier((sums[2], layer_out, input_grad))

    parts = []
    for chain in range(CHAINS):
        line = sums[chain].astype(jnp.bfloat16).reshape(3, experts, 4, 2, columns)
        own, first, second, across = line.transpose(2, 0, 3, 1, 4)
        one = jnp.where(core == 0, first, second)
        back = jnp.where(core == 0, second, first)
        parts.append(scatter([own, one, back, across], AXES[chain][0]))

    grads = jnp.concatenate(parts, 1).transpose(2, 0, 1, 3)
    scaled = grads / loss_scale
    new_first = beta_first * first_moment + (1.0 - beta_first) * scaled
    new_second = beta_second * second_moment + (1.0 - beta_second) * scaled * scaled
    new_master = master - learn_rate * (new_first / bias_first) / (
        jnp.sqrt(new_second / bias_second) + adam_epsilon
    )

    return layer_out, input_grad, new_master, new_first, new_second


def solution(mesh):
    state = P(None, None, "group", "local")
    rows = P(("group", "local"), None)
    return jax.shard_map(
        shards,
        mesh=mesh,
        in_specs=(rows, rows, P(("group", "local")), P(), state, state, state),
        out_specs=(rows, rows, state, state, state),
        check_vma=False,
    )
```

```python
import functools
import jax
import jax.numpy as jnp
import numpy as np
from jax import lax
from jax.experimental import pallas as pl
from jax.experimental.pallas import tpu as pltpu
from jax.sharding import PartitionSpec as P

loss_scale = 4.0
beta_first = 0.9
beta_second = 0.95
learn_rate = 0.001
adam_epsilon = 1e-08
bias_first = 1.0 - 0.9**10
bias_second = 1.0 - 0.95**10

SIDE = 4
CHAINS = 3
BOTH = ("group", "local")
SHIFTS = (4, 2, 0)
AXES = ((2, 1, 0), (1, 0, 2), (0, 2, 1))


def place(coords, core):
    return ((coords[0] * SIDE + coords[1]) * SIDE + coords[2]) * 2 + core


def step_pairs(axis, offsets):
    pairs = []
    for group in range(SIDE**3):
        for core in range(2):
            coords = [group // 16, group // 4 % 4, group % 4]
            here = place(coords, core)
            coords[axis] ^= offsets[core]
            pairs.append((here, place(coords, core)))
    return pairs


CORE_PAIRS = [(i, i ^ 1) for i in range(2 * SIDE**3)]
ONE, BACK, ACROSS = (1, 3), (3, 1), (2, 2)
STEPS = ((0, 0), ONE, BACK, ACROSS)


def hop(value, axis, offsets):
    return lax.ppermute(value, BOTH, step_pairs(axis, offsets))


def swap(value):
    return lax.ppermute(value, BOTH, CORE_PAIRS)


def gather(block, axis):
    one = hop(block, axis, ONE)
    back = hop(block, axis, BACK)
    return [block, one, back, hop(one, axis, BACK)]


def gather_small(block, axis):
    one = hop(block, axis, ONE)
    return [block, one, hop(jnp.stack([block, one], 0), axis, BACK)]


def scatter(own, one, rest, axis):
    came = hop(rest, axis, BACK)
    one = (one.astype(jnp.float32) + came[1].astype(jnp.float32)).astype(jnp.bfloat16)
    return own, came, hop(one, axis, ONE)


def contract_last(left, right):
    return lax.dot_general(
        left, right, (((1,), (1,)), ((), ())), preferred_element_type=jnp.float32
    )


def contract_first(left, right):
    return lax.dot_general(
        left, right, (((0,), (0,)), ((), ())), preferred_element_type=jnp.float32
    )


def matmul(left, right):
    return jnp.dot(left, right, preferred_element_type=jnp.float32)


VMEM = pl.BlockSpec(memory_space=pltpu.VMEM)
SMEM = pl.BlockSpec(memory_space=pltpu.SMEM)
LIMIT = pltpu.CompilerParams(vmem_limit_bytes=16 * 1024 * 1024)


def shape_of(*dims):
    return jax.ShapeDtypeStruct(dims, jnp.bfloat16)


def spots(core):
    return (0, 1 + core, 2 - core, 3)


def weave_kernel(table_ref, own, one, rest, out, turned):
    first = table_ref[8] == 0
    for m in range(3):
        for r in range(2):
            near = one[m, r].astype(jnp.float32)
            back = rest[0, m, r].astype(jnp.float32)
            turned[m, :, r] = own[m, r].astype(jnp.float32)
            turned[m, :, 2 + r] = jnp.where(first, near, back)
            turned[m, :, 4 + r] = jnp.where(first, back, near)
            turned[m, :, 6 + r] = rest[1, m, r].astype(jnp.float32)
    out[...] = turned[...].astype(jnp.bfloat16)


def weave(table, own, one, rest):
    _, _, experts, columns = own.shape
    return pl.pallas_call(
        weave_kernel,
        out_shape=shape_of(3, experts, 8, columns),
        in_specs=[SMEM] + [VMEM] * 3,
        out_specs=VMEM,
        scratch_shapes=[pltpu.VMEM((3, experts, 8, columns), jnp.float32)],
        compiler_params=LIMIT,
        name="weave",
    )(table, own, one, rest)


def unweave_kernel(table_ref, own, came, last, out, one, rest, turned):
    first = table_ref[8] == 0
    turned[...] = (
        own[...].astype(jnp.float32) + came[0].astype(jnp.float32) + last[...].astype(jnp.float32)
    )
    for m in range(3):
        for r in range(2):
            left = turned[m, :, 2 + r]
            right = turned[m, :, 4 + r]
            out[m, r] = turned[m, :, r]
            one[m, r] = jnp.where(first, left, right).astype(jnp.bfloat16)
            rest[0, m, r] = jnp.where(first, right, left).astype(jnp.bfloat16)
            rest[1, m, r] = turned[m, :, 6 + r].astype(jnp.bfloat16)


def unweave(table, own, came, last):
    _, experts, _, columns = own.shape
    return pl.pallas_call(
        unweave_kernel,
        out_shape=[
            jax.ShapeDtypeStruct((3, 2, experts, columns), jnp.float32),
            shape_of(3, 2, experts, columns),
            shape_of(2, 3, 2, experts, columns),
        ],
        in_specs=[SMEM] + [VMEM] * 3,
        out_specs=[VMEM] * 3,
        scratch_shapes=[pltpu.VMEM((3, experts, 8, columns), jnp.float32)],
        compiler_params=LIMIT,
        name="unweave",
    )(table, own, came, last)


def pick_kernel(table_ref, p0, p1, p2, p3, *outs):
    spot = spots(table_ref[8])
    for index, out in enumerate(outs):
        for k in range(2):
            e = table_ref[2 * index + k]
            for b, p in enumerate((p0, p1, p2, p3)):
                out[k, :, spot[b]] = p[:, e]


def pick(table, plane):
    columns = plane[0].shape[-1]
    return pl.pallas_call(
        pick_kernel,
        out_shape=[shape_of(2, 3, 4, 8, columns)] * 4,
        in_specs=[SMEM] + [VMEM] * 4,
        out_specs=[VMEM] * 4,
        compiler_params=LIMIT,
        name="pick",
    )(table, *plane)


def join_kernel(table_ref, a0, a1, a2, a3, keep, give):
    spot = spots(table_ref[8])
    for o, a in enumerate((a0, a1, a2, a3)):
        keep[:, spot[o]] = a[0]
        give[:, spot[o]] = a[1]


def join(table, arrived):
    columns = arrived[0].shape[-1]
    return pl.pallas_call(
        join_kernel,
        out_shape=[shape_of(3, 4, 32, columns)] * 2,
        in_specs=[SMEM] + [VMEM] * 4,
        out_specs=[VMEM] * 2,
        compiler_params=LIMIT,
        name="join",
    )(table, *arrived)


def work_kernel(
    table_ref, tok0, tok1, cot0, cot1, mask, keep, got, hidden, pair, own_term, far_term, turned
):
    core = table_ref[8]
    columns = keep.shape[-1]
    rows = tok0.shape[0]
    step = 256
    near = pl.multiple_of(core * columns, columns)
    far = pl.multiple_of((1 - core) * columns, columns)
    sides = [
        (pl.ds(start, columns), w[0:2].reshape(256, columns), w[2])
        for start, w in ((near, keep), (far, got))
    ]
    for b, (tok, cot) in enumerate(((tok0, cot0), (tok1, cot1))):
        for r in range(0, rows, step):
            here = slice(r, r + step)
            pre = d_hidden = 0.0
            for cols, w_pair, w_down in sides:
                pre = pre + contract_last(tok[here, cols], w_pair)
                d_hidden = d_hidden + contract_last(cot[here, cols], w_down)
            gate_pre = pre[:, :128]
            up_pre = pre[:, 128:]
            there = slice(rows * b + r, rows * b + r + step)
            chosen = mask[there]
            sigmoid_gate = jax.nn.sigmoid(gate_pre)
            act = gate_pre * sigmoid_gate
            d_hidden = chosen * d_hidden
            d_gate = d_hidden * up_pre * sigmoid_gate * (1.0 + gate_pre * (1.0 - sigmoid_gate))
            d_gate = d_gate.astype(jnp.bfloat16)
            d_up = (d_hidden * act).astype(jnp.bfloat16)
            out = (chosen * (act * up_pre)).astype(jnp.bfloat16)
            hidden[there] = out
            pair[there, :128] = d_gate
            pair[there, 128:] = d_up
            turned[:128, there] = d_gate.T
            turned[128:256, there] = d_up.T
            turned[256:, there] = out.T
    for start, out in ((near, own_term), (far, far_term)):
        for c in range(0, columns, step):
            cols = pl.ds(start + c, step)
            both = 0.0
            down = 0.0
            for b, (tok, cot) in enumerate(((tok0, cot0), (tok1, cot1))):
                there = slice(rows * b, rows * b + rows)
                both = both + matmul(turned[:256, there], tok[:, cols])
                down = down + matmul(turned[256:, there], cot[:, cols])
            out[0, :, c : c + step] = both[:128].astype(jnp.bfloat16)
            out[1, :, c : c + step] = both[128:].astype(jnp.bfloat16)
            out[2, :, c : c + step] = down.astype(jnp.bfloat16)


def work(table, rows_in, mask, keep, got):
    columns = keep.shape[-1]
    rows = mask.shape[0]
    return pl.pallas_call(
        work_kernel,
        out_shape=[
            shape_of(rows, 128),
            shape_of(rows, 256),
            shape_of(3, 128, columns),
            shape_of(3, 128, columns),
        ],
        in_specs=[SMEM] + [VMEM] * 7,
        out_specs=[VMEM] * 4,
        scratch_shapes=[pltpu.VMEM((384, rows), jnp.bfloat16)],
        compiler_params=pltpu.CompilerParams(vmem_limit_bytes=32 * 1024 * 1024),
        name="work",
    )(table, *rows_in, mask, keep.reshape(3, 128, columns), got.reshape(3, 128, columns))


def rows_kernel(first, table_ref, *refs):
    core = table_ref[8]
    hidden, pair, keep, got = refs[0:3], refs[3:6], refs[6:9], refs[9:12]
    added, (layer_out, grad_out) = refs[12:-2], refs[-2:]
    columns = keep[0].shape[-1]
    step = 512
    rows = slice(first, first + layer_out.shape[0])
    for side, w in ((core, keep), (1 - core, got)):
        start = pl.multiple_of(side * columns, columns)
        for c in range(0, columns, step):
            cols = pl.ds(start + c, step)
            part = slice(c, c + step)
            layer = 0.0
            grad = 0.0
            for chain in range(CHAINS):
                layer = layer + matmul(hidden[chain][rows], w[chain][2, :, part])
                w_pair = w[chain][0:2, :, part].reshape(256, step)
                grad = grad + matmul(pair[chain][rows], w_pair)
            layer = layer.astype(jnp.bfloat16)
            grad = grad.astype(jnp.bfloat16)
            if added:
                layer = layer + added[0][:, cols]
                grad = grad + added[1][:, cols]
            layer_out[:, cols] = layer
            grad_out[:, cols] = grad


def rows_out(table, first, hidden, pair, keep, got, added):
    columns = keep[0].shape[-1]
    rows = hidden[0].shape[0] // 2
    keep = [k.reshape(3, 128, columns) for k in keep]
    got = [g.reshape(3, 128, columns) for g in got]
    return pl.pallas_call(
        functools.partial(rows_kernel, first),
        out_shape=[shape_of(rows, 2 * columns)] * 2,
        in_specs=[SMEM] + [VMEM] * (12 + len(added)),
        out_specs=[VMEM] * 2,
        compiler_params=pltpu.CompilerParams(vmem_limit_bytes=32 * 1024 * 1024),
        name="rows_out",
    )(table, *hidden, *pair, *keep, *got, *added)


def cut_kernel(table_ref, own, got, *outs):
    spot = spots(table_ref[8])
    for o, out in enumerate(outs):
        out[0] = own[:, spot[o]]
        out[1] = got[:, spot[o]]


def cut(table, own, got):
    columns = own.shape[-1]
    return pl.pallas_call(
        cut_kernel,
        out_shape=[shape_of(2, 3, 32, columns)] * 4,
        in_specs=[SMEM] + [VMEM] * 2,
        out_specs=[VMEM] * 4,
        compiler_params=LIMIT,
        name="cut",
    )(table, own.reshape(3, 4, 32, columns), got.reshape(3, 4, 32, columns))


def merge_kernel(table_ref, c0, c1, c2, c3, own, one, rest, total):
    spot = spots(table_ref[8])
    total[...] = jnp.zeros_like(total)
    for index, came in enumerate((c0, c1, c2, c3)):
        for k in range(2):
            e = table_ref[2 * index + k]
            for p in range(4):
                total[p, :, e] += came[k, :, p].astype(jnp.float32)
    own[...] = total[0].astype(jnp.bfloat16)
    one[...] = total[spot[1]].astype(jnp.bfloat16)
    rest[0] = total[spot[2]].astype(jnp.bfloat16)
    rest[1] = total[3].astype(jnp.bfloat16)


def merge(table, came, experts):
    columns = came[0].shape[-1]
    return pl.pallas_call(
        merge_kernel,
        out_shape=[shape_of(*lead, 3, experts, 8, columns) for lead in ((), (), (2,))],
        in_specs=[SMEM] + [VMEM] * 4,
        out_specs=[VMEM] * 3,
        scratch_shapes=[pltpu.VMEM((4, 3, experts, 8, columns), jnp.float32)],
        compiler_params=LIMIT,
        name="merge",
    )(table, *[c.reshape(2, 3, 4, 8, columns) for c in came])


def shards(tokens, cotangent, row_slot, placement, master, first_moment, second_moment):
    group = lax.axis_index("group")
    core = lax.axis_index("local")
    experts = master.shape[0]
    columns = master.shape[3]
    rows = tokens.shape[0]

    steps = np.array(
        [[[step[c] << SHIFTS[axes[2]] for step in STEPS] for axes in AXES] for c in range(2)], np.int32
    ).reshape(2, -1)
    there = group ^ jnp.where(core == 0, jnp.asarray(steps[0]), jnp.asarray(steps[1]))
    seen = there[:, None] == jnp.arange(SIDE**3)[None]
    pairs = jnp.sum(jnp.where(seen[:, :, None], placement[None], 0), 1)
    pairs = jnp.where(core == 0, pairs, pairs[:, ::-1]).reshape(CHAINS, 2 * SIDE)
    table = jnp.concatenate([pairs, jnp.full((CHAINS, 1), core)], 1)

    narrow = master.astype(jnp.bfloat16).transpose(1, 2, 0, 3)
    lines = [
        gather_small(narrow[:, 2 * chain : 2 * chain + 2], AXES[chain][0]) for chain in range(CHAINS)
    ]
    lines[0][1], tokens, cotangent, row_slot = lax.optimization_barrier(
        (lines[0][1], tokens, cotangent, row_slot)
    )
    lines = [weave(row, *line) for row, line in zip(table, lines)]
    rows_in = [tokens, swap(tokens), cotangent, swap(cotangent)]
    slots = jnp.concatenate([row_slot, swap(row_slot)], 0)
    chosen = jnp.broadcast_to((slots == core)[:, None], (2 * rows, 128)).astype(jnp.float32)
    lines, rows_in, chosen = lax.optimization_barrier((lines, rows_in, chosen))
    planes = [gather(line, axes[1]) for line, axes in zip(lines, AXES)]

    mine_w = []
    other_w = []
    for chain in range(CHAINS):
        packed = pick(table[chain], planes[chain])
        arrived = [packed[0]] + [hop(p, AXES[chain][2], s) for p, s in zip(packed[1:], STEPS[1:])]
        keep, give = join(table[chain], [a.reshape(2, 3, 32, columns) for a in arrived])
        mine_w.append(keep)
        other_w.append(swap(give))

    hidden = []
    pair = []
    sent = []
    for chain in range(CHAINS):
        if chain == 2:
            other_w[2], sent[0] = lax.optimization_barrier((other_w[2], sent[0]))
        one_hidden, one_pair, own, far = work(
            table[chain], rows_in, chosen, mine_w[chain], other_w[chain]
        )
        hidden.append(one_hidden)
        pair.append(one_pair)
        sent.append(cut(table[chain], own, swap(far)))

    sums = []
    for chain in range(CHAINS):
        packed = sent[chain]
        came = [packed[0]] + [hop(p, AXES[chain][2], s) for p, s in zip(packed[1:], STEPS[1:])]
        merged = merge(table[chain], came, experts)
        sums.append(unweave(table[chain], *scatter(*merged, AXES[chain][1])))

    far_rows = rows_out(table[0], rows, hidden, pair, mine_w, other_w, [])
    layer_out, input_grad = rows_out(
        table[0], 0, hidden, pair, mine_w, other_w, [swap(r) for r in far_rows]
    )
    sums[2], layer_out, input_grad = lax.optimization_barrier((sums[2], layer_out, input_grad))

    parts = []
    for chain in range(CHAINS):
        own, came, last = scatter(*sums[chain], AXES[chain][0])
        parts.append(own + came[0].astype(jnp.float32) + last.astype(jnp.float32))

    grads = jnp.concatenate(parts, 1).transpose(2, 0, 1, 3)
    scaled = grads / loss_scale
    new_first = beta_first * first_moment + (1.0 - beta_first) * scaled
    new_second = beta_second * second_moment + (1.0 - beta_second) * scaled * scaled
    new_master = master - learn_rate * (new_first / bias_first) / (
        jnp.sqrt(new_second / bias_second) + adam_epsilon
    )

    return layer_out, input_grad, new_master, new_first, new_second


def solution(mesh):
    state = P(None, None, "group", "local")
    rows = P(("group", "local"), None)
    return jax.shard_map(
        shards,
        mesh=mesh,
        in_specs=(rows, rows, P(("group", "local")), P(), state, state, state),
        out_specs=(rows, rows, state, state, state),
        check_vma=False,
    )
```

```python
import functools
import jax
import jax.numpy as jnp
import numpy as np
from jax import lax
from jax.experimental import pallas as pl
from jax.experimental.pallas import tpu as pltpu
from jax.sharding import PartitionSpec as P

loss_scale = 4.0
beta_first = 0.9
beta_second = 0.95
learn_rate = 0.001
adam_epsilon = 1e-08
bias_first = 1.0 - 0.9**10
bias_second = 1.0 - 0.95**10

SIDE = 4
CHAINS = 3
BOTH = ("group", "local")
SHIFTS = (4, 2, 0)
AXES = ((2, 1, 0), (1, 0, 2), (0, 2, 1))


def place(coords, core):
    return ((coords[0] * SIDE + coords[1]) * SIDE + coords[2]) * 2 + core


def step_pairs(axis, offsets):
    pairs = []
    for group in range(SIDE**3):
        for core in range(2):
            coords = [group // 16, group // 4 % 4, group % 4]
            here = place(coords, core)
            coords[axis] ^= offsets[core]
            pairs.append((here, place(coords, core)))
    return pairs


CORE_PAIRS = [(i, i ^ 1) for i in range(2 * SIDE**3)]
ONE, BACK, ACROSS = (1, 3), (3, 1), (2, 2)
STEPS = ((0, 0), ONE, BACK, ACROSS)


def hop(value, axis, offsets):
    return lax.ppermute(value, BOTH, step_pairs(axis, offsets))


def swap(value):
    return lax.ppermute(value, BOTH, CORE_PAIRS)


def together(*values):
    return lax.optimization_barrier(values)


def contract_last(left, right):
    return lax.dot_general(
        left, right, (((1,), (1,)), ((), ())), preferred_element_type=jnp.float32
    )


def contract_first(left, right):
    return lax.dot_general(
        left, right, (((0,), (0,)), ((), ())), preferred_element_type=jnp.float32
    )


def matmul(left, right):
    return jnp.dot(left, right, preferred_element_type=jnp.float32)


VMEM = pl.BlockSpec(memory_space=pltpu.VMEM)
SMEM = pl.BlockSpec(memory_space=pltpu.SMEM)
LIMIT = pltpu.CompilerParams(vmem_limit_bytes=16 * 1024 * 1024)


def shape_of(*dims):
    return jax.ShapeDtypeStruct(dims, jnp.bfloat16)


def spots(core):
    return (0, 1 + core, 2 - core, 3)


def weave_kernel(table_ref, own, one, rest, out, turned):
    first = table_ref[8] == 0
    for m in range(3):
        for r in range(2):
            near = one[m, r].astype(jnp.float32)
            back = rest[0, m, r].astype(jnp.float32)
            turned[m, :, r] = own[m, r].astype(jnp.float32)
            turned[m, :, 2 + r] = jnp.where(first, near, back)
            turned[m, :, 4 + r] = jnp.where(first, back, near)
            turned[m, :, 6 + r] = rest[1, m, r].astype(jnp.float32)
    out[...] = turned[...].astype(jnp.bfloat16)


def weave(table, own, one, rest):
    _, _, experts, columns = own.shape
    return pl.pallas_call(
        weave_kernel,
        out_shape=shape_of(3, experts, 8, columns),
        in_specs=[SMEM] + [VMEM] * 3,
        out_specs=VMEM,
        scratch_shapes=[pltpu.VMEM((3, experts, 8, columns), jnp.float32)],
        compiler_params=LIMIT,
        name="weave",
    )(table, own, one, rest)


def unweave_kernel(table_ref, own, came, last, out, one, rest, turned):
    first = table_ref[8] == 0
    turned[...] = (
        own[...].astype(jnp.float32) + came[0].astype(jnp.float32) + last[...].astype(jnp.float32)
    )
    for m in range(3):
        for r in range(2):
            left = turned[m, :, 2 + r]
            right = turned[m, :, 4 + r]
            out[m, r] = turned[m, :, r]
            one[m, r] = jnp.where(first, left, right).astype(jnp.bfloat16)
            rest[0, m, r] = jnp.where(first, right, left).astype(jnp.bfloat16)
            rest[1, m, r] = turned[m, :, 6 + r].astype(jnp.bfloat16)


def unweave(table, own, came, last):
    _, experts, _, columns = own.shape
    return pl.pallas_call(
        unweave_kernel,
        out_shape=[
            jax.ShapeDtypeStruct((3, 2, experts, columns), jnp.float32),
            shape_of(3, 2, experts, columns),
            shape_of(2, 3, 2, experts, columns),
        ],
        in_specs=[SMEM] + [VMEM] * 3,
        out_specs=[VMEM] * 3,
        scratch_shapes=[pltpu.VMEM((3, experts, 8, columns), jnp.float32)],
        compiler_params=LIMIT,
        name="unweave",
    )(table, own, came, last)


def pick_kernel(table_ref, p0, p1, p2, p3, *outs):
    spot = spots(table_ref[8])
    for index, out in enumerate(outs):
        for k in range(2):
            e = table_ref[2 * index + k]
            for b, p in enumerate((p0, p1, p2, p3)):
                out[k, :, spot[b]] = p[:, e]


def pick(table, plane):
    columns = plane[0].shape[-1]
    return pl.pallas_call(
        pick_kernel,
        out_shape=[shape_of(2, 3, 4, 8, columns)] * 4,
        in_specs=[SMEM] + [VMEM] * 4,
        out_specs=[VMEM] * 4,
        compiler_params=LIMIT,
        name="pick",
    )(table, *plane)


def join_kernel(table_ref, a0, a1, a2, a3, keep, give):
    spot = spots(table_ref[8])
    for o, a in enumerate((a0, a1, a2, a3)):
        keep[:, spot[o]] = a[0]
        give[:, spot[o]] = a[1]


def join(table, arrived):
    columns = arrived[0].shape[-1]
    return pl.pallas_call(
        join_kernel,
        out_shape=[shape_of(3, 4, 32, columns)] * 2,
        in_specs=[SMEM] + [VMEM] * 4,
        out_specs=[VMEM] * 2,
        compiler_params=LIMIT,
        name="join",
    )(table, *arrived)


def work_kernel(
    table_ref, tok0, tok1, cot0, cot1, mask, keep, got, hidden, pair, own_term, far_term, turned
):
    core = table_ref[8]
    columns = keep.shape[-1]
    rows = tok0.shape[0]
    step = 256
    near = pl.multiple_of(core * columns, columns)
    far = pl.multiple_of((1 - core) * columns, columns)
    sides = [
        (pl.ds(start, columns), w[0:2].reshape(256, columns), w[2])
        for start, w in ((near, keep), (far, got))
    ]
    for b, (tok, cot) in enumerate(((tok0, cot0), (tok1, cot1))):
        for r in range(0, rows, step):
            here = slice(r, r + step)
            pre = d_hidden = 0.0
            for cols, w_pair, w_down in sides:
                pre = pre + contract_last(tok[here, cols], w_pair)
                d_hidden = d_hidden + contract_last(cot[here, cols], w_down)
            gate_pre = pre[:, :128]
            up_pre = pre[:, 128:]
            there = slice(rows * b + r, rows * b + r + step)
            chosen = mask[there]
            sigmoid_gate = jax.nn.sigmoid(gate_pre)
            act = gate_pre * sigmoid_gate
            d_hidden = chosen * d_hidden
            d_gate = d_hidden * up_pre * sigmoid_gate * (1.0 + gate_pre * (1.0 - sigmoid_gate))
            d_gate = d_gate.astype(jnp.bfloat16)
            d_up = (d_hidden * act).astype(jnp.bfloat16)
            out = (chosen * (act * up_pre)).astype(jnp.bfloat16)
            hidden[there] = out
            pair[there, :128] = d_gate
            pair[there, 128:] = d_up
            turned[:128, there] = d_gate.T
            turned[128:256, there] = d_up.T
            turned[256:, there] = out.T
    for start, out in ((near, own_term), (far, far_term)):
        for c in range(0, columns, step):
            cols = pl.ds(start + c, step)
            both = 0.0
            down = 0.0
            for b, (tok, cot) in enumerate(((tok0, cot0), (tok1, cot1))):
                there = slice(rows * b, rows * b + rows)
                both = both + matmul(turned[:256, there], tok[:, cols])
                down = down + matmul(turned[256:, there], cot[:, cols])
            out[0, :, c : c + step] = both[:128].astype(jnp.bfloat16)
            out[1, :, c : c + step] = both[128:].astype(jnp.bfloat16)
            out[2, :, c : c + step] = down.astype(jnp.bfloat16)


def work(table, rows_in, mask, keep, got):
    columns = keep.shape[-1]
    rows = mask.shape[0]
    return pl.pallas_call(
        work_kernel,
        out_shape=[
            shape_of(rows, 128),
            shape_of(rows, 256),
            shape_of(3, 128, columns),
            shape_of(3, 128, columns),
        ],
        in_specs=[SMEM] + [VMEM] * 7,
        out_specs=[VMEM] * 4,
        scratch_shapes=[pltpu.VMEM((384, rows), jnp.bfloat16)],
        compiler_params=pltpu.CompilerParams(vmem_limit_bytes=32 * 1024 * 1024),
        name="work",
    )(table, *rows_in, mask, keep.reshape(3, 128, columns), got.reshape(3, 128, columns))


def rows_kernel(first, table_ref, *refs):
    core = table_ref[8]
    hidden, pair, keep, got = refs[0:3], refs[3:6], refs[6:9], refs[9:12]
    added, (layer_out, grad_out) = refs[12:-2], refs[-2:]
    columns = keep[0].shape[-1]
    step = 512
    rows = slice(first, first + layer_out.shape[0])
    for side, w in ((core, keep), (1 - core, got)):
        start = pl.multiple_of(side * columns, columns)
        for c in range(0, columns, step):
            cols = pl.ds(start + c, step)
            part = slice(c, c + step)
            layer = 0.0
            grad = 0.0
            for chain in range(CHAINS):
                layer = layer + matmul(hidden[chain][rows], w[chain][2, :, part])
                w_pair = w[chain][0:2, :, part].reshape(256, step)
                grad = grad + matmul(pair[chain][rows], w_pair)
            layer = layer.astype(jnp.bfloat16)
            grad = grad.astype(jnp.bfloat16)
            if added:
                layer = layer + added[0][:, cols]
                grad = grad + added[1][:, cols]
            layer_out[:, cols] = layer
            grad_out[:, cols] = grad


def rows_out(table, first, hidden, pair, keep, got, added):
    columns = keep[0].shape[-1]
    rows = hidden[0].shape[0] // 2
    keep = [k.reshape(3, 128, columns) for k in keep]
    got = [g.reshape(3, 128, columns) for g in got]
    return pl.pallas_call(
        functools.partial(rows_kernel, first),
        out_shape=[shape_of(rows, 2 * columns)] * 2,
        in_specs=[SMEM] + [VMEM] * (12 + len(added)),
        out_specs=[VMEM] * 2,
        compiler_params=pltpu.CompilerParams(vmem_limit_bytes=32 * 1024 * 1024),
        name="rows_out",
    )(table, *hidden, *pair, *keep, *got, *added)


def cut_kernel(table_ref, own, got, *outs):
    spot = spots(table_ref[8])
    for o, out in enumerate(outs):
        out[0] = own[:, spot[o]]
        out[1] = got[:, spot[o]]


def cut(table, own, got):
    columns = own.shape[-1]
    return pl.pallas_call(
        cut_kernel,
        out_shape=[shape_of(2, 3, 32, columns)] * 4,
        in_specs=[SMEM] + [VMEM] * 2,
        out_specs=[VMEM] * 4,
        compiler_params=LIMIT,
        name="cut",
    )(table, own.reshape(3, 4, 32, columns), got.reshape(3, 4, 32, columns))


def merge_kernel(table_ref, c0, c1, c2, c3, own, one, rest, total):
    spot = spots(table_ref[8])
    total[...] = jnp.zeros_like(total)
    for index, came in enumerate((c0, c1, c2, c3)):
        for k in range(2):
            e = table_ref[2 * index + k]
            for p in range(4):
                total[p, :, e] += came[k, :, p].astype(jnp.float32)
    own[...] = total[0].astype(jnp.bfloat16)
    one[...] = total[spot[1]].astype(jnp.bfloat16)
    rest[0] = total[spot[2]].astype(jnp.bfloat16)
    rest[1] = total[3].astype(jnp.bfloat16)


def merge(table, came, experts):
    columns = came[0].shape[-1]
    return pl.pallas_call(
        merge_kernel,
        out_shape=[shape_of(*lead, 3, experts, 8, columns) for lead in ((), (), (2,))],
        in_specs=[SMEM] + [VMEM] * 4,
        out_specs=[VMEM] * 3,
        scratch_shapes=[pltpu.VMEM((4, 3, experts, 8, columns), jnp.float32)],
        compiler_params=LIMIT,
        name="merge",
    )(table, *[c.reshape(2, 3, 4, 8, columns) for c in came])


def shards(tokens, cotangent, row_slot, placement, master, first_moment, second_moment):
    group = lax.axis_index("group")
    core = lax.axis_index("local")
    experts = master.shape[0]
    columns = master.shape[3]
    rows = tokens.shape[0]

    steps = np.array(
        [[[step[c] << SHIFTS[axes[2]] for step in STEPS] for axes in AXES] for c in range(2)], np.int32
    ).reshape(2, -1)
    there = group ^ jnp.where(core == 0, jnp.asarray(steps[0]), jnp.asarray(steps[1]))
    seen = there[:, None] == jnp.arange(SIDE**3)[None]
    pairs = jnp.sum(jnp.where(seen[:, :, None], placement[None], 0), 1)
    pairs = jnp.where(core == 0, pairs, pairs[:, ::-1]).reshape(CHAINS, 2 * SIDE)
    table = jnp.concatenate([pairs, jnp.full((CHAINS, 1), core)], 1)

    narrow = master.astype(jnp.bfloat16).transpose(1, 2, 0, 3)
    near = [axes[0] for axes in AXES]
    mid = [axes[1] for axes in AXES]
    last = [axes[2] for axes in AXES]
    each = range(CHAINS)
    blocks = [narrow[:, 2 * c : 2 * c + 2] for c in each]
    ones, tokens, cotangent, row_slot = together(
        [hop(blocks[c], near[c], ONE) for c in each], tokens, cotangent, row_slot
    )
    rests = [hop(jnp.stack([blocks[c], ones[c]], 0), near[c], BACK) for c in each]
    rows_in = [tokens, swap(tokens), cotangent, swap(cotangent)]
    slots = jnp.concatenate([row_slot, swap(row_slot)], 0)
    chosen = jnp.broadcast_to((slots == core)[:, None], (2 * rows, 128)).astype(jnp.float32)
    rests, rows_in, chosen = together(rests, rows_in, chosen)
    (lines,) = together([weave(table[c], blocks[c], ones[c], rests[c]) for c in each])
    backs = [hop(lines[c], mid[c], BACK) for c in each]
    (ones,) = together([hop(lines[c], mid[c], ONE) for c in each])
    acrosses = [hop(ones[c], mid[c], BACK) for c in each]
    backs, acrosses = together(backs, acrosses)
    packed = [pick(table[c], [lines[c], ones[c], backs[c], acrosses[c]]) for c in each]
    (packed,) = together(packed)
    acrosses = [hop(packed[c][3], last[c], ACROSS) for c in each]
    (ones,) = together([hop(packed[c][1], last[c], ONE) for c in each])
    backs = [hop(packed[c][2], last[c], BACK) for c in each]
    mine_w = []
    other_w = []
    for c in each:
        arrived = [packed[c][0], ones[c], backs[c], acrosses[c]]
        keep, give = join(table[c], [a.reshape(2, 3, 32, columns) for a in arrived])
        mine_w.append(keep)
        other_w.append(swap(give))

    hidden = []
    pair = []
    sent = []
    for chain in range(CHAINS):
        if chain == 2:
            other_w[2], sent[0] = lax.optimization_barrier((other_w[2], sent[0]))
        one_hidden, one_pair, own, far = work(
            table[chain], rows_in, chosen, mine_w[chain], other_w[chain]
        )
        hidden.append(one_hidden)
        pair.append(one_pair)
        sent.append(cut(table[chain], own, swap(far)))

    merged = []
    for c in each:
        came = [sent[c][0]] + [hop(p, last[c], s) for p, s in zip(sent[c][1:], STEPS[1:])]
        merged.append(merge(table[c], came, experts))

    def add(one, came):
        return (one.astype(jnp.float32) + came[1].astype(jnp.float32)).astype(jnp.bfloat16)

    def scatter(parts, axes):
        (came,) = together([hop(parts[c][2], axes[c], BACK) for c in each])
        (ones,) = together([add(parts[c][1], came[c]) for c in each])
        (ones,) = together([hop(ones[c], axes[c], ONE) for c in each])
        return [(parts[c][0], came[c], ones[c]) for c in each]

    merged = scatter(merged, mid)
    sums = [unweave(table[c], *merged[c]) for c in each]

    far_rows = rows_out(table[0], rows, hidden, pair, mine_w, other_w, [])
    layer_out, input_grad = rows_out(
        table[0], 0, hidden, pair, mine_w, other_w, [swap(r) for r in far_rows]
    )
    sums, layer_out, input_grad = together(sums, layer_out, input_grad)
    parts = [
        own + came[0].astype(jnp.float32) + one.astype(jnp.float32)
        for own, came, one in scatter(sums, near)
    ]

    grads = jnp.concatenate(parts, 1).transpose(2, 0, 1, 3)
    scaled = grads / loss_scale
    new_first = beta_first * first_moment + (1.0 - beta_first) * scaled
    new_second = beta_second * second_moment + (1.0 - beta_second) * scaled * scaled
    new_master = master - learn_rate * (new_first / bias_first) / (
        jnp.sqrt(new_second / bias_second) + adam_epsilon
    )

    return layer_out, input_grad, new_master, new_first, new_second


def solution(mesh):
    state = P(None, None, "group", "local")
    rows = P(("group", "local"), None)
    return jax.shard_map(
        shards,
        mesh=mesh,
        in_specs=(rows, rows, P(("group", "local")), P(), state, state, state),
        out_specs=(rows, rows, state, state, state),
        check_vma=False,
    )
```

```python
import functools
import jax
import jax.numpy as jnp
import numpy as np
from jax import lax
from jax.experimental import pallas as pl
from jax.experimental.pallas import tpu as pltpu
from jax.sharding import PartitionSpec as P

loss_scale = 4.0
beta_first = 0.9
beta_second = 0.95
learn_rate = 0.001
adam_epsilon = 1e-08
bias_first = 1.0 - 0.9**10
bias_second = 1.0 - 0.95**10

SIDE = 4
CHAINS = 3
BOTH = ("group", "local")
SHIFTS = (4, 2, 0)
AXES = ((2, 1, 0), (1, 0, 2), (0, 2, 1))


def place(coords, core):
    return ((coords[0] * SIDE + coords[1]) * SIDE + coords[2]) * 2 + core


def step_pairs(axis, offsets):
    pairs = []
    for group in range(SIDE**3):
        for core in range(2):
            coords = [group // 16, group // 4 % 4, group % 4]
            here = place(coords, core)
            coords[axis] ^= offsets[core]
            pairs.append((here, place(coords, core)))
    return pairs


CORE_PAIRS = [(i, i ^ 1) for i in range(2 * SIDE**3)]
ONE, BACK, ACROSS = (1, 3), (3, 1), (2, 2)
STEPS = ((0, 0), ONE, BACK, ACROSS)


def hop(value, axis, offsets):
    return lax.ppermute(value, BOTH, step_pairs(axis, offsets))


def swap(value):
    return lax.ppermute(value, BOTH, CORE_PAIRS)


def together(*values):
    return lax.optimization_barrier(values)


def contract_last(left, right):
    return lax.dot_general(
        left, right, (((1,), (1,)), ((), ())), preferred_element_type=jnp.float32
    )


def contract_first(left, right):
    return lax.dot_general(
        left, right, (((0,), (0,)), ((), ())), preferred_element_type=jnp.float32
    )


def matmul(left, right):
    return jnp.dot(left, right, preferred_element_type=jnp.float32)


VMEM = pl.BlockSpec(memory_space=pltpu.VMEM)
SMEM = pl.BlockSpec(memory_space=pltpu.SMEM)
LIMIT = pltpu.CompilerParams(vmem_limit_bytes=16 * 1024 * 1024)


def shape_of(*dims):
    return jax.ShapeDtypeStruct(dims, jnp.bfloat16)


def spots(core):
    return (0, 1 + core, 2 - core, 3)


def weave_kernel(table_ref, own, one, rest, out, turned):
    first = table_ref[8] == 0
    for m in range(3):
        for r in range(2):
            near = one[m, r].astype(jnp.float32)
            back = rest[0, m, r].astype(jnp.float32)
            turned[m, :, r] = own[m, r].astype(jnp.float32)
            turned[m, :, 2 + r] = jnp.where(first, near, back)
            turned[m, :, 4 + r] = jnp.where(first, back, near)
            turned[m, :, 6 + r] = rest[1, m, r].astype(jnp.float32)
    out[...] = turned[...].astype(jnp.bfloat16)


def weave(table, own, one, rest):
    _, _, experts, columns = own.shape
    return pl.pallas_call(
        weave_kernel,
        out_shape=shape_of(3, experts, 8, columns),
        in_specs=[SMEM] + [VMEM] * 3,
        out_specs=VMEM,
        scratch_shapes=[pltpu.VMEM((3, experts, 8, columns), jnp.float32)],
        compiler_params=LIMIT,
        name="weave",
    )(table, own, one, rest)


def unweave_kernel(table_ref, own, came, last, out, one, rest, turned):
    first = table_ref[8] == 0
    turned[...] = (
        own[...].astype(jnp.float32) + came[0].astype(jnp.float32) + last[...].astype(jnp.float32)
    )
    for m in range(3):
        for r in range(2):
            left = turned[m, :, 2 + r]
            right = turned[m, :, 4 + r]
            out[m, r] = turned[m, :, r]
            one[m, r] = jnp.where(first, left, right).astype(jnp.bfloat16)
            rest[0, m, r] = jnp.where(first, right, left).astype(jnp.bfloat16)
            rest[1, m, r] = turned[m, :, 6 + r].astype(jnp.bfloat16)


def unweave(table, own, came, last):
    _, experts, _, columns = own.shape
    return pl.pallas_call(
        unweave_kernel,
        out_shape=[
            jax.ShapeDtypeStruct((3, 2, experts, columns), jnp.float32),
            shape_of(3, 2, experts, columns),
            shape_of(2, 3, 2, experts, columns),
        ],
        in_specs=[SMEM] + [VMEM] * 3,
        out_specs=[VMEM] * 3,
        scratch_shapes=[pltpu.VMEM((3, experts, 8, columns), jnp.float32)],
        compiler_params=LIMIT,
        name="unweave",
    )(table, own, came, last)


def pick_kernel(table_ref, p0, p1, p2, p3, *outs):
    spot = spots(table_ref[8])
    for index, out in enumerate(outs):
        for k in range(2):
            e = table_ref[2 * index + k]
            for b, p in enumerate((p0, p1, p2, p3)):
                out[k, :, spot[b]] = p[:, e]


def pick(table, plane):
    columns = plane[0].shape[-1]
    return pl.pallas_call(
        pick_kernel,
        out_shape=[shape_of(2, 3, 4, 8, columns)] * 4,
        in_specs=[SMEM] + [VMEM] * 4,
        out_specs=[VMEM] * 4,
        compiler_params=LIMIT,
        name="pick",
    )(table, *plane)


def first_kernel(table_ref, tok0, tok1, cot0, cot1, mask, a0, a1, a2, a3, sums, weights):
    core = table_ref[8]
    columns = a0.shape[-1]
    rows = tok0.shape[0]
    step = 256
    for spot, a in zip(spots(core), (a0, a1, a2, a3)):
        weights[:, :, spot] = a[...]
    half = pl.ds(pl.multiple_of(core * columns, columns), columns)
    w = [
        (weights[k, 0:2].reshape(256, columns), weights[k, 2].reshape(128, columns))
        for k in range(2)
    ]
    for b, (tok, cot) in enumerate(((tok0, cot0), (tok1, cot1))):
        for r in range(0, rows, step):
            here = slice(r, r + step)
            there = slice(rows * b + r, rows * b + r + step)
            chosen = mask[there] > 0.0
            tok_part = tok[here, half]
            cot_part = cot[here, half]
            pre = [contract_last(tok_part, w[k][0]) for k in range(2)]
            d_hidden = [contract_last(cot_part, w[k][1]) for k in range(2)]
            sums[0, there] = jnp.where(chosen, pre[0][:, :128], pre[1][:, :128])
            sums[1, there] = jnp.where(chosen, pre[0][:, 128:], pre[1][:, 128:])
            sums[2, there] = jnp.where(chosen, d_hidden[0], d_hidden[1])


def first(table, rows_in, mask, arrived):
    columns = arrived[0].shape[-1]
    rows = mask.shape[0]
    return pl.pallas_call(
        first_kernel,
        out_shape=[
            jax.ShapeDtypeStruct((3, rows, 128), jnp.float32),
            shape_of(2, 3, 4, 32, columns),
        ],
        in_specs=[SMEM] + [VMEM] * 9,
        out_specs=[VMEM] * 2,
        compiler_params=pltpu.CompilerParams(vmem_limit_bytes=24 * 1024 * 1024),
        name="first",
    )(table, *rows_in, mask, *arrived)


def second_kernel(
    table_ref, tok0, tok1, cot0, cot1, mask, sums, got, o0, o1, o2, o3, hidden, pair, turned
):
    core = table_ref[8]
    columns = o0.shape[-1]
    rows = tok0.shape[0]
    step = 256
    for r in range(0, 2 * rows, step):
        here = slice(r, r + step)
        there = slice((r + rows) % (2 * rows), (r + rows) % (2 * rows) + step)
        gate_pre = sums[0, here] + got[0, there]
        up_pre = sums[1, here] + got[1, there]
        d_hidden = sums[2, here] + got[2, there]
        sigmoid_gate = jax.nn.sigmoid(gate_pre)
        act = gate_pre * sigmoid_gate
        d_gate = d_hidden * up_pre * sigmoid_gate * (1.0 + gate_pre * (1.0 - sigmoid_gate))
        three = (d_gate, d_hidden * act, act * up_pre)
        chosen = mask[here] > 0.0
        for k in range(2):
            for m in range(3):
                part = jnp.where(chosen, three[m], 0.0) if k == 0 else jnp.where(chosen, 0.0, three[m])
                part = part.astype(jnp.bfloat16)
                if m < 2:
                    pair[here, 256 * k + 128 * m : 256 * k + 128 * m + 128] = part
                else:
                    hidden[here, 128 * k : 128 * k + 128] = part
                line = 256 * k + 128 * m if m < 2 else 512 + 128 * k
                turned[line : line + 128, here] = part.T
    start = pl.multiple_of(core * columns, columns)
    swapped = core == 1
    for c in range(0, columns, step):
        cols = pl.ds(start + c, step)
        out_cols = slice(c, c + step)
        both = matmul(turned[:512, :rows], tok0[:, cols]) + matmul(turned[:512, rows:], tok1[:, cols])
        down = matmul(turned[512:, :rows], cot0[:, cols]) + matmul(turned[512:, rows:], cot1[:, cols])
        for k in range(2):
            for m in range(3):
                line = both[256 * k + 128 * m :][:128] if m < 2 else down[128 * k :][:128]
                line = line.astype(jnp.bfloat16)
                q = [line[32 * i : 32 * i + 32] for i in range(4)]
                o0[k, m, :, out_cols] = q[0]
                o1[k, m, :, out_cols] = jnp.where(swapped, q[2], q[1])
                o2[k, m, :, out_cols] = jnp.where(swapped, q[1], q[2])
                o3[k, m, :, out_cols] = q[3]


def second(table, rows_in, mask, sums, got, columns):
    rows = mask.shape[0]
    return pl.pallas_call(
        second_kernel,
        out_shape=[shape_of(2, 3, 32, columns)] * 4 + [shape_of(rows, 256), shape_of(rows, 512)],
        in_specs=[SMEM] + [VMEM] * 7,
        out_specs=[VMEM] * 6,
        scratch_shapes=[pltpu.VMEM((768, rows), jnp.bfloat16)],
        compiler_params=pltpu.CompilerParams(vmem_limit_bytes=24 * 1024 * 1024),
        name="second",
    )(table, *rows_in, mask, sums, got)


def rows_kernel(start, table_ref, *refs):
    hidden, pair, weights = refs[0:3], refs[3:6], refs[6:9]
    added, (layer_out, grad_out) = refs[9:-2], refs[-2:]
    columns = weights[0].shape[-1]
    rows = slice(start, start + layer_out.shape[0])
    step = 512
    if added:
        core = table_ref[8]
        near = pl.multiple_of(core * columns, columns)
        far = pl.ds(pl.multiple_of((1 - core) * columns, columns), columns)
        layer_out[:, far] = added[0][...]
        grad_out[:, far] = added[1][...]
    for c in range(0, columns, step):
        part = slice(c, c + step)
        cols = pl.ds(near + c, step) if added else part
        layer = 0.0
        grad = 0.0
        for chain in range(CHAINS):
            w = weights[chain]
            down = jnp.concatenate([w[k, 2, :, :, part].reshape(128, step) for k in range(2)], 0)
            layer = layer + matmul(hidden[chain][rows], down)
            for k in range(2):
                both = w[k, 0:2, :, :, part].reshape(256, step)
                grad = grad + matmul(pair[chain][rows, 256 * k : 256 * k + 256], both)
        layer_out[:, cols] = layer.astype(jnp.bfloat16)
        grad_out[:, cols] = grad.astype(jnp.bfloat16)


def rows_out(table, start, hidden, pair, weights, added):
    columns = weights[0].shape[-1]
    rows = hidden[0].shape[0] // 2
    return pl.pallas_call(
        functools.partial(rows_kernel, start),
        out_shape=[shape_of(rows, 2 * columns if added else columns)] * 2,
        in_specs=[SMEM] + [VMEM] * (9 + len(added)),
        out_specs=[VMEM] * 2,
        compiler_params=pltpu.CompilerParams(vmem_limit_bytes=24 * 1024 * 1024),
        name="rows_out",
    )(table, *hidden, *pair, *weights, *added)


def merge_kernel(table_ref, c0, c1, c2, c3, own, one, rest, total):
    spot = spots(table_ref[8])
    total[...] = jnp.zeros_like(total)
    for index, came in enumerate((c0, c1, c2, c3)):
        for k in range(2):
            e = table_ref[2 * index + k]
            for p in range(4):
                total[p, :, e] += came[k, :, p].astype(jnp.float32)
    own[...] = total[0].astype(jnp.bfloat16)
    one[...] = total[spot[1]].astype(jnp.bfloat16)
    rest[0] = total[spot[2]].astype(jnp.bfloat16)
    rest[1] = total[3].astype(jnp.bfloat16)


def merge(table, came, experts):
    columns = came[0].shape[-1]
    return pl.pallas_call(
        merge_kernel,
        out_shape=[shape_of(*lead, 3, experts, 8, columns) for lead in ((), (), (2,))],
        in_specs=[SMEM] + [VMEM] * 4,
        out_specs=[VMEM] * 3,
        scratch_shapes=[pltpu.VMEM((4, 3, experts, 8, columns), jnp.float32)],
        compiler_params=LIMIT,
        name="merge",
    )(table, *[c.reshape(2, 3, 4, 8, columns) for c in came])


def shards(tokens, cotangent, row_slot, placement, master, first_moment, second_moment):
    group = lax.axis_index("group")
    core = lax.axis_index("local")
    experts = master.shape[0]
    columns = master.shape[3]
    rows = tokens.shape[0]

    steps = np.array(
        [[[step[c] << SHIFTS[axes[2]] for step in STEPS] for axes in AXES] for c in range(2)], np.int32
    ).reshape(2, -1)
    there = group ^ jnp.where(core == 0, jnp.asarray(steps[0]), jnp.asarray(steps[1]))
    seen = there[:, None] == jnp.arange(SIDE**3)[None]
    pairs = jnp.sum(jnp.where(seen[:, :, None], placement[None], 0), 1)
    pairs = pairs.reshape(CHAINS, 2 * SIDE)
    table = jnp.concatenate([pairs, jnp.full((CHAINS, 1), core)], 1)

    narrow = master.astype(jnp.bfloat16).transpose(1, 2, 0, 3)
    near = [axes[0] for axes in AXES]
    mid = [axes[1] for axes in AXES]
    last = [axes[2] for axes in AXES]
    each = range(CHAINS)
    blocks = [narrow[:, 2 * c : 2 * c + 2] for c in each]
    (ones,) = together([hop(blocks[c], near[c], ONE) for c in each])
    rests = [hop(jnp.stack([blocks[c], ones[c]], 0), near[c], BACK) for c in each]
    rows_in = [tokens, swap(tokens), cotangent, swap(cotangent)]
    slots = jnp.concatenate([row_slot, swap(row_slot)], 0)
    chosen = jnp.broadcast_to((slots == 0)[:, None], (2 * rows, 128)).astype(jnp.float32)
    rests, rows_in, chosen = together(rests, rows_in, chosen)
    (lines,) = together([weave(table[c], blocks[c], ones[c], rests[c]) for c in each])
    backs = [hop(lines[c], mid[c], BACK) for c in each]
    (ones,) = together([hop(lines[c], mid[c], ONE) for c in each])
    acrosses = [hop(ones[c], mid[c], BACK) for c in each]
    backs, acrosses = together(backs, acrosses)
    packed = [pick(table[c], [lines[c], ones[c], backs[c], acrosses[c]]) for c in each]
    (packed,) = together(packed)
    arrived = [
        [packed[c][0]] + [hop(p, last[c], s) for p, s in zip(packed[c][1:], STEPS[1:])] for c in each
    ]
    (arrived,) = together(arrived)

    sums = []
    weights = []
    for c in each:
        blocks = [a.reshape(2, 3, 32, columns) for a in arrived[c]]
        one_sums, one_weights = first(table[c], rows_in, chosen, blocks)
        sums.append(one_sums)
        weights.append(one_weights)
    got = [swap(v) for v in sums]
    sent = []
    hidden = []
    pair = []
    for c in each:
        *packed, one_hidden, one_pair = second(table[c], rows_in, chosen, sums[c], got[c], columns)
        sent.append(packed)
        hidden.append(one_hidden)
        pair.append(one_pair)

    merged = []
    for c in each:
        came = [sent[c][0]] + [hop(p, last[c], s) for p, s in zip(sent[c][1:], STEPS[1:])]
        merged.append(merge(table[c], came, experts))

    def add(one, came):
        return (one.astype(jnp.float32) + came[1].astype(jnp.float32)).astype(jnp.bfloat16)

    def scatter(parts, axes):
        (came,) = together([hop(parts[c][2], axes[c], BACK) for c in each])
        (ones,) = together([add(parts[c][1], came[c]) for c in each])
        (ones,) = together([hop(ones[c], axes[c], ONE) for c in each])
        return [(parts[c][0], came[c], ones[c]) for c in each]

    merged = scatter(merged, mid)
    sums = [unweave(table[c], *merged[c]) for c in each]

    far_rows = rows_out(table[0], rows, hidden, pair, weights, [])
    layer_out, input_grad = rows_out(
        table[0], 0, hidden, pair, weights, [swap(r) for r in far_rows]
    )
    sums, layer_out, input_grad = together(sums, layer_out, input_grad)
    parts = [
        own + came[0].astype(jnp.float32) + one.astype(jnp.float32)
        for own, came, one in scatter(sums, near)
    ]

    grads = jnp.concatenate(parts, 1).transpose(2, 0, 1, 3)
    scaled = grads / loss_scale
    new_first = beta_first * first_moment + (1.0 - beta_first) * scaled
    new_second = beta_second * second_moment + (1.0 - beta_second) * scaled * scaled
    new_master = master - learn_rate * (new_first / bias_first) / (
        jnp.sqrt(new_second / bias_second) + adam_epsilon
    )

    return layer_out, input_grad, new_master, new_first, new_second


def solution(mesh):
    state = P(None, None, "group", "local")
    rows = P(("group", "local"), None)
    return jax.shard_map(
        shards,
        mesh=mesh,
        in_specs=(rows, rows, P(("group", "local")), P(), state, state, state),
        out_specs=(rows, rows, state, state, state),
        check_vma=False,
    )
```

```python
import functools
import jax
import jax.numpy as jnp
import numpy as np
from jax import lax
from jax.experimental import pallas as pl
from jax.experimental.pallas import tpu as pltpu
from jax.sharding import PartitionSpec as P

loss_scale = 4.0
beta_first = 0.9
beta_second = 0.95
learn_rate = 0.001
adam_epsilon = 1e-08
bias_first = 1.0 - 0.9**10
bias_second = 1.0 - 0.95**10

SIDE = 4
CHAINS = 3
BOTH = ("group", "local")
SHIFTS = (4, 2, 0)
AXES = ((2, 1, 0), (1, 0, 2), (0, 2, 1))


def place(coords, core):
    return ((coords[0] * SIDE + coords[1]) * SIDE + coords[2]) * 2 + core


def step_pairs(axis, offsets):
    pairs = []
    for group in range(SIDE**3):
        for core in range(2):
            coords = [group // 16, group // 4 % 4, group % 4]
            here = place(coords, core)
            coords[axis] ^= offsets[core]
            pairs.append((here, place(coords, core)))
    return pairs


CORE_PAIRS = [(i, i ^ 1) for i in range(2 * SIDE**3)]
ONE, BACK, ACROSS = (1, 3), (3, 1), (2, 2)
STEPS = ((0, 0), ONE, BACK, ACROSS)


def hop(value, axis, offsets):
    return lax.ppermute(value, BOTH, step_pairs(axis, offsets))


def swap(value):
    return lax.ppermute(value, BOTH, CORE_PAIRS)


def together(*values):
    return lax.optimization_barrier(values)


def contract_last(left, right):
    return lax.dot_general(
        left, right, (((1,), (1,)), ((), ())), preferred_element_type=jnp.float32
    )


def contract_first(left, right):
    return lax.dot_general(
        left, right, (((0,), (0,)), ((), ())), preferred_element_type=jnp.float32
    )


def matmul(left, right):
    return jnp.dot(left, right, preferred_element_type=jnp.float32)


VMEM = pl.BlockSpec(memory_space=pltpu.VMEM)
SMEM = pl.BlockSpec(memory_space=pltpu.SMEM)
LIMIT = pltpu.CompilerParams(vmem_limit_bytes=16 * 1024 * 1024)


def shape_of(*dims):
    return jax.ShapeDtypeStruct(dims, jnp.bfloat16)


def spots(core):
    return (0, 1 + core, 2 - core, 3)


def weave_kernel(table_ref, own, one, rest, out, turned):
    first = table_ref[8] == 0
    for m in range(3):
        for r in range(2):
            near = one[m, r].astype(jnp.float32)
            back = rest[0, m, r].astype(jnp.float32)
            turned[m, :, r] = own[m, r].astype(jnp.float32)
            turned[m, :, 2 + r] = jnp.where(first, near, back)
            turned[m, :, 4 + r] = jnp.where(first, back, near)
            turned[m, :, 6 + r] = rest[1, m, r].astype(jnp.float32)
    out[...] = turned[...].astype(jnp.bfloat16)


def weave(table, own, one, rest):
    _, _, experts, columns = own.shape
    return pl.pallas_call(
        weave_kernel,
        out_shape=shape_of(3, experts, 8, columns),
        in_specs=[SMEM] + [VMEM] * 3,
        out_specs=VMEM,
        scratch_shapes=[pltpu.VMEM((3, experts, 8, columns), jnp.float32)],
        compiler_params=LIMIT,
        name="weave",
    )(table, own, one, rest)


def unweave_kernel(table_ref, own, came, last, out, one, rest, turned):
    first = table_ref[8] == 0
    turned[...] = (
        own[...].astype(jnp.float32) + came[0].astype(jnp.float32) + last[...].astype(jnp.float32)
    )
    for m in range(3):
        for r in range(2):
            left = turned[m, :, 2 + r]
            right = turned[m, :, 4 + r]
            out[m, r] = turned[m, :, r]
            one[m, r] = jnp.where(first, left, right).astype(jnp.bfloat16)
            rest[0, m, r] = jnp.where(first, right, left).astype(jnp.bfloat16)
            rest[1, m, r] = turned[m, :, 6 + r].astype(jnp.bfloat16)


def unweave(table, own, came, last):
    _, experts, _, columns = own.shape
    return pl.pallas_call(
        unweave_kernel,
        out_shape=[
            jax.ShapeDtypeStruct((3, 2, experts, columns), jnp.float32),
            shape_of(3, 2, experts, columns),
            shape_of(2, 3, 2, experts, columns),
        ],
        in_specs=[SMEM] + [VMEM] * 3,
        out_specs=[VMEM] * 3,
        scratch_shapes=[pltpu.VMEM((3, experts, 8, columns), jnp.float32)],
        compiler_params=LIMIT,
        name="unweave",
    )(table, own, came, last)


def pick_kernel(table_ref, p0, p1, p2, p3, own, ahead, back):
    spot = spots(table_ref[8])
    for index, out in enumerate((own, ahead.at[0], back, ahead.at[1])):
        for k in range(2):
            e = table_ref[2 * index + k]
            for b, p in enumerate((p0, p1, p2, p3)):
                out[k, :, spot[b]] = p[:, e]


def pick(table, plane):
    columns = plane[0].shape[-1]
    return pl.pallas_call(
        pick_kernel,
        out_shape=[shape_of(*lead, 2, 3, 4, 8, columns) for lead in ((), (2,), ())],
        in_specs=[SMEM] + [VMEM] * 4,
        out_specs=[VMEM] * 3,
        compiler_params=LIMIT,
        name="pick",
    )(table, *plane)


def first_kernel(table_ref, tok0, tok1, cot0, cot1, mask, own, came, back, across, sums, weights):
    core = table_ref[8]
    columns = own.shape[-1]
    rows = tok0.shape[0]
    for spot, a in zip(spots(core), (own, came.at[0], back, across)):
        weights[:, :, spot] = a[...]
    half = pl.ds(pl.multiple_of(core * columns, columns), columns)
    w_pair = jnp.concatenate([weights[k, 0:2].reshape(256, columns) for k in range(2)], 0)
    w_down = jnp.concatenate([weights[k, 2].reshape(128, columns) for k in range(2)], 0)
    parts = ((tok0[:, half], cot0[:, half]), (tok1[...], cot1[...]))
    for b, (tok, cot) in enumerate(parts):
        here = slice(rows * b, rows * b + rows)
        chosen = mask[here] > 0.0
        pre = contract_last(tok, w_pair)
        d_hidden = contract_last(cot, w_down)
        sums[0, here] = jnp.where(chosen, pre[:, :128], pre[:, 256:384])
        sums[1, here] = jnp.where(chosen, pre[:, 128:256], pre[:, 384:])
        sums[2, here] = jnp.where(chosen, d_hidden[:, :128], d_hidden[:, 128:])


def first(table, rows_in, mask, arrived):
    columns = arrived[0].shape[-1]
    rows = mask.shape[0]
    return pl.pallas_call(
        first_kernel,
        out_shape=[
            jax.ShapeDtypeStruct((3, rows, 128), jnp.float32),
            shape_of(2, 3, 4, 32, columns),
        ],
        in_specs=[SMEM] + [VMEM] * 9,
        out_specs=[VMEM] * 2,
        compiler_params=pltpu.CompilerParams(vmem_limit_bytes=24 * 1024 * 1024),
        name="first",
    )(table, *rows_in, mask, *arrived)


def second_kernel(
    table_ref, tok0, tok1, cot0, cot1, mask, sums, got, own, ahead, back, hidden, pair, turned
):
    core = table_ref[8]
    columns = own.shape[-1]
    rows = tok0.shape[0]
    step = 256
    for r in range(0, 2 * rows, step):
        here = slice(r, r + step)
        there = slice((r + rows) % (2 * rows), (r + rows) % (2 * rows) + step)
        gate_pre = sums[0, here] + got[0, there]
        up_pre = sums[1, here] + got[1, there]
        d_hidden = sums[2, here] + got[2, there]
        sigmoid_gate = jax.nn.sigmoid(gate_pre)
        act = gate_pre * sigmoid_gate
        d_gate = d_hidden * up_pre * sigmoid_gate * (1.0 + gate_pre * (1.0 - sigmoid_gate))
        three = (d_gate, d_hidden * act, act * up_pre)
        chosen = mask[here] > 0.0
        for k in range(2):
            for m in range(3):
                part = jnp.where(chosen, three[m], 0.0) if k == 0 else jnp.where(chosen, 0.0, three[m])
                part = part.astype(jnp.bfloat16)
                if m < 2:
                    pair[here, 256 * k + 128 * m : 256 * k + 128 * m + 128] = part
                else:
                    hidden[here, 128 * k : 128 * k + 128] = part
                line = 256 * k + 128 * m if m < 2 else 512 + 128 * k
                turned[line : line + 128, here] = part.T
    start = pl.multiple_of(core * columns, columns)
    swapped = core == 1
    for c in range(0, columns, step):
        cols = pl.ds(start + c, step)
        out_cols = slice(c, c + step)
        both = matmul(turned[:512, :rows], tok0[:, cols]) + matmul(
            turned[:512, rows:], tok1[:, out_cols]
        )
        down = matmul(turned[512:, :rows], cot0[:, cols]) + matmul(
            turned[512:, rows:], cot1[:, out_cols]
        )
        for k in range(2):
            for m in range(3):
                line = both[256 * k + 128 * m :][:128] if m < 2 else down[128 * k :][:128]
                line = line.astype(jnp.bfloat16)
                q = [line[32 * i : 32 * i + 32] for i in range(4)]
                own[k, m, :, out_cols] = q[0]
                ahead[0, k, m, :, out_cols] = jnp.where(swapped, q[2], q[1])
                back[k, m, :, out_cols] = jnp.where(swapped, q[1], q[2])
                ahead[1, k, m, :, out_cols] = q[3]


def second(table, rows_in, mask, sums, got, columns):
    rows = mask.shape[0]
    return pl.pallas_call(
        second_kernel,
        out_shape=[shape_of(*lead, 2, 3, 32, columns) for lead in ((), (2,), ())]
        + [shape_of(rows, 256), shape_of(rows, 512)],
        in_specs=[SMEM] + [VMEM] * 7,
        out_specs=[VMEM] * 5,
        scratch_shapes=[pltpu.VMEM((768, rows), jnp.bfloat16)],
        compiler_params=pltpu.CompilerParams(vmem_limit_bytes=24 * 1024 * 1024),
        name="second",
    )(table, *rows_in, mask, sums, got)


def rows_kernel(start, table_ref, *refs):
    hidden, pair, weights = refs[0:3], refs[3:6], refs[6:9]
    added, (layer_out, grad_out) = refs[9:-2], refs[-2:]
    columns = weights[0].shape[-1]
    rows = slice(start, start + layer_out.shape[0])
    step = 512
    if added:
        core = table_ref[8]
        near = pl.multiple_of(core * columns, columns)
        far = pl.ds(pl.multiple_of((1 - core) * columns, columns), columns)
        layer_out[:, far] = added[0][...]
        grad_out[:, far] = added[1][...]
    for c in range(0, columns, step):
        part = slice(c, c + step)
        cols = pl.ds(near + c, step) if added else part
        layer = 0.0
        grad = 0.0
        for chain in range(CHAINS):
            w = weights[chain]
            down = jnp.concatenate([w[k, 2, :, :, part].reshape(128, step) for k in range(2)], 0)
            layer = layer + matmul(hidden[chain][rows], down)
            for k in range(2):
                both = w[k, 0:2, :, :, part].reshape(256, step)
                grad = grad + matmul(pair[chain][rows, 256 * k : 256 * k + 256], both)
        layer_out[:, cols] = layer.astype(jnp.bfloat16)
        grad_out[:, cols] = grad.astype(jnp.bfloat16)


def rows_out(table, start, hidden, pair, weights, added):
    columns = weights[0].shape[-1]
    rows = hidden[0].shape[0] // 2
    return pl.pallas_call(
        functools.partial(rows_kernel, start),
        out_shape=[shape_of(rows, 2 * columns if added else columns)] * 2,
        in_specs=[SMEM] + [VMEM] * (9 + len(added)),
        out_specs=[VMEM] * 2,
        compiler_params=pltpu.CompilerParams(vmem_limit_bytes=24 * 1024 * 1024),
        name="rows_out",
    )(table, *hidden, *pair, *weights, *added)


def merge_kernel(table_ref, kept, came, back, across, own, one, rest, total):
    spot = spots(table_ref[8])
    total[...] = jnp.zeros_like(total)
    for index, block in enumerate((kept, came.at[0], back, across)):
        for k in range(2):
            e = table_ref[2 * index + k]
            for p in range(4):
                total[p, :, e] += block[k, :, p].astype(jnp.float32)
    own[...] = total[0].astype(jnp.bfloat16)
    one[...] = total[spot[1]].astype(jnp.bfloat16)
    rest[0] = total[spot[2]].astype(jnp.bfloat16)
    rest[1] = total[3].astype(jnp.bfloat16)


def merge(table, came, experts):
    columns = came[0].shape[-1]
    return pl.pallas_call(
        merge_kernel,
        out_shape=[shape_of(*lead, 3, experts, 8, columns) for lead in ((), (), (2,))],
        in_specs=[SMEM] + [VMEM] * 4,
        out_specs=[VMEM] * 3,
        scratch_shapes=[pltpu.VMEM((4, 3, experts, 8, columns), jnp.float32)],
        compiler_params=LIMIT,
        name="merge",
    )(table, *[c.reshape(*c.shape[:-2], 4, 8, columns) for c in came])


def shards(tokens, cotangent, row_slot, placement, master, first_moment, second_moment):
    group = lax.axis_index("group")
    core = lax.axis_index("local")
    experts = master.shape[0]
    columns = master.shape[3]
    rows = tokens.shape[0]

    steps = np.array(
        [[[step[c] << SHIFTS[axes[2]] for step in STEPS] for axes in AXES] for c in range(2)], np.int32
    ).reshape(2, -1)
    there = group ^ jnp.where(core == 0, jnp.asarray(steps[0]), jnp.asarray(steps[1]))
    seen = there[:, None] == jnp.arange(SIDE**3)[None]
    pairs = jnp.sum(jnp.where(seen[:, :, None], placement[None], 0), 1)
    pairs = pairs.reshape(CHAINS, 2 * SIDE)
    table = jnp.concatenate([pairs, jnp.full((CHAINS, 1), core)], 1)

    narrow = master.astype(jnp.bfloat16).transpose(1, 2, 0, 3)
    near = [axes[0] for axes in AXES]
    mid = [axes[1] for axes in AXES]
    last = [axes[2] for axes in AXES]
    each = range(CHAINS)
    blocks = [narrow[:, 2 * c : 2 * c + 2] for c in each]
    (ones,) = together([hop(blocks[c], near[c], ONE) for c in each])
    rests = [hop(jnp.stack([blocks[c], ones[c]], 0), near[c], BACK) for c in each]
    far = (1 - core) * columns
    got_rows = [swap(lax.dynamic_slice_in_dim(v, far, columns, 1)) for v in (tokens, cotangent)]
    rows_in = [tokens, got_rows[0], cotangent, got_rows[1]]
    slots = jnp.concatenate([row_slot, swap(row_slot)], 0)
    chosen = jnp.broadcast_to((slots == 0)[:, None], (2 * rows, 128)).astype(jnp.float32)
    rests, rows_in, chosen = together(rests, rows_in, chosen)
    (lines,) = together([weave(table[c], blocks[c], ones[c], rests[c]) for c in each])
    backs = [hop(lines[c], mid[c], BACK) for c in each]
    (ones,) = together([hop(lines[c], mid[c], ONE) for c in each])
    acrosses = [hop(ones[c], mid[c], BACK) for c in each]
    backs, acrosses = together(backs, acrosses)
    packed = [pick(table[c], [lines[c], ones[c], backs[c], acrosses[c]]) for c in each]
    (packed,) = together(packed)

    def exchange(ahead, back, axis):
        came = hop(ahead, axis, ONE)
        return came, hop(back, axis, BACK), hop(came[1], axis, BACK)

    (came,) = together([hop(packed[c][1], last[c], ONE) for c in each])
    acrosses = [hop(came[c][1], last[c], BACK) for c in each]
    backs = [hop(packed[c][2], last[c], BACK) for c in each]
    backs, acrosses = together(backs, acrosses)

    sums = []
    weights = []
    for c in each:
        blocks = [packed[c][0], came[c], backs[c], acrosses[c]]
        blocks = [a.reshape(*a.shape[:-3], 32, columns) for a in blocks]
        one_sums, one_weights = first(table[c], rows_in, chosen, blocks)
        sums.append(one_sums)
        weights.append(one_weights)
    got = [swap(v) for v in sums]
    sent = []
    hidden = []
    pair = []
    for c in each:
        own, ahead, back, one_hidden, one_pair = second(
            table[c], rows_in, chosen, sums[c], got[c], columns
        )
        sent.append((own, *exchange(ahead, back, last[c])))
        hidden.append(one_hidden)
        pair.append(one_pair)
    merged = [merge(table[c], sent[c], experts) for c in each]

    def add(one, came):
        return (one.astype(jnp.float32) + came[1].astype(jnp.float32)).astype(jnp.bfloat16)

    def scatter(parts, axes):
        (came,) = together([hop(parts[c][2], axes[c], BACK) for c in each])
        (ones,) = together([add(parts[c][1], came[c]) for c in each])
        return [(parts[c][0], came[c], hop(ones[c], axes[c], ONE)) for c in each]

    merged = scatter(merged, mid)
    sums = [unweave(table[c], *merged[c]) for c in each]

    far_rows = rows_out(table[0], rows, hidden, pair, weights, [])
    layer_out, input_grad = rows_out(
        table[0], 0, hidden, pair, weights, [swap(r) for r in far_rows]
    )
    sums, layer_out, input_grad = together(sums, layer_out, input_grad)
    parts = [
        own + came[0].astype(jnp.float32) + one.astype(jnp.float32)
        for own, came, one in scatter(sums, near)
    ]

    grads = jnp.concatenate(parts, 1).transpose(2, 0, 1, 3)
    scaled = grads / loss_scale
    new_first = beta_first * first_moment + (1.0 - beta_first) * scaled
    new_second = beta_second * second_moment + (1.0 - beta_second) * scaled * scaled
    new_master = master - learn_rate * (new_first / bias_first) / (
        jnp.sqrt(new_second / bias_second) + adam_epsilon
    )

    return layer_out, input_grad, new_master, new_first, new_second


def solution(mesh):
    state = P(None, None, "group", "local")
    rows = P(("group", "local"), None)
    return jax.shard_map(
        shards,
        mesh=mesh,
        in_specs=(rows, rows, P(("group", "local")), P(), state, state, state),
        out_specs=(rows, rows, state, state, state),
        check_vma=False,
    )
```

```python
import functools
import jax
import jax.numpy as jnp
import numpy as np
from jax import lax
from jax.experimental import pallas as pl
from jax.experimental.pallas import tpu as pltpu
from jax.sharding import PartitionSpec as P

loss_scale = 4.0
beta_first = 0.9
beta_second = 0.95
learn_rate = 0.001
adam_epsilon = 1e-08
bias_first = 1.0 - 0.9**10
bias_second = 1.0 - 0.95**10

SIDE = 4
CHAINS = 3
BOTH = ("group", "local")
SHIFTS = (4, 2, 0)
AXES = ((2, 1, 0), (1, 0, 2), (0, 2, 1))


def place(coords, core):
    return ((coords[0] * SIDE + coords[1]) * SIDE + coords[2]) * 2 + core


def step_pairs(axis, offsets):
    pairs = []
    for group in range(SIDE**3):
        for core in range(2):
            coords = [group // 16, group // 4 % 4, group % 4]
            here = place(coords, core)
            coords[axis] ^= offsets[core]
            pairs.append((here, place(coords, core)))
    return pairs


CORE_PAIRS = [(i, i ^ 1) for i in range(2 * SIDE**3)]
ONE, BACK, ACROSS = (1, 3), (3, 1), (2, 2)
STEPS = ((0, 0), ONE, BACK, ACROSS)


def hop(value, axis, offsets):
    return lax.ppermute(value, BOTH, step_pairs(axis, offsets))


def swap(value):
    return lax.ppermute(value, BOTH, CORE_PAIRS)


def contract_last(left, right):
    return lax.dot_general(
        left, right, (((1,), (1,)), ((), ())), preferred_element_type=jnp.float32
    )


def contract_first(left, right):
    return lax.dot_general(
        left, right, (((0,), (0,)), ((), ())), preferred_element_type=jnp.float32
    )


def matmul(left, right):
    return jnp.dot(left, right, preferred_element_type=jnp.float32)


VMEM = pl.BlockSpec(memory_space=pltpu.VMEM)
SMEM = pl.BlockSpec(memory_space=pltpu.SMEM)
LIMIT = pltpu.CompilerParams(vmem_limit_bytes=16 * 1024 * 1024)


def shape_of(*dims):
    return jax.ShapeDtypeStruct(dims, jnp.bfloat16)


def spots(core):
    return (0, 1 + core, 2 - core, 3)


def weave_kernel(table_ref, own, one, rest, out, turned):
    first = table_ref[8] == 0
    for m in range(3):
        for r in range(2):
            near = one[m, r].astype(jnp.float32)
            back = rest[0, m, r].astype(jnp.float32)
            turned[m, :, r] = own[m, r].astype(jnp.float32)
            turned[m, :, 2 + r] = jnp.where(first, near, back)
            turned[m, :, 4 + r] = jnp.where(first, back, near)
            turned[m, :, 6 + r] = rest[1, m, r].astype(jnp.float32)
    out[...] = turned[...].astype(jnp.bfloat16)


def weave(table, own, one, rest):
    _, _, experts, columns = own.shape
    return pl.pallas_call(
        weave_kernel,
        out_shape=shape_of(3, experts, 8, columns),
        in_specs=[SMEM] + [VMEM] * 3,
        out_specs=VMEM,
        scratch_shapes=[pltpu.VMEM((3, experts, 8, columns), jnp.float32)],
        compiler_params=LIMIT,
        name="weave",
    )(table, own, one, rest)


def unweave_kernel(table_ref, own, came, last, out, one, rest, turned):
    first = table_ref[8] == 0
    turned[...] = (
        own[...].astype(jnp.float32) + came[0].astype(jnp.float32) + last[...].astype(jnp.float32)
    )
    for m in range(3):
        for r in range(2):
            left = turned[m, :, 2 + r]
            right = turned[m, :, 4 + r]
            out[m, r] = turned[m, :, r]
            one[m, r] = jnp.where(first, left, right).astype(jnp.bfloat16)
            rest[0, m, r] = jnp.where(first, right, left).astype(jnp.bfloat16)
            rest[1, m, r] = turned[m, :, 6 + r].astype(jnp.bfloat16)


def unweave(table, own, came, last):
    _, experts, _, columns = own.shape
    return pl.pallas_call(
        unweave_kernel,
        out_shape=[
            jax.ShapeDtypeStruct((3, 2, experts, columns), jnp.float32),
            shape_of(3, 2, experts, columns),
            shape_of(2, 3, 2, experts, columns),
        ],
        in_specs=[SMEM] + [VMEM] * 3,
        out_specs=[VMEM] * 3,
        scratch_shapes=[pltpu.VMEM((3, experts, 8, columns), jnp.float32)],
        compiler_params=LIMIT,
        name="unweave",
    )(table, own, came, last)


def pick_kernel(table_ref, kept, one, rest, own, ahead, back):
    spot = spots(table_ref[8])
    for index, out in enumerate((own, ahead.at[0], back, ahead.at[1])):
        for k in range(2):
            e = table_ref[2 * index + k]
            for b, p in enumerate((kept, one, rest.at[0], rest.at[1])):
                out[k, :, spot[b]] = p[:, e]


def pick(table, *plane):
    columns = plane[0].shape[-1]
    return pl.pallas_call(
        pick_kernel,
        out_shape=[shape_of(*lead, 2, 3, 4, 8, columns) for lead in ((), (2,), ())],
        in_specs=[SMEM] + [VMEM] * 3,
        out_specs=[VMEM] * 3,
        compiler_params=LIMIT,
        name="pick",
    )(table, *plane)


def first_kernel(table_ref, tok0, tok1, cot0, cot1, mask, own, came, back, across, sums, weights):
    core = table_ref[8]
    columns = own.shape[-1]
    rows = tok0.shape[0]
    for spot, a in zip(spots(core), (own, came.at[0], back, across)):
        weights[:, :, spot] = a[...]
    half = pl.ds(pl.multiple_of(core * columns, columns), columns)
    w_pair = jnp.concatenate([weights[k, 0:2].reshape(256, columns) for k in range(2)], 0)
    w_down = jnp.concatenate([weights[k, 2].reshape(128, columns) for k in range(2)], 0)
    parts = ((tok0[:, half], cot0[:, half]), (tok1[...], cot1[...]))
    for b, (tok, cot) in enumerate(parts):
        here = slice(rows * b, rows * b + rows)
        chosen = mask[here] > 0.0
        pre = contract_last(tok, w_pair)
        d_hidden = contract_last(cot, w_down)
        sums[0, here] = jnp.where(chosen, pre[:, :128], pre[:, 256:384])
        sums[1, here] = jnp.where(chosen, pre[:, 128:256], pre[:, 384:])
        sums[2, here] = jnp.where(chosen, d_hidden[:, :128], d_hidden[:, 128:])


def first(table, rows_in, mask, arrived):
    columns = arrived[0].shape[-1]
    rows = mask.shape[0]
    return pl.pallas_call(
        first_kernel,
        out_shape=[
            jax.ShapeDtypeStruct((3, rows, 128), jnp.float32),
            shape_of(2, 3, 4, 32, columns),
        ],
        in_specs=[SMEM] + [VMEM] * 9,
        out_specs=[VMEM] * 2,
        compiler_params=pltpu.CompilerParams(vmem_limit_bytes=24 * 1024 * 1024),
        name="first",
    )(table, *rows_in, mask, *arrived)


def second_kernel(
    table_ref, tok0, tok1, cot0, cot1, mask, sums, got, own, ahead, back, hidden, pair, turned
):
    core = table_ref[8]
    columns = own.shape[-1]
    rows = tok0.shape[0]
    step = 256
    for r in range(0, 2 * rows, step):
        here = slice(r, r + step)
        there = slice((r + rows) % (2 * rows), (r + rows) % (2 * rows) + step)
        gate_pre = sums[0, here] + got[0, there]
        up_pre = sums[1, here] + got[1, there]
        d_hidden = sums[2, here] + got[2, there]
        sigmoid_gate = jax.nn.sigmoid(gate_pre)
        act = gate_pre * sigmoid_gate
        d_gate = d_hidden * up_pre * sigmoid_gate * (1.0 + gate_pre * (1.0 - sigmoid_gate))
        three = (d_gate, d_hidden * act, act * up_pre)
        chosen = mask[here] > 0.0
        for k in range(2):
            for m in range(3):
                part = jnp.where(chosen, three[m], 0.0) if k == 0 else jnp.where(chosen, 0.0, three[m])
                part = part.astype(jnp.bfloat16)
                if m < 2:
                    pair[here, 256 * k + 128 * m : 256 * k + 128 * m + 128] = part
                else:
                    hidden[here, 128 * k : 128 * k + 128] = part
                line = 256 * k + 128 * m if m < 2 else 512 + 128 * k
                turned[line : line + 128, here] = part.T
    start = pl.multiple_of(core * columns, columns)
    swapped = core == 1
    for c in range(0, columns, step):
        cols = pl.ds(start + c, step)
        out_cols = slice(c, c + step)
        both = matmul(turned[:512, :rows], tok0[:, cols]) + matmul(
            turned[:512, rows:], tok1[:, out_cols]
        )
        down = matmul(turned[512:, :rows], cot0[:, cols]) + matmul(
            turned[512:, rows:], cot1[:, out_cols]
        )
        for k in range(2):
            for m in range(3):
                line = both[256 * k + 128 * m :][:128] if m < 2 else down[128 * k :][:128]
                line = line.astype(jnp.bfloat16)
                q = [line[32 * i : 32 * i + 32] for i in range(4)]
                own[k, m, :, out_cols] = q[0]
                ahead[0, k, m, :, out_cols] = jnp.where(swapped, q[2], q[1])
                back[k, m, :, out_cols] = jnp.where(swapped, q[1], q[2])
                ahead[1, k, m, :, out_cols] = q[3]


def second(table, rows_in, mask, sums, got, columns):
    rows = mask.shape[0]
    return pl.pallas_call(
        second_kernel,
        out_shape=[shape_of(*lead, 2, 3, 32, columns) for lead in ((), (2,), ())]
        + [shape_of(rows, 256), shape_of(rows, 512)],
        in_specs=[SMEM] + [VMEM] * 7,
        out_specs=[VMEM] * 5,
        scratch_shapes=[pltpu.VMEM((768, rows), jnp.bfloat16)],
        compiler_params=pltpu.CompilerParams(vmem_limit_bytes=24 * 1024 * 1024),
        name="second",
    )(table, *rows_in, mask, sums, got)


def rows_kernel(start, table_ref, *refs):
    hidden, pair, weights = refs[0:3], refs[3:6], refs[6:9]
    added, (layer_out, grad_out) = refs[9:-2], refs[-2:]
    columns = weights[0].shape[-1]
    rows = slice(start, start + layer_out.shape[0])
    step = 512
    if added:
        core = table_ref[8]
        near = pl.multiple_of(core * columns, columns)
        far = pl.ds(pl.multiple_of((1 - core) * columns, columns), columns)
        layer_out[:, far] = added[0][...]
        grad_out[:, far] = added[1][...]
    for c in range(0, columns, step):
        part = slice(c, c + step)
        cols = pl.ds(near + c, step) if added else part
        layer = 0.0
        grad = 0.0
        for chain in range(CHAINS):
            w = weights[chain]
            down = jnp.concatenate([w[k, 2, :, :, part].reshape(128, step) for k in range(2)], 0)
            layer = layer + matmul(hidden[chain][rows], down)
            for k in range(2):
                both = w[k, 0:2, :, :, part].reshape(256, step)
                grad = grad + matmul(pair[chain][rows, 256 * k : 256 * k + 256], both)
        layer_out[:, cols] = layer.astype(jnp.bfloat16)
        grad_out[:, cols] = grad.astype(jnp.bfloat16)


def rows_out(table, hidden, pair, weights, added, start):
    columns = weights[0].shape[-1]
    rows = hidden[0].shape[0] // 2
    return pl.pallas_call(
        functools.partial(rows_kernel, start),
        out_shape=[shape_of(rows, 2 * columns if added else columns)] * 2,
        in_specs=[SMEM] + [VMEM] * (9 + len(added)),
        out_specs=[VMEM] * 2,
        compiler_params=pltpu.CompilerParams(vmem_limit_bytes=24 * 1024 * 1024),
        name="rows_out",
    )(table, *hidden, *pair, *weights, *added)


def merge_kernel(table_ref, kept, came, back, across, own, one, rest, total):
    spot = spots(table_ref[8])
    total[...] = jnp.zeros_like(total)
    for index, block in enumerate((kept, came.at[0], back, across)):
        for k in range(2):
            e = table_ref[2 * index + k]
            for p in range(4):
                total[p, :, e] += block[k, :, p].astype(jnp.float32)
    own[...] = total[0].astype(jnp.bfloat16)
    one[...] = total[spot[1]].astype(jnp.bfloat16)
    rest[0] = total[spot[2]].astype(jnp.bfloat16)
    rest[1] = total[3].astype(jnp.bfloat16)


def merge(table, came, experts):
    columns = came[0].shape[-1]
    return pl.pallas_call(
        merge_kernel,
        out_shape=[shape_of(*lead, 3, experts, 8, columns) for lead in ((), (), (2,))],
        in_specs=[SMEM] + [VMEM] * 4,
        out_specs=[VMEM] * 3,
        scratch_shapes=[pltpu.VMEM((4, 3, experts, 8, columns), jnp.float32)],
        compiler_params=LIMIT,
        name="merge",
    )(table, *[c.reshape(*c.shape[:-2], 4, 8, columns) for c in came])


def shards(tokens, cotangent, row_slot, placement, master, first_moment, second_moment):
    group = lax.axis_index("group")
    core = lax.axis_index("local")
    experts = master.shape[0]
    columns = master.shape[3]
    rows = tokens.shape[0]

    steps = np.array(
        [[[step[c] << SHIFTS[axes[2]] for step in STEPS] for axes in AXES] for c in range(2)], np.int32
    ).reshape(2, -1)
    there = group ^ jnp.where(core == 0, jnp.asarray(steps[0]), jnp.asarray(steps[1]))
    seen = there[:, None] == jnp.arange(SIDE**3)[None]
    pairs = jnp.sum(jnp.where(seen[:, :, None], placement[None], 0), 1)
    pairs = pairs.reshape(CHAINS, 2 * SIDE)
    table = jnp.concatenate([pairs, jnp.full((CHAINS, 1), core)], 1)

    narrow = master.astype(jnp.bfloat16).transpose(1, 2, 0, 3)
    near = [axes[0] for axes in AXES]
    mid = [axes[1] for axes in AXES]
    last = [axes[2] for axes in AXES]
    each = range(CHAINS)
    blocks = [narrow[:, 2 * c : 2 * c + 2] for c in each]
    ones = [hop(blocks[c], near[c], ONE) for c in each]
    both = [jnp.stack([blocks[c], ones[c]], 0) for c in each]
    rests = [hop(both[c], near[c], BACK) for c in each]
    lines = [weave(table[c], blocks[c], ones[c], rests[c]) for c in each]

    def other_rows(*rows):
        far = (1 - core) * columns
        return [lax.dynamic_slice_in_dim(v, far, columns, 1) for v in rows]

    lines, tokens, cotangent, row_slot = lax.optimization_barrier(
        (lines, tokens, cotangent, row_slot)
    )
    far_tokens, far_cotangent = other_rows(tokens, cotangent)
    rows_in = [tokens, swap(far_tokens), cotangent, swap(far_cotangent)]
    slots = jnp.concatenate([row_slot, swap(row_slot)], 0)
    chosen = jnp.broadcast_to((slots == 0)[:, None], (2 * rows, 128)).astype(jnp.float32)

    ones = [hop(lines[c], mid[c], ONE) for c in each]
    both = [jnp.stack([lines[c], ones[c]], 0) for c in each]
    rests = [hop(both[c], mid[c], BACK) for c in each]
    rests, rows_in, chosen = lax.optimization_barrier((rests, rows_in, chosen))
    packed = [pick(table[c], lines[c], ones[c], rests[c]) for c in each]

    def exchange(packed):
        came = [hop(packed[c][1], last[c], ONE) for c in each]
        backs = [hop(packed[c][2], last[c], BACK) for c in each]
        passed = [came[c][1] for c in each]
        acrosses = [hop(passed[c], last[c], BACK) for c in each]
        return [(packed[c][0], came[c], backs[c], acrosses[c]) for c in each]

    arrived = exchange(packed)
    blocks = [[a.reshape(*a.shape[:-3], 32, columns) for a in arrived[c]] for c in each]
    firsts = [first(table[c], rows_in, chosen, blocks[c]) for c in each]
    got = [swap(f[0]) for f in firsts]
    seconds = [
        second(table[c], rows_in, chosen, firsts[c][0], got[c], columns)
        for c in each
    ]
    weights = [f[1] for f in firsts]
    hidden = [v[3] for v in seconds]
    pair = [v[4] for v in seconds]
    sent = exchange(seconds)
    merged = [merge(table[c], sent[c], experts) for c in each]

    def add(one, came):
        return (one.astype(jnp.float32) + came[1].astype(jnp.float32)).astype(jnp.bfloat16)

    def scatter(parts, axes):
        came = [hop(parts[c][2], axes[c], BACK) for c in each]
        ones = [add(parts[c][1], came[c]) for c in each]
        return [(parts[c][0], came[c], hop(ones[c], axes[c], ONE)) for c in each]

    far_rows = rows_out(table[0], hidden, pair, weights, [], rows)
    layer_out, input_grad = rows_out(
        table[0], hidden, pair, weights, [swap(r) for r in far_rows], 0
    )
    merged = scatter(merged, mid)
    sums = [unweave(table[c], *merged[c]) for c in each]
    parts = [
        own + came[0].astype(jnp.float32) + one.astype(jnp.float32)
        for own, came, one in scatter(sums, near)
    ]

    grads = jnp.concatenate(parts, 1).transpose(2, 0, 1, 3)
    scaled = grads / loss_scale
    new_first = beta_first * first_moment + (1.0 - beta_first) * scaled
    new_second = beta_second * second_moment + (1.0 - beta_second) * scaled * scaled
    new_master = master - learn_rate * (new_first / bias_first) / (
        jnp.sqrt(new_second / bias_second) + adam_epsilon
    )

    return layer_out, input_grad, new_master, new_first, new_second


def solution(mesh):
    state = P(None, None, "group", "local")
    rows = P(("group", "local"), None)
    return jax.shard_map(
        shards,
        mesh=mesh,
        in_specs=(rows, rows, P(("group", "local")), P(), state, state, state),
        out_specs=(rows, rows, state, state, state),
        check_vma=False,
    )
```

```python
import functools
import jax
import jax.numpy as jnp
import numpy as np
from jax import lax
from jax.experimental import pallas as pl
from jax.experimental.pallas import tpu as pltpu
from jax.sharding import PartitionSpec as P

loss_scale = 4.0
beta_first = 0.9
beta_second = 0.95
learn_rate = 0.001
adam_epsilon = 1e-08
bias_first = 1.0 - 0.9**10
bias_second = 1.0 - 0.95**10

SIDE = 4
CHAINS = 3
BOTH = ("group", "local")
SHIFTS = (4, 2, 0)
AXES = ((2, 1, 0), (1, 0, 2), (0, 2, 1))


def place(coords, core):
    return ((coords[0] * SIDE + coords[1]) * SIDE + coords[2]) * 2 + core


def step_pairs(axis, offsets):
    pairs = []
    for group in range(SIDE**3):
        for core in range(2):
            coords = [group // 16, group // 4 % 4, group % 4]
            here = place(coords, core)
            coords[axis] ^= offsets[core]
            pairs.append((here, place(coords, core)))
    return pairs


CORE_PAIRS = [(i, i ^ 1) for i in range(2 * SIDE**3)]
ONE, BACK, ACROSS = (1, 3), (3, 1), (2, 2)
STEPS = ((0, 0), ONE, BACK, ACROSS)


def hop(value, axis, offsets):
    return lax.ppermute(value, BOTH, step_pairs(axis, offsets))


def swap(value):
    return lax.ppermute(value, BOTH, CORE_PAIRS)


def contract_last(left, right):
    return lax.dot_general(
        left, right, (((1,), (1,)), ((), ())), preferred_element_type=jnp.float32
    )


def contract_first(left, right):
    return lax.dot_general(
        left, right, (((0,), (0,)), ((), ())), preferred_element_type=jnp.float32
    )


def matmul(left, right):
    return jnp.dot(left, right, preferred_element_type=jnp.float32)


VMEM = pl.BlockSpec(memory_space=pltpu.VMEM)
SMEM = pl.BlockSpec(memory_space=pltpu.SMEM)
LIMIT = pltpu.CompilerParams(vmem_limit_bytes=16 * 1024 * 1024)


def shape_of(*dims):
    return jax.ShapeDtypeStruct(dims, jnp.bfloat16)


def spots(core):
    return (0, 1 + core, 2 - core, 3)


def weave_kernel(table_ref, own, one, rest, out, turned):
    first = table_ref[8] == 0
    for m in range(3):
        for r in range(2):
            near = one[m, r].astype(jnp.float32)
            back = rest[0, m, r].astype(jnp.float32)
            turned[m, :, r] = own[m, r].astype(jnp.float32)
            turned[m, :, 2 + r] = jnp.where(first, near, back)
            turned[m, :, 4 + r] = jnp.where(first, back, near)
            turned[m, :, 6 + r] = rest[1, m, r].astype(jnp.float32)
    out[...] = turned[...].astype(jnp.bfloat16)


def weave(table, own, one, rest):
    _, _, experts, columns = own.shape
    return pl.pallas_call(
        weave_kernel,
        out_shape=shape_of(3, experts, 8, columns),
        in_specs=[SMEM] + [VMEM] * 3,
        out_specs=VMEM,
        scratch_shapes=[pltpu.VMEM((3, experts, 8, columns), jnp.float32)],
        compiler_params=LIMIT,
        name="weave",
    )(table, own, one, rest)


def unweave_kernel(table_ref, own, came, last, out, one, rest):
    first = table_ref[8] == 0
    for m in range(3):
        total = own[m].astype(jnp.float32) + came[0, m].astype(jnp.float32)
        turned = jnp.swapaxes(total + last[m].astype(jnp.float32), 0, 1)
        left = turned[2:4]
        right = turned[4:6]
        out[m] = turned[0:2]
        one[m] = jnp.where(first, left, right).astype(jnp.bfloat16)
        rest[0, m] = jnp.where(first, right, left).astype(jnp.bfloat16)
        rest[1, m] = turned[6:8].astype(jnp.bfloat16)


def unweave(table, own, came, last):
    _, experts, _, columns = own.shape
    return pl.pallas_call(
        unweave_kernel,
        out_shape=[
            jax.ShapeDtypeStruct((3, 2, experts, columns), jnp.float32),
            shape_of(3, 2, experts, columns),
            shape_of(2, 3, 2, experts, columns),
        ],
        in_specs=[SMEM] + [VMEM] * 3,
        out_specs=[VMEM] * 3,
        compiler_params=LIMIT,
        name="unweave",
    )(table, own, came, last)


def pick_kernel(table_ref, kept, one, rest, own, ahead, back):
    spot = spots(table_ref[8])
    for index, out in enumerate((own, ahead.at[0], back, ahead.at[1])):
        for k in range(2):
            e = table_ref[2 * index + k]
            for b, p in enumerate((kept, one, rest.at[0], rest.at[1])):
                out[k, :, spot[b]] = p[:, e]


def pick(table, *plane):
    columns = plane[0].shape[-1]
    return pl.pallas_call(
        pick_kernel,
        out_shape=[shape_of(*lead, 2, 3, 4, 8, columns) for lead in ((), (2,), ())],
        in_specs=[SMEM] + [VMEM] * 3,
        out_specs=[VMEM] * 3,
        compiler_params=LIMIT,
        name="pick",
    )(table, *plane)


def first_kernel(table_ref, tok0, tok1, cot0, cot1, mask, own, came, rest, sums, weights):
    core = table_ref[8]
    columns = own.shape[-1]
    rows = tok0.shape[0]
    for spot, a in zip(spots(core), (own, came.at[0], rest.at[0], rest.at[1])):
        weights[:, :, spot] = a[...]
    half = pl.ds(pl.multiple_of(core * columns, columns), columns)
    w_pair = jnp.concatenate([weights[k, 0:2].reshape(256, columns) for k in range(2)], 0)
    w_down = jnp.concatenate([weights[k, 2].reshape(128, columns) for k in range(2)], 0)
    parts = ((tok0[:, half], cot0[:, half]), (tok1[...], cot1[...]))
    for b, (tok, cot) in enumerate(parts):
        here = slice(rows * b, rows * b + rows)
        chosen = mask[here] > 0.0
        pre = contract_last(tok, w_pair)
        d_hidden = contract_last(cot, w_down)
        sums[0, here] = jnp.where(chosen, pre[:, :128], pre[:, 256:384])
        sums[1, here] = jnp.where(chosen, pre[:, 128:256], pre[:, 384:])
        sums[2, here] = jnp.where(chosen, d_hidden[:, :128], d_hidden[:, 128:])


def first(table, rows_in, mask, arrived):
    columns = arrived[0].shape[-1]
    rows = mask.shape[0]
    return pl.pallas_call(
        first_kernel,
        out_shape=[
            jax.ShapeDtypeStruct((3, rows, 128), jnp.float32),
            shape_of(2, 3, 4, 32, columns),
        ],
        in_specs=[SMEM] + [VMEM] * 8,
        out_specs=[VMEM] * 2,
        compiler_params=pltpu.CompilerParams(vmem_limit_bytes=24 * 1024 * 1024),
        name="first",
    )(table, *rows_in, mask, *arrived)


def second_kernel(
    table_ref, tok0, tok1, cot0, cot1, mask, sums, got, own, ahead, back, hidden, pair, turned
):
    core = table_ref[8]
    columns = own.shape[-1]
    rows = tok0.shape[0]
    step = 256
    for r in range(0, 2 * rows, step):
        here = slice(r, r + step)
        there = slice((r + rows) % (2 * rows), (r + rows) % (2 * rows) + step)
        gate_pre = sums[0, here] + got[0, there]
        up_pre = sums[1, here] + got[1, there]
        d_hidden = sums[2, here] + got[2, there]
        sigmoid_gate = jax.nn.sigmoid(gate_pre)
        act = gate_pre * sigmoid_gate
        d_gate = d_hidden * up_pre * sigmoid_gate * (1.0 + gate_pre * (1.0 - sigmoid_gate))
        three = (d_gate, d_hidden * act, act * up_pre)
        chosen = mask[here] > 0.0
        for k in range(2):
            for m in range(3):
                part = jnp.where(chosen, three[m], 0.0) if k == 0 else jnp.where(chosen, 0.0, three[m])
                part = part.astype(jnp.bfloat16)
                if m < 2:
                    pair[here, 256 * k + 128 * m : 256 * k + 128 * m + 128] = part
                else:
                    hidden[here, 128 * k : 128 * k + 128] = part
                line = 256 * k + 128 * m if m < 2 else 512 + 128 * k
                turned[line : line + 128, here] = part.T
    start = pl.multiple_of(core * columns, columns)
    swapped = core == 1
    for c in range(0, columns, step):
        cols = pl.ds(start + c, step)
        out_cols = slice(c, c + step)
        both = matmul(turned[:512, :rows], tok0[:, cols]) + matmul(
            turned[:512, rows:], tok1[:, out_cols]
        )
        down = matmul(turned[512:, :rows], cot0[:, cols]) + matmul(
            turned[512:, rows:], cot1[:, out_cols]
        )
        for k in range(2):
            for m in range(3):
                line = both[256 * k + 128 * m :][:128] if m < 2 else down[128 * k :][:128]
                line = line.astype(jnp.bfloat16)
                q = [line[32 * i : 32 * i + 32] for i in range(4)]
                own[k, m, :, out_cols] = q[0]
                ahead[0, k, m, :, out_cols] = jnp.where(swapped, q[2], q[1])
                back[k, m, :, out_cols] = jnp.where(swapped, q[1], q[2])
                ahead[1, k, m, :, out_cols] = q[3]


def second(table, rows_in, mask, sums, got, columns):
    rows = mask.shape[0]
    return pl.pallas_call(
        second_kernel,
        out_shape=[shape_of(*lead, 2, 3, 32, columns) for lead in ((), (2,), ())]
        + [shape_of(rows, 256), shape_of(rows, 512)],
        in_specs=[SMEM] + [VMEM] * 7,
        out_specs=[VMEM] * 5,
        scratch_shapes=[pltpu.VMEM((768, rows), jnp.bfloat16)],
        compiler_params=pltpu.CompilerParams(vmem_limit_bytes=24 * 1024 * 1024),
        name="second",
    )(table, *rows_in, mask, sums, got)


def rows_kernel(start, table_ref, *refs):
    hidden, pair, weights = refs[0:3], refs[3:6], refs[6:9]
    added, (layer_out, grad_out) = refs[9:-2], refs[-2:]
    columns = weights[0].shape[-1]
    rows = slice(start, start + layer_out.shape[0])
    step = 512
    if added:
        core = table_ref[8]
        near = pl.multiple_of(core * columns, columns)
        far = pl.ds(pl.multiple_of((1 - core) * columns, columns), columns)
        layer_out[:, far] = added[0][...]
        grad_out[:, far] = added[1][...]
    for c in range(0, columns, step):
        part = slice(c, c + step)
        cols = pl.ds(near + c, step) if added else part
        layer = 0.0
        grad = 0.0
        for chain in range(CHAINS):
            w = weights[chain]
            down = jnp.concatenate([w[k, 2, :, :, part].reshape(128, step) for k in range(2)], 0)
            layer = layer + matmul(hidden[chain][rows], down)
            for k in range(2):
                both = w[k, 0:2, :, :, part].reshape(256, step)
                grad = grad + matmul(pair[chain][rows, 256 * k : 256 * k + 256], both)
        layer_out[:, cols] = layer.astype(jnp.bfloat16)
        grad_out[:, cols] = grad.astype(jnp.bfloat16)


def rows_out(table, hidden, pair, weights, added, start):
    columns = weights[0].shape[-1]
    rows = hidden[0].shape[0] // 2
    return pl.pallas_call(
        functools.partial(rows_kernel, start),
        out_shape=[shape_of(rows, 2 * columns if added else columns)] * 2,
        in_specs=[SMEM] + [VMEM] * (9 + len(added)),
        out_specs=[VMEM] * 2,
        compiler_params=pltpu.CompilerParams(vmem_limit_bytes=24 * 1024 * 1024),
        name="rows_out",
    )(table, *hidden, *pair, *weights, *added)


def merge_kernel(table_ref, kept, came, passed, own, one, rest, total):
    spot = spots(table_ref[8])
    total[...] = jnp.zeros_like(total)
    for index, block in enumerate((kept, came.at[0], passed.at[0], passed.at[1])):
        for k in range(2):
            e = table_ref[2 * index + k]
            for p in range(4):
                total[p, :, e] += block[k, :, p].astype(jnp.float32)
    own[...] = total[0].astype(jnp.bfloat16)
    one[...] = total[spot[1]].astype(jnp.bfloat16)
    rest[0] = total[spot[2]].astype(jnp.bfloat16)
    rest[1] = total[3].astype(jnp.bfloat16)


def merge(table, came, experts):
    columns = came[0].shape[-1]
    return pl.pallas_call(
        merge_kernel,
        out_shape=[shape_of(*lead, 3, experts, 8, columns) for lead in ((), (), (2,))],
        in_specs=[SMEM] + [VMEM] * 3,
        out_specs=[VMEM] * 3,
        scratch_shapes=[pltpu.VMEM((4, 3, experts, 8, columns), jnp.float32)],
        compiler_params=LIMIT,
        name="merge",
    )(table, *[c.reshape(*c.shape[:-2], 4, 8, columns) for c in came])


def shards(tokens, cotangent, row_slot, placement, master, first_moment, second_moment):
    group = lax.axis_index("group")
    core = lax.axis_index("local")
    experts = master.shape[0]
    columns = master.shape[3]
    rows = tokens.shape[0]

    steps = np.array(
        [[[step[c] << SHIFTS[axes[2]] for step in STEPS] for axes in AXES] for c in range(2)], np.int32
    ).reshape(2, -1)
    there = group ^ jnp.where(core == 0, jnp.asarray(steps[0]), jnp.asarray(steps[1]))
    seen = there[:, None] == jnp.arange(SIDE**3)[None]
    pairs = jnp.sum(jnp.where(seen[:, :, None], placement[None], 0), 1)
    pairs = pairs.reshape(CHAINS, 2 * SIDE)
    table = jnp.concatenate([pairs, jnp.full((CHAINS, 1), core)], 1)

    narrow = master.astype(jnp.bfloat16).transpose(1, 2, 0, 3)
    near = [axes[0] for axes in AXES]
    mid = [axes[1] for axes in AXES]
    last = [axes[2] for axes in AXES]
    each = range(CHAINS)
    blocks = [narrow[:, 2 * c : 2 * c + 2] for c in each]
    ones = [hop(blocks[c], near[c], ONE) for c in each]
    both = [jnp.stack([blocks[c], ones[c]], 0) for c in each]
    rests = [hop(both[c], near[c], BACK) for c in each]
    lines = [weave(table[c], blocks[c], ones[c], rests[c]) for c in each]

    def other_rows(*rows):
        far = (1 - core) * columns
        return [lax.dynamic_slice_in_dim(v, far, columns, 1) for v in rows]

    lines[2], tokens, cotangent, row_slot = lax.optimization_barrier(
        (lines[2], tokens, cotangent, row_slot)
    )
    far_tokens, far_cotangent = other_rows(tokens, cotangent)
    rows_in = [tokens, swap(far_tokens), cotangent, swap(far_cotangent)]
    slots = jnp.concatenate([row_slot, swap(row_slot)], 0)
    chosen = jnp.broadcast_to((slots == 0)[:, None], (2 * rows, 128)).astype(jnp.float32)

    ones = [hop(lines[c], mid[c], ONE) for c in each]
    both = [jnp.stack([lines[c], ones[c]], 0) for c in each]
    rests = [hop(both[c], mid[c], BACK) for c in each]
    rests[0], rows_in, chosen = lax.optimization_barrier((rests[0], rows_in, chosen))
    packed = [pick(table[c], lines[c], ones[c], rests[c]) for c in each]

    def exchange(packed):
        came = [hop(packed[c][1], last[c], ONE) for c in each]
        both = [jnp.stack([packed[c][2], came[c][1]], 0) for c in each]
        return [(packed[c][0], came[c], hop(both[c], last[c], BACK)) for c in each]

    arrived = exchange(packed)
    blocks = [[a.reshape(*a.shape[:-3], 32, columns) for a in arrived[c]] for c in each]
    firsts = [first(table[c], rows_in, chosen, blocks[c]) for c in each]
    got = [swap(f[0]) for f in firsts]
    seconds = [
        second(table[c], rows_in, chosen, firsts[c][0], got[c], columns)
        for c in each
    ]
    weights = [f[1] for f in firsts]
    hidden = [v[3] for v in seconds]
    pair = [v[4] for v in seconds]
    sent = exchange(seconds)
    merged = [merge(table[c], sent[c], experts) for c in each]

    def add(one, came):
        return (one.astype(jnp.float32) + came[1].astype(jnp.float32)).astype(jnp.bfloat16)

    def scatter(parts, axes):
        came = [hop(parts[c][2], axes[c], BACK) for c in each]
        ones = [add(parts[c][1], came[c]) for c in each]
        return [(parts[c][0], came[c], hop(ones[c], axes[c], ONE)) for c in each]

    far_rows = rows_out(table[0], hidden, pair, weights, [], rows)
    layer_out, input_grad = rows_out(
        table[0], hidden, pair, weights, [swap(r) for r in far_rows], 0
    )
    merged = scatter(merged, mid)
    sums = [unweave(table[c], *merged[c]) for c in each]
    parts = [
        own + came[0].astype(jnp.float32) + one.astype(jnp.float32)
        for own, came, one in scatter(sums, near)
    ]

    grads = jnp.concatenate(parts, 1).transpose(2, 0, 1, 3)
    scaled = grads / loss_scale
    new_first = beta_first * first_moment + (1.0 - beta_first) * scaled
    new_second = beta_second * second_moment + (1.0 - beta_second) * scaled * scaled
    new_master = master - learn_rate * (new_first / bias_first) / (
        jnp.sqrt(new_second / bias_second) + adam_epsilon
    )

    return layer_out, input_grad, new_master, new_first, new_second


def solution(mesh):
    state = P(None, None, "group", "local")
    rows = P(("group", "local"), None)
    return jax.shard_map(
        shards,
        mesh=mesh,
        in_specs=(rows, rows, P(("group", "local")), P(), state, state, state),
        out_specs=(rows, rows, state, state, state),
        check_vma=False,
    )
```

```python
import functools
import jax
import jax.numpy as jnp
import numpy as np
from jax import lax
from jax.experimental import pallas as pl
from jax.experimental.pallas import tpu as pltpu
from jax.sharding import PartitionSpec as P

loss_scale = 4.0
beta_first = 0.9
beta_second = 0.95
learn_rate = 0.001
adam_epsilon = 1e-08
bias_first = 1.0 - 0.9**10
bias_second = 1.0 - 0.95**10

SIDE = 4
CHAINS = 3
BOTH = ("group", "local")
SHIFTS = (4, 2, 0)
AXES = ((2, 1, 0), (0, 2, 1), (1, 0, 2))


def place(coords, core):
    return ((coords[0] * SIDE + coords[1]) * SIDE + coords[2]) * 2 + core


def step_pairs(axis, offsets):
    pairs = []
    for group in range(SIDE**3):
        for core in range(2):
            coords = [group // 16, group // 4 % 4, group % 4]
            here = place(coords, core)
            coords[axis] ^= offsets[core]
            pairs.append((here, place(coords, core)))
    return pairs


CORE_PAIRS = [(i, i ^ 1) for i in range(2 * SIDE**3)]
ONE, BACK, ACROSS = (1, 3), (3, 1), (2, 2)
STEPS = ((0, 0), ONE, BACK, ACROSS)


def hop(value, axis, offsets):
    return lax.ppermute(value, BOTH, step_pairs(axis, offsets))


def swap(value):
    return lax.ppermute(value, BOTH, CORE_PAIRS)


def contract_last(left, right):
    return lax.dot_general(
        left, right, (((1,), (1,)), ((), ())), preferred_element_type=jnp.float32
    )


def contract_first(left, right):
    return lax.dot_general(
        left, right, (((0,), (0,)), ((), ())), preferred_element_type=jnp.float32
    )


def matmul(left, right):
    return jnp.dot(left, right, preferred_element_type=jnp.float32)


VMEM = pl.BlockSpec(memory_space=pltpu.VMEM)
SMEM = pl.BlockSpec(memory_space=pltpu.SMEM)
LIMIT = pltpu.CompilerParams(vmem_limit_bytes=16 * 1024 * 1024)


def shape_of(*dims):
    return jax.ShapeDtypeStruct(dims, jnp.bfloat16)


def spots(core):
    return (0, 1 + core, 2 - core, 3)


def weave_kernel(table_ref, own, one, rest, out, turned):
    first = table_ref[8] == 0
    for m in range(3):
        for r in range(2):
            near = one[m, r].astype(jnp.float32)
            back = rest[0, m, r].astype(jnp.float32)
            turned[m, :, r] = own[m, r].astype(jnp.float32)
            turned[m, :, 2 + r] = jnp.where(first, near, back)
            turned[m, :, 4 + r] = jnp.where(first, back, near)
            turned[m, :, 6 + r] = rest[1, m, r].astype(jnp.float32)
    out[...] = turned[...].astype(jnp.bfloat16)


def weave(table, own, one, rest):
    _, _, experts, columns = own.shape
    return pl.pallas_call(
        weave_kernel,
        out_shape=shape_of(3, experts, 8, columns),
        in_specs=[SMEM] + [VMEM] * 3,
        out_specs=VMEM,
        scratch_shapes=[pltpu.VMEM((3, experts, 8, columns), jnp.float32)],
        compiler_params=LIMIT,
        name="weave",
    )(table, own, one, rest)


def unweave_kernel(table_ref, own, came, last, out, one, rest):
    first = table_ref[8] == 0
    for m in range(3):
        total = own[m].astype(jnp.float32) + came[0, m].astype(jnp.float32)
        turned = jnp.swapaxes(total + last[m].astype(jnp.float32), 0, 1)
        left = turned[2:4]
        right = turned[4:6]
        out[m] = turned[0:2]
        one[m] = jnp.where(first, left, right).astype(jnp.bfloat16)
        rest[0, m] = jnp.where(first, right, left).astype(jnp.bfloat16)
        rest[1, m] = turned[6:8].astype(jnp.bfloat16)


def unweave(table, own, came, last):
    _, experts, _, columns = own.shape
    return pl.pallas_call(
        unweave_kernel,
        out_shape=[
            jax.ShapeDtypeStruct((3, 2, experts, columns), jnp.float32),
            shape_of(3, 2, experts, columns),
            shape_of(2, 3, 2, experts, columns),
        ],
        in_specs=[SMEM] + [VMEM] * 3,
        out_specs=[VMEM] * 3,
        compiler_params=LIMIT,
        name="unweave",
    )(table, own, came, last)


def split_kernel(master, *outs):
    for c, out in enumerate(outs):
        out[...] = master[:, 2 * c : 2 * c + 2].astype(jnp.bfloat16)


def split(master):
    parts, _, experts, columns = master.shape
    return pl.pallas_call(
        split_kernel,
        out_shape=[shape_of(parts, 2, experts, columns)] * CHAINS,
        in_specs=[VMEM],
        out_specs=[VMEM] * CHAINS,
        compiler_params=LIMIT,
        name="split",
    )(master)


def pick_kernel(table_ref, kept, one, rest, own, ahead, back):
    spot = spots(table_ref[8])
    for index, out in enumerate((own, ahead.at[0], back, ahead.at[1])):
        for k in range(2):
            e = table_ref[2 * index + k]
            for b, p in enumerate((kept, one, rest.at[0], rest.at[1])):
                out[k, :, spot[b]] = p[:, e]


def pick(table, *plane):
    columns = plane[0].shape[-1]
    return pl.pallas_call(
        pick_kernel,
        out_shape=[shape_of(*lead, 2, 3, 4, 8, columns) for lead in ((), (2,), ())],
        in_specs=[SMEM] + [VMEM] * 3,
        out_specs=[VMEM] * 3,
        compiler_params=LIMIT,
        name="pick",
    )(table, *plane)


def first_kernel(table_ref, tok0, tok1, cot0, cot1, mask, own, came, rest, sums, weights):
    core = table_ref[8]
    columns = own.shape[-1]
    rows = tok0.shape[0]
    for spot, a in zip(spots(core), (own, came.at[0], rest.at[0], rest.at[1])):
        weights[:, :, spot] = a[...]
    half = pl.ds(pl.multiple_of(core * columns, columns), columns)
    w_pair = jnp.concatenate([weights[k, 0:2].reshape(256, columns) for k in range(2)], 0)
    w_down = jnp.concatenate([weights[k, 2].reshape(128, columns) for k in range(2)], 0)
    parts = ((tok0[:, half], cot0[:, half]), (tok1[...], cot1[...]))
    for b, (tok, cot) in enumerate(parts):
        here = slice(rows * b, rows * b + rows)
        chosen = mask[here] > 0.0
        pre = contract_last(tok, w_pair)
        d_hidden = contract_last(cot, w_down)
        sums[0, here] = jnp.where(chosen, pre[:, :128], pre[:, 256:384])
        sums[1, here] = jnp.where(chosen, pre[:, 128:256], pre[:, 384:])
        sums[2, here] = jnp.where(chosen, d_hidden[:, :128], d_hidden[:, 128:])


def first(table, rows_in, mask, arrived):
    columns = arrived[0].shape[-1]
    rows = mask.shape[0]
    return pl.pallas_call(
        first_kernel,
        out_shape=[
            jax.ShapeDtypeStruct((3, rows, 128), jnp.float32),
            shape_of(2, 3, 4, 32, columns),
        ],
        in_specs=[SMEM] + [VMEM] * 8,
        out_specs=[VMEM] * 2,
        compiler_params=pltpu.CompilerParams(vmem_limit_bytes=24 * 1024 * 1024),
        name="first",
    )(table, *rows_in, mask, *arrived)


def second_kernel(
    table_ref, tok0, tok1, cot0, cot1, mask, sums, got, own, ahead, back, hidden, pair, turned
):
    core = table_ref[8]
    columns = own.shape[-1]
    rows = tok0.shape[0]
    step = 256
    for r in range(0, 2 * rows, step):
        here = slice(r, r + step)
        there = slice((r + rows) % (2 * rows), (r + rows) % (2 * rows) + step)
        gate_pre = sums[0, here] + got[0, there]
        up_pre = sums[1, here] + got[1, there]
        d_hidden = sums[2, here] + got[2, there]
        sigmoid_gate = jax.nn.sigmoid(gate_pre)
        act = gate_pre * sigmoid_gate
        d_gate = d_hidden * up_pre * sigmoid_gate * (1.0 + gate_pre * (1.0 - sigmoid_gate))
        three = (d_gate, d_hidden * act, act * up_pre)
        chosen = mask[here] > 0.0
        for k in range(2):
            for m in range(3):
                part = jnp.where(chosen, three[m], 0.0) if k == 0 else jnp.where(chosen, 0.0, three[m])
                part = part.astype(jnp.bfloat16)
                if m < 2:
                    pair[here, 256 * k + 128 * m : 256 * k + 128 * m + 128] = part
                else:
                    hidden[here, 128 * k : 128 * k + 128] = part
                line = 256 * k + 128 * m if m < 2 else 512 + 128 * k
                turned[line : line + 128, here] = part.T
    start = pl.multiple_of(core * columns, columns)
    swapped = core == 1
    for c in range(0, columns, step):
        cols = pl.ds(start + c, step)
        out_cols = slice(c, c + step)
        both = matmul(turned[:512, :rows], tok0[:, cols]) + matmul(
            turned[:512, rows:], tok1[:, out_cols]
        )
        down = matmul(turned[512:, :rows], cot0[:, cols]) + matmul(
            turned[512:, rows:], cot1[:, out_cols]
        )
        for k in range(2):
            for m in range(3):
                line = both[256 * k + 128 * m :][:128] if m < 2 else down[128 * k :][:128]
                line = line.astype(jnp.bfloat16)
                q = [line[32 * i : 32 * i + 32] for i in range(4)]
                own[k, m, :, out_cols] = q[0]
                ahead[0, k, m, :, out_cols] = jnp.where(swapped, q[2], q[1])
                back[k, m, :, out_cols] = jnp.where(swapped, q[1], q[2])
                ahead[1, k, m, :, out_cols] = q[3]


def second(table, rows_in, mask, sums, got, columns):
    rows = mask.shape[0]
    return pl.pallas_call(
        second_kernel,
        out_shape=[shape_of(*lead, 2, 3, 32, columns) for lead in ((), (2,), ())]
        + [shape_of(rows, 256), shape_of(rows, 512)],
        in_specs=[SMEM] + [VMEM] * 7,
        out_specs=[VMEM] * 5,
        scratch_shapes=[pltpu.VMEM((768, rows), jnp.bfloat16)],
        compiler_params=pltpu.CompilerParams(vmem_limit_bytes=24 * 1024 * 1024),
        name="second",
    )(table, *rows_in, mask, sums, got)


def rows_kernel(start, table_ref, *refs):
    hidden, pair, weights = refs[0:3], refs[3:6], refs[6:9]
    added, (layer_out, grad_out) = refs[9:-2], refs[-2:]
    columns = weights[0].shape[-1]
    rows = slice(start, start + layer_out.shape[0])
    step = 512
    if added:
        core = table_ref[8]
        near = pl.multiple_of(core * columns, columns)
        far = pl.ds(pl.multiple_of((1 - core) * columns, columns), columns)
        layer_out[:, far] = added[0][...]
        grad_out[:, far] = added[1][...]
    for c in range(0, columns, step):
        part = slice(c, c + step)
        cols = pl.ds(near + c, step) if added else part
        layer = 0.0
        grad = 0.0
        for chain in range(CHAINS):
            w = weights[chain]
            down = jnp.concatenate([w[k, 2, :, :, part].reshape(128, step) for k in range(2)], 0)
            layer = layer + matmul(hidden[chain][rows], down)
            for k in range(2):
                both = w[k, 0:2, :, :, part].reshape(256, step)
                grad = grad + matmul(pair[chain][rows, 256 * k : 256 * k + 256], both)
        layer_out[:, cols] = layer.astype(jnp.bfloat16)
        grad_out[:, cols] = grad.astype(jnp.bfloat16)


def rows_out(table, hidden, pair, weights, added, start):
    columns = weights[0].shape[-1]
    rows = hidden[0].shape[0] // 2
    return pl.pallas_call(
        functools.partial(rows_kernel, start),
        out_shape=[shape_of(rows, 2 * columns if added else columns)] * 2,
        in_specs=[SMEM] + [VMEM] * (9 + len(added)),
        out_specs=[VMEM] * 2,
        compiler_params=pltpu.CompilerParams(vmem_limit_bytes=24 * 1024 * 1024),
        name="rows_out",
    )(table, *hidden, *pair, *weights, *added)


def merge_kernel(table_ref, kept, came, passed, own, one, rest, total):
    spot = spots(table_ref[8])
    total[...] = jnp.zeros_like(total)
    for index, block in enumerate((kept, came.at[0], passed.at[0], passed.at[1])):
        for k in range(2):
            e = table_ref[2 * index + k]
            for p in range(4):
                total[p, :, e] += block[k, :, p].astype(jnp.float32)
    own[...] = total[0].astype(jnp.bfloat16)
    one[...] = total[spot[1]].astype(jnp.bfloat16)
    rest[0] = total[spot[2]].astype(jnp.bfloat16)
    rest[1] = total[3].astype(jnp.bfloat16)


def merge(table, came, experts):
    columns = came[0].shape[-1]
    return pl.pallas_call(
        merge_kernel,
        out_shape=[shape_of(*lead, 3, experts, 8, columns) for lead in ((), (), (2,))],
        in_specs=[SMEM] + [VMEM] * 3,
        out_specs=[VMEM] * 3,
        scratch_shapes=[pltpu.VMEM((4, 3, experts, 8, columns), jnp.float32)],
        compiler_params=LIMIT,
        name="merge",
    )(table, *[c.reshape(*c.shape[:-2], 4, 8, columns) for c in came])


def shards(tokens, cotangent, row_slot, placement, master, first_moment, second_moment):
    group = lax.axis_index("group")
    core = lax.axis_index("local")
    experts = master.shape[0]
    columns = master.shape[3]
    rows = tokens.shape[0]

    steps = np.array(
        [[[step[c] << SHIFTS[axes[2]] for step in STEPS] for axes in AXES] for c in range(2)], np.int32
    ).reshape(2, -1)
    there = group ^ jnp.where(core == 0, jnp.asarray(steps[0]), jnp.asarray(steps[1]))
    seen = there[:, None] == jnp.arange(SIDE**3)[None]
    pairs = jnp.sum(jnp.where(seen[:, :, None], placement[None], 0), 1)
    pairs = pairs.reshape(CHAINS, 2 * SIDE)
    table = jnp.concatenate([pairs, jnp.full((CHAINS, 1), core)], 1)

    near = [axes[0] for axes in AXES]
    mid = [axes[1] for axes in AXES]
    last = [axes[2] for axes in AXES]
    each = range(CHAINS)
    blocks = split(master.transpose(1, 2, 0, 3))
    ones = [hop(blocks[c], near[c], ONE) for c in each]
    both = [jnp.stack([blocks[c], ones[c]], 0) for c in each]
    rests = [hop(both[c], near[c], BACK) for c in each]
    lines = [weave(table[c], blocks[c], ones[c], rests[c]) for c in each]

    def other_rows(*rows):
        far = (1 - core) * columns
        return [lax.dynamic_slice_in_dim(v, far, columns, 1) for v in rows]

    lines[2], tokens, cotangent, row_slot = lax.optimization_barrier(
        (lines[2], tokens, cotangent, row_slot)
    )
    far_tokens, far_cotangent = other_rows(tokens, cotangent)
    rows_in = [tokens, swap(far_tokens), cotangent, swap(far_cotangent)]
    slots = jnp.concatenate([row_slot, swap(row_slot)], 0)
    chosen = jnp.broadcast_to((slots == 0)[:, None], (2 * rows, 128)).astype(jnp.float32)

    ones = [hop(lines[c], mid[c], ONE) for c in each]
    both = [jnp.stack([lines[c], ones[c]], 0) for c in each]
    rests = [hop(both[c], mid[c], BACK) for c in each]
    rests[0], rows_in, chosen = lax.optimization_barrier((rests[0], rows_in, chosen))
    packed = [pick(table[c], lines[c], ones[c], rests[c]) for c in each]

    def exchange(packed):
        came = [hop(packed[c][1], last[c], ONE) for c in each]
        both = [jnp.stack([packed[c][2], came[c][1]], 0) for c in each]
        return [(packed[c][0], came[c], hop(both[c], last[c], BACK)) for c in each]

    arrived = exchange(packed)
    blocks = [[a.reshape(*a.shape[:-3], 32, columns) for a in arrived[c]] for c in each]
    firsts = [first(table[c], rows_in, chosen, blocks[c]) for c in each]
    got = [swap(f[0]) for f in firsts]
    seconds = [
        second(table[c], rows_in, chosen, firsts[c][0], got[c], columns)
        for c in each
    ]
    weights = [f[1] for f in firsts]
    hidden = [v[3] for v in seconds]
    pair = [v[4] for v in seconds]
    sent = exchange(seconds)
    far_rows = rows_out(table[0], hidden, pair, weights, [], rows)
    sent[1], far_rows = lax.optimization_barrier((sent[1], far_rows))
    merged = [merge(table[c], sent[c], experts) for c in each]

    def add(one, came):
        return (one.astype(jnp.float32) + came[1].astype(jnp.float32)).astype(jnp.bfloat16)

    def scatter(parts, axes):
        came = [hop(parts[c][2], axes[c], BACK) for c in each]
        ones = [add(parts[c][1], came[c]) for c in each]
        return [(parts[c][0], came[c], hop(ones[c], axes[c], ONE)) for c in each]

    layer_out, input_grad = rows_out(
        table[0], hidden, pair, weights, [swap(r) for r in far_rows], 0
    )
    merged = scatter(merged, mid)
    sums = [unweave(table[c], *merged[c]) for c in each]
    parts = [
        own + came[0].astype(jnp.float32) + one.astype(jnp.float32)
        for own, came, one in scatter(sums, near)
    ]

    grads = jnp.concatenate(parts, 1).transpose(2, 0, 1, 3)
    scaled = grads / loss_scale
    new_first = beta_first * first_moment + (1.0 - beta_first) * scaled
    new_second = beta_second * second_moment + (1.0 - beta_second) * scaled * scaled
    new_master = master - learn_rate * (new_first / bias_first) / (
        jnp.sqrt(new_second / bias_second) + adam_epsilon
    )

    return layer_out, input_grad, new_master, new_first, new_second


def solution(mesh):
    state = P(None, None, "group", "local")
    rows = P(("group", "local"), None)
    return jax.shard_map(
        shards,
        mesh=mesh,
        in_specs=(rows, rows, P(("group", "local")), P(), state, state, state),
        out_specs=(rows, rows, state, state, state),
        check_vma=False,
    )
```

```python
import functools
import jax
import jax.numpy as jnp
import numpy as np
from jax import lax
from jax.experimental import pallas as pl
from jax.experimental.pallas import tpu as pltpu
from jax.sharding import PartitionSpec as P

loss_scale = 4.0
beta_first = 0.9
beta_second = 0.95
learn_rate = 0.001
adam_epsilon = 1e-08
bias_first = 1.0 - 0.9**10
bias_second = 1.0 - 0.95**10

SIDE = 4
CHAINS = 3
BOTH = ("group", "local")
SHIFTS = (4, 2, 0)
AXES = ((2, 1, 0), (0, 2, 1), (1, 0, 2))


def place(coords, core):
    return ((coords[0] * SIDE + coords[1]) * SIDE + coords[2]) * 2 + core


def step_pairs(axis, offsets):
    pairs = []
    for group in range(SIDE**3):
        for core in range(2):
            coords = [group // 16, group // 4 % 4, group % 4]
            here = place(coords, core)
            coords[axis] ^= offsets[core]
            pairs.append((here, place(coords, core)))
    return pairs


CORE_PAIRS = [(i, i ^ 1) for i in range(2 * SIDE**3)]
ONE, BACK, ACROSS = (1, 3), (3, 1), (2, 2)
STEPS = ((0, 0), ONE, BACK, ACROSS)


def hop(value, axis, offsets):
    return lax.ppermute(value, BOTH, step_pairs(axis, offsets))


def swap(value):
    return lax.ppermute(value, BOTH, CORE_PAIRS)


def contract_last(left, right):
    return lax.dot_general(
        left, right, (((1,), (1,)), ((), ())), preferred_element_type=jnp.float32
    )


def contract_first(left, right):
    return lax.dot_general(
        left, right, (((0,), (0,)), ((), ())), preferred_element_type=jnp.float32
    )


def matmul(left, right):
    return jnp.dot(left, right, preferred_element_type=jnp.float32)


VMEM = pl.BlockSpec(memory_space=pltpu.VMEM)
SMEM = pl.BlockSpec(memory_space=pltpu.SMEM)
LIMIT = pltpu.CompilerParams(vmem_limit_bytes=16 * 1024 * 1024)


def shape_of(*dims):
    return jax.ShapeDtypeStruct(dims, jnp.bfloat16)


def spots(core):
    return (0, 1 + core, 2 - core, 3)


def weave_kernel(table_ref, own, one, rest, out, turned):
    first = table_ref[8] == 0
    for m in range(3):
        for r in range(2):
            near = one[m, r].astype(jnp.float32)
            back = rest[0, m, r].astype(jnp.float32)
            turned[m, :, r] = own[m, r].astype(jnp.float32)
            turned[m, :, 2 + r] = jnp.where(first, near, back)
            turned[m, :, 4 + r] = jnp.where(first, back, near)
            turned[m, :, 6 + r] = rest[1, m, r].astype(jnp.float32)
    out[...] = turned[...].astype(jnp.bfloat16)


def weave(table, own, one, rest):
    _, _, experts, columns = own.shape
    return pl.pallas_call(
        weave_kernel,
        out_shape=shape_of(3, experts, 8, columns),
        in_specs=[SMEM] + [VMEM] * 3,
        out_specs=VMEM,
        scratch_shapes=[pltpu.VMEM((3, experts, 8, columns), jnp.float32)],
        compiler_params=LIMIT,
        name="weave",
    )(table, own, one, rest)


def unweave_kernel(table_ref, own, came, last, out, one, rest):
    first = table_ref[8] == 0
    for m in range(3):
        total = own[m].astype(jnp.float32) + came[0, m].astype(jnp.float32)
        turned = jnp.swapaxes(total + last[m].astype(jnp.float32), 0, 1)
        left = turned[2:4]
        right = turned[4:6]
        out[m] = turned[0:2]
        one[m] = jnp.where(first, left, right).astype(jnp.bfloat16)
        rest[0, m] = jnp.where(first, right, left).astype(jnp.bfloat16)
        rest[1, m] = turned[6:8].astype(jnp.bfloat16)


def unweave(table, own, came, last):
    _, experts, _, columns = own.shape
    return pl.pallas_call(
        unweave_kernel,
        out_shape=[
            jax.ShapeDtypeStruct((3, 2, experts, columns), jnp.float32),
            shape_of(3, 2, experts, columns),
            shape_of(2, 3, 2, experts, columns),
        ],
        in_specs=[SMEM] + [VMEM] * 3,
        out_specs=[VMEM] * 3,
        compiler_params=LIMIT,
        name="unweave",
    )(table, own, came, last)


def split_kernel(master, *outs):
    for c, out in enumerate(outs):
        out[...] = master[:, 2 * c : 2 * c + 2].astype(jnp.bfloat16)


def split(master):
    parts, _, experts, columns = master.shape
    return pl.pallas_call(
        split_kernel,
        out_shape=[shape_of(parts, 2, experts, columns)] * CHAINS,
        in_specs=[VMEM],
        out_specs=[VMEM] * CHAINS,
        compiler_params=LIMIT,
        name="split",
    )(master)


def pick_kernel(table_ref, kept, one, rest, own, ahead, back):
    spot = spots(table_ref[8])
    for index, out in enumerate((own, ahead.at[0], back, ahead.at[1])):
        for k in range(2):
            e = table_ref[2 * index + k]
            for b, p in enumerate((kept, one, rest.at[0], rest.at[1])):
                out[k, :, spot[b]] = p[:, e]


def pick(table, *plane):
    columns = plane[0].shape[-1]
    return pl.pallas_call(
        pick_kernel,
        out_shape=[shape_of(*lead, 2, 3, 4, 8, columns) for lead in ((), (2,), ())],
        in_specs=[SMEM] + [VMEM] * 3,
        out_specs=[VMEM] * 3,
        compiler_params=LIMIT,
        name="pick",
    )(table, *plane)


def first_kernel(table_ref, tok0, tok1, cot0, cot1, mask, own, came, rest, sums, weights):
    core = table_ref[8]
    columns = own.shape[-1]
    rows = tok0.shape[0]
    for spot, a in zip(spots(core), (own, came.at[0], rest.at[0], rest.at[1])):
        weights[:, :, spot] = a[...]
    half = pl.ds(pl.multiple_of(core * columns, columns), columns)
    w_pair = jnp.concatenate([weights[k, 0:2].reshape(256, columns) for k in range(2)], 0)
    w_down = jnp.concatenate([weights[k, 2].reshape(128, columns) for k in range(2)], 0)
    parts = ((tok0[:, half], cot0[:, half]), (tok1[...], cot1[...]))
    for b, (tok, cot) in enumerate(parts):
        here = slice(rows * b, rows * b + rows)
        chosen = mask[here] > 0.0
        pre = contract_last(tok, w_pair)
        d_hidden = contract_last(cot, w_down)
        sums[0, here] = jnp.where(chosen, pre[:, :128], pre[:, 256:384])
        sums[1, here] = jnp.where(chosen, pre[:, 128:256], pre[:, 384:])
        sums[2, here] = jnp.where(chosen, d_hidden[:, :128], d_hidden[:, 128:])


def first(table, rows_in, mask, arrived):
    columns = arrived[0].shape[-1]
    rows = mask.shape[0]
    return pl.pallas_call(
        first_kernel,
        out_shape=[
            jax.ShapeDtypeStruct((3, rows, 128), jnp.float32),
            shape_of(2, 3, 4, 32, columns),
        ],
        in_specs=[SMEM] + [VMEM] * 8,
        out_specs=[VMEM] * 2,
        compiler_params=pltpu.CompilerParams(vmem_limit_bytes=24 * 1024 * 1024),
        name="first",
    )(table, *rows_in, mask, *arrived)


def second_kernel(
    table_ref, tok0, tok1, cot0, cot1, mask, sums, got, own, ahead, back, hidden, pair, turned
):
    core = table_ref[8]
    columns = own.shape[-1]
    rows = tok0.shape[0]
    step = 256
    for r in range(0, 2 * rows, step):
        here = slice(r, r + step)
        there = slice((r + rows) % (2 * rows), (r + rows) % (2 * rows) + step)
        gate_pre = sums[0, here] + got[0, there]
        up_pre = sums[1, here] + got[1, there]
        d_hidden = sums[2, here] + got[2, there]
        sigmoid_gate = jax.nn.sigmoid(gate_pre)
        act = gate_pre * sigmoid_gate
        d_gate = d_hidden * up_pre * sigmoid_gate * (1.0 + gate_pre * (1.0 - sigmoid_gate))
        three = (d_gate, d_hidden * act, act * up_pre)
        chosen = mask[here] > 0.0
        for k in range(2):
            for m in range(3):
                part = jnp.where(chosen, three[m], 0.0) if k == 0 else jnp.where(chosen, 0.0, three[m])
                part = part.astype(jnp.bfloat16)
                if m < 2:
                    pair[here, 256 * k + 128 * m : 256 * k + 128 * m + 128] = part
                else:
                    hidden[here, 128 * k : 128 * k + 128] = part
                line = 256 * k + 128 * m if m < 2 else 512 + 128 * k
                turned[line : line + 128, here] = part.T
    start = pl.multiple_of(core * columns, columns)
    swapped = core == 1
    for c in range(0, columns, step):
        cols = pl.ds(start + c, step)
        out_cols = slice(c, c + step)
        both = matmul(turned[:512, :rows], tok0[:, cols]) + matmul(
            turned[:512, rows:], tok1[:, out_cols]
        )
        down = matmul(turned[512:, :rows], cot0[:, cols]) + matmul(
            turned[512:, rows:], cot1[:, out_cols]
        )
        for k in range(2):
            for m in range(3):
                line = both[256 * k + 128 * m :][:128] if m < 2 else down[128 * k :][:128]
                line = line.astype(jnp.bfloat16)
                q = [line[32 * i : 32 * i + 32] for i in range(4)]
                own[k, m, :, out_cols] = q[0]
                ahead[0, k, m, :, out_cols] = jnp.where(swapped, q[2], q[1])
                back[k, m, :, out_cols] = jnp.where(swapped, q[1], q[2])
                ahead[1, k, m, :, out_cols] = q[3]


def second(table, rows_in, mask, sums, got, columns):
    rows = mask.shape[0]
    return pl.pallas_call(
        second_kernel,
        out_shape=[shape_of(*lead, 2, 3, 32, columns) for lead in ((), (2,), ())]
        + [shape_of(rows, 256), shape_of(rows, 512)],
        in_specs=[SMEM] + [VMEM] * 7,
        out_specs=[VMEM] * 5,
        scratch_shapes=[pltpu.VMEM((768, rows), jnp.bfloat16)],
        compiler_params=pltpu.CompilerParams(vmem_limit_bytes=24 * 1024 * 1024),
        name="second",
    )(table, *rows_in, mask, sums, got)


def rows_kernel(start, table_ref, *refs):
    hidden, pair, weights = refs[0:3], refs[3:6], refs[6:9]
    columns = weights[0].shape[-1]
    count = hidden[0].shape[0] // 2
    rows = slice(start, start + count)
    step = 512
    copies = []
    if start:
        outs = refs[9:]
        ready = outs
    else:
        got, outs, (ready, sems) = refs[9:11], refs[11:13], refs[13:]
        core = table_ref[8]
        near = pl.multiple_of(core * columns, columns)
        far = pl.ds(pl.multiple_of((1 - core) * columns, columns), columns)
        for i in range(2):
            copies.append(pltpu.make_async_copy(got[i], outs[i].at[:, far], sems.at[i]))
            copies[-1].start()
        ready = [ready.at[i] for i in range(2)]
    for c in range(0, columns, step):
        part = slice(c, c + step)
        layer = 0.0
        grad = 0.0
        for chain in range(CHAINS):
            w = weights[chain]
            down = jnp.concatenate([w[k, 2, :, :, part].reshape(128, step) for k in range(2)], 0)
            layer = layer + matmul(hidden[chain][rows], down)
            for k in range(2):
                both = w[k, 0:2, :, :, part].reshape(256, step)
                grad = grad + matmul(pair[chain][rows, 256 * k : 256 * k + 256], both)
        ready[0][:, part] = layer.astype(jnp.bfloat16)
        ready[1][:, part] = grad.astype(jnp.bfloat16)
        if not start:
            for i in range(2):
                target = outs[i].at[:, pl.ds(near + c, step)]
                sem = sems.at[len(copies)]
                copies.append(pltpu.make_async_copy(ready[i].at[:, part], target, sem))
                copies[-1].start()
    for copy in copies:
        copy.wait()


def rows_out(table, hidden, pair, weights, added, start):
    columns = weights[0].shape[-1]
    rows = hidden[0].shape[0] // 2
    scratch = [pltpu.VMEM((2, rows, columns), jnp.bfloat16), pltpu.SemaphoreType.DMA((6,))]
    return pl.pallas_call(
        functools.partial(rows_kernel, start),
        out_shape=[shape_of(rows, columns if start else 2 * columns)] * 2,
        in_specs=[SMEM] + [VMEM] * (9 + len(added)),
        out_specs=[VMEM if start else pl.BlockSpec(memory_space=pl.ANY)] * 2,
        scratch_shapes=[] if start else scratch,
        compiler_params=pltpu.CompilerParams(vmem_limit_bytes=24 * 1024 * 1024),
        name="rows_out",
    )(table, *hidden, *pair, *weights, *added)


def merge_kernel(table_ref, kept, came, passed, own, one, rest, total):
    spot = spots(table_ref[8])
    total[...] = jnp.zeros_like(total)
    for index, block in enumerate((kept, came.at[0], passed.at[0], passed.at[1])):
        for k in range(2):
            e = table_ref[2 * index + k]
            for p in range(4):
                total[p, :, e] += block[k, :, p].astype(jnp.float32)
    own[...] = total[0].astype(jnp.bfloat16)
    one[...] = total[spot[1]].astype(jnp.bfloat16)
    rest[0] = total[spot[2]].astype(jnp.bfloat16)
    rest[1] = total[3].astype(jnp.bfloat16)


def merge(table, came, experts):
    columns = came[0].shape[-1]
    return pl.pallas_call(
        merge_kernel,
        out_shape=[shape_of(*lead, 3, experts, 8, columns) for lead in ((), (), (2,))],
        in_specs=[SMEM] + [VMEM] * 3,
        out_specs=[VMEM] * 3,
        scratch_shapes=[pltpu.VMEM((4, 3, experts, 8, columns), jnp.float32)],
        compiler_params=LIMIT,
        name="merge",
    )(table, *[c.reshape(*c.shape[:-2], 4, 8, columns) for c in came])


def shards(tokens, cotangent, row_slot, placement, master, first_moment, second_moment):
    group = lax.axis_index("group")
    core = lax.axis_index("local")
    experts = master.shape[0]
    columns = master.shape[3]
    rows = tokens.shape[0]

    near = [axes[0] for axes in AXES]
    mid = [axes[1] for axes in AXES]
    last = [axes[2] for axes in AXES]
    each = range(CHAINS)
    blocks = split(master.transpose(1, 2, 0, 3))
    ones = [hop(blocks[c], near[c], ONE) for c in each]
    both = [jnp.stack([blocks[c], ones[c]], 0) for c in each]
    rests = [hop(both[c], near[c], BACK) for c in each]
    cores = jnp.full((9,), core)
    lines = [weave(cores, blocks[c], ones[c], rests[c]) for c in each]

    def other_rows(*rows):
        far = (1 - core) * columns
        return [lax.dynamic_slice_in_dim(v, far, columns, 1) for v in rows]

    lines[0], tokens, cotangent, row_slot, placement = lax.optimization_barrier(
        (lines[0], tokens, cotangent, row_slot, placement)
    )
    steps = np.array(
        [[[step[c] << SHIFTS[axes[2]] for step in STEPS] for axes in AXES] for c in range(2)], np.int32
    ).reshape(2, -1)
    there = group ^ jnp.where(core == 0, jnp.asarray(steps[0]), jnp.asarray(steps[1]))
    seen = there[:, None] == jnp.arange(SIDE**3)[None]
    pairs = jnp.sum(jnp.where(seen[:, :, None], placement[None], 0), 1)
    pairs = pairs.reshape(CHAINS, 2 * SIDE)
    table = jnp.concatenate([pairs, jnp.full((CHAINS, 1), core)], 1)

    far_tokens, far_cotangent = other_rows(tokens, cotangent)
    rows_in = [tokens, swap(far_tokens), cotangent, swap(far_cotangent)]
    slots = jnp.concatenate([row_slot, swap(row_slot)], 0)
    chosen = jnp.broadcast_to((slots == 0)[:, None], (2 * rows, 128)).astype(jnp.float32)

    ones = [hop(lines[c], mid[c], ONE) for c in each]
    both = [jnp.stack([lines[c], ones[c]], 0) for c in each]
    rests = [hop(both[c], mid[c], BACK) for c in each]
    rests[0], rows_in, chosen = lax.optimization_barrier((rests[0], rows_in, chosen))
    packed = [pick(table[c], lines[c], ones[c], rests[c]) for c in each]

    def exchange(packed):
        came = [hop(packed[c][1], last[c], ONE) for c in each]
        both = [jnp.stack([packed[c][2], came[c][1]], 0) for c in each]
        return [(packed[c][0], came[c], hop(both[c], last[c], BACK)) for c in each]

    arrived = exchange(packed)
    blocks = [[a.reshape(*a.shape[:-3], 32, columns) for a in arrived[c]] for c in each]
    firsts = [first(table[c], rows_in, chosen, blocks[c]) for c in each]
    got = [swap(f[0]) for f in firsts]
    seconds = [
        second(table[c], rows_in, chosen, firsts[c][0], got[c], columns)
        for c in each
    ]
    weights = [f[1] for f in firsts]
    hidden = [v[3] for v in seconds]
    pair = [v[4] for v in seconds]
    sent = exchange(seconds)
    far_rows = rows_out(table[0], hidden, pair, weights, [], rows)
    sent[1], far_rows = lax.optimization_barrier((sent[1], far_rows))
    merged = [merge(table[c], sent[c], experts) for c in each]

    def add(one, came):
        return (one.astype(jnp.float32) + came[1].astype(jnp.float32)).astype(jnp.bfloat16)

    def scatter(parts, axes):
        came = [hop(parts[c][2], axes[c], BACK) for c in each]
        ones = [add(parts[c][1], came[c]) for c in each]
        return [(parts[c][0], came[c], hop(ones[c], axes[c], ONE)) for c in each]

    layer_out, input_grad = rows_out(
        table[0], hidden, pair, weights, [swap(r) for r in far_rows], 0
    )
    merged = scatter(merged, mid)
    sums = [unweave(table[c], *merged[c]) for c in each]
    parts = [
        own + came[0].astype(jnp.float32) + one.astype(jnp.float32)
        for own, came, one in scatter(sums, near)
    ]

    grads = jnp.concatenate(parts, 1).transpose(2, 0, 1, 3)
    scaled = grads / loss_scale
    new_first = beta_first * first_moment + (1.0 - beta_first) * scaled
    new_second = beta_second * second_moment + (1.0 - beta_second) * scaled * scaled
    new_master = master - learn_rate * (new_first / bias_first) / (
        jnp.sqrt(new_second / bias_second) + adam_epsilon
    )

    return layer_out, input_grad, new_master, new_first, new_second


def solution(mesh):
    state = P(None, None, "group", "local")
    rows = P(("group", "local"), None)
    return jax.shard_map(
        shards,
        mesh=mesh,
        in_specs=(rows, rows, P(("group", "local")), P(), state, state, state),
        out_specs=(rows, rows, state, state, state),
        check_vma=False,
    )
```

```python
import functools
import jax
import jax.numpy as jnp
import numpy as np
from jax import lax
from jax.experimental import pallas as pl
from jax.experimental.pallas import tpu as pltpu
from jax.sharding import PartitionSpec as P

loss_scale = 4.0
beta_first = 0.9
beta_second = 0.95
learn_rate = 0.001
adam_epsilon = 1e-08
bias_first = 1.0 - 0.9**10
bias_second = 1.0 - 0.95**10

SIDE = 4
CHAINS = 3
BOTH = ("group", "local")
SHIFTS = (4, 2, 0)
AXES = ((2, 1, 0), (0, 2, 1), (1, 0, 2))


def place(coords, core):
    return ((coords[0] * SIDE + coords[1]) * SIDE + coords[2]) * 2 + core


def step_pairs(axis, offsets):
    pairs = []
    for group in range(SIDE**3):
        for core in range(2):
            coords = [group // 16, group // 4 % 4, group % 4]
            here = place(coords, core)
            coords[axis] ^= offsets[core]
            pairs.append((here, place(coords, core)))
    return pairs


CORE_PAIRS = [(i, i ^ 1) for i in range(2 * SIDE**3)]
ONE, BACK, ACROSS = (1, 3), (3, 1), (2, 2)
STEPS = ((0, 0), ONE, BACK, ACROSS)


def hop(value, axis, offsets):
    return lax.ppermute(value, BOTH, step_pairs(axis, offsets))


def swap(value):
    return lax.ppermute(value, BOTH, CORE_PAIRS)


def contract_last(left, right):
    return lax.dot_general(
        left, right, (((1,), (1,)), ((), ())), preferred_element_type=jnp.float32
    )


def contract_first(left, right):
    return lax.dot_general(
        left, right, (((0,), (0,)), ((), ())), preferred_element_type=jnp.float32
    )


def matmul(left, right):
    return jnp.dot(left, right, preferred_element_type=jnp.float32)


VMEM = pl.BlockSpec(memory_space=pltpu.VMEM)
SMEM = pl.BlockSpec(memory_space=pltpu.SMEM)
LIMIT = pltpu.CompilerParams(vmem_limit_bytes=16 * 1024 * 1024)


def shape_of(*dims):
    return jax.ShapeDtypeStruct(dims, jnp.bfloat16)


def spots(core):
    return (0, 1 + core, 2 - core, 3)


def weave_kernel(table_ref, own, one, rest, out, turned):
    first = table_ref[8] == 0
    for m in range(3):
        for r in range(2):
            near = one[m, r].astype(jnp.float32)
            back = rest[0, m, r].astype(jnp.float32)
            turned[m, :, r] = own[m, r].astype(jnp.float32)
            turned[m, :, 2 + r] = jnp.where(first, near, back)
            turned[m, :, 4 + r] = jnp.where(first, back, near)
            turned[m, :, 6 + r] = rest[1, m, r].astype(jnp.float32)
    out[...] = turned[...].astype(jnp.bfloat16)


def weave(table, own, one, rest):
    _, _, experts, columns = own.shape
    return pl.pallas_call(
        weave_kernel,
        out_shape=shape_of(3, experts, 8, columns),
        in_specs=[SMEM] + [VMEM] * 3,
        out_specs=VMEM,
        scratch_shapes=[pltpu.VMEM((3, experts, 8, columns), jnp.float32)],
        compiler_params=LIMIT,
        name="weave",
    )(table, own, one, rest)


def unweave_kernel(table_ref, own, came, last, out, one, rest):
    first = table_ref[8] == 0
    for m in range(3):
        total = own[m].astype(jnp.float32) + came[0, m].astype(jnp.float32)
        turned = jnp.swapaxes(total + last[m].astype(jnp.float32), 0, 1)
        left = turned[2:4]
        right = turned[4:6]
        out[m] = turned[0:2]
        one[m] = jnp.where(first, left, right).astype(jnp.bfloat16)
        rest[0, m] = jnp.where(first, right, left).astype(jnp.bfloat16)
        rest[1, m] = turned[6:8].astype(jnp.bfloat16)


def unweave(table, own, came, last):
    _, experts, _, columns = own.shape
    return pl.pallas_call(
        unweave_kernel,
        out_shape=[
            jax.ShapeDtypeStruct((3, 2, experts, columns), jnp.float32),
            shape_of(3, 2, experts, columns),
            shape_of(2, 3, 2, experts, columns),
        ],
        in_specs=[SMEM] + [VMEM] * 3,
        out_specs=[VMEM] * 3,
        compiler_params=LIMIT,
        name="unweave",
    )(table, own, came, last)


def split_kernel(master, *outs):
    for c, out in enumerate(outs):
        out[...] = master[:, 2 * c : 2 * c + 2].astype(jnp.bfloat16)


def split(master):
    parts, _, experts, columns = master.shape
    return pl.pallas_call(
        split_kernel,
        out_shape=[shape_of(parts, 2, experts, columns)] * CHAINS,
        in_specs=[VMEM],
        out_specs=[VMEM] * CHAINS,
        compiler_params=LIMIT,
        name="split",
    )(master)


def pick_kernel(table_ref, kept, one, rest, own, ahead, back):
    spot = spots(table_ref[8])
    for index, out in enumerate((own, ahead.at[0], back, ahead.at[1])):
        for k in range(2):
            e = table_ref[2 * index + k]
            for b, p in enumerate((kept, one, rest.at[0], rest.at[1])):
                out[k, :, spot[b]] = p[:, e]


def pick(table, *plane):
    columns = plane[0].shape[-1]
    return pl.pallas_call(
        pick_kernel,
        out_shape=[shape_of(*lead, 2, 3, 4, 8, columns) for lead in ((), (2,), ())],
        in_specs=[SMEM] + [VMEM] * 3,
        out_specs=[VMEM] * 3,
        compiler_params=LIMIT,
        name="pick",
    )(table, *plane)


def first_kernel(table_ref, tok0, tok1, cot0, cot1, mask, own, came, rest, sums, weights):
    core = table_ref[8]
    columns = own.shape[-1]
    rows = tok0.shape[0]
    for spot, a in zip(spots(core), (own, came.at[0], rest.at[0], rest.at[1])):
        weights[:, :, spot] = a[...]
    half = pl.ds(pl.multiple_of(core * columns, columns), columns)
    w_pair = jnp.concatenate([weights[k, 0:2].reshape(256, columns) for k in range(2)], 0)
    w_down = jnp.concatenate([weights[k, 2].reshape(128, columns) for k in range(2)], 0)
    parts = ((tok0[:, half], cot0[:, half]), (tok1[...], cot1[...]))
    for b, (tok, cot) in enumerate(parts):
        here = slice(rows * b, rows * b + rows)
        chosen = mask[here] > 0.0
        pre = contract_last(tok, w_pair)
        d_hidden = contract_last(cot, w_down)
        sums[0, here] = jnp.where(chosen, pre[:, :128], pre[:, 256:384])
        sums[1, here] = jnp.where(chosen, pre[:, 128:256], pre[:, 384:])
        sums[2, here] = jnp.where(chosen, d_hidden[:, :128], d_hidden[:, 128:])


def first(table, rows_in, mask, arrived):
    columns = arrived[0].shape[-1]
    rows = mask.shape[0]
    return pl.pallas_call(
        first_kernel,
        out_shape=[
            jax.ShapeDtypeStruct((3, rows, 128), jnp.float32),
            shape_of(2, 3, 4, 32, columns),
        ],
        in_specs=[SMEM] + [VMEM] * 8,
        out_specs=[VMEM] * 2,
        compiler_params=pltpu.CompilerParams(vmem_limit_bytes=24 * 1024 * 1024),
        name="first",
    )(table, *rows_in, mask, *arrived)


def second_kernel(
    table_ref, tok0, tok1, cot0, cot1, mask, sums, got, own, ahead, back, hidden, pair, turned
):
    core = table_ref[8]
    columns = own.shape[-1]
    rows = tok0.shape[0]
    step = 256
    for r in range(0, 2 * rows, step):
        here = slice(r, r + step)
        there = slice((r + rows) % (2 * rows), (r + rows) % (2 * rows) + step)
        gate_pre = sums[0, here] + got[0, there]
        up_pre = sums[1, here] + got[1, there]
        d_hidden = sums[2, here] + got[2, there]
        sigmoid_gate = jax.nn.sigmoid(gate_pre)
        act = gate_pre * sigmoid_gate
        d_gate = d_hidden * up_pre * sigmoid_gate * (1.0 + gate_pre * (1.0 - sigmoid_gate))
        three = (d_gate, d_hidden * act, act * up_pre)
        chosen = mask[here] > 0.0
        for k in range(2):
            for m in range(3):
                part = jnp.where(chosen, three[m], 0.0) if k == 0 else jnp.where(chosen, 0.0, three[m])
                part = part.astype(jnp.bfloat16)
                if m < 2:
                    pair[here, 256 * k + 128 * m : 256 * k + 128 * m + 128] = part
                else:
                    hidden[here, 128 * k : 128 * k + 128] = part
                line = 256 * k + 128 * m if m < 2 else 512 + 128 * k
                turned[line : line + 128, here] = part.T
    start = pl.multiple_of(core * columns, columns)
    swapped = core == 1
    for c in range(0, columns, step):
        cols = pl.ds(start + c, step)
        out_cols = slice(c, c + step)
        both = matmul(turned[:512, :rows], tok0[:, cols]) + matmul(
            turned[:512, rows:], tok1[:, out_cols]
        )
        down = matmul(turned[512:, :rows], cot0[:, cols]) + matmul(
            turned[512:, rows:], cot1[:, out_cols]
        )
        for k in range(2):
            for m in range(3):
                line = both[256 * k + 128 * m :][:128] if m < 2 else down[128 * k :][:128]
                line = line.astype(jnp.bfloat16)
                q = [line[32 * i : 32 * i + 32] for i in range(4)]
                own[k, m, :, out_cols] = q[0]
                ahead[0, k, m, :, out_cols] = jnp.where(swapped, q[2], q[1])
                back[k, m, :, out_cols] = jnp.where(swapped, q[1], q[2])
                ahead[1, k, m, :, out_cols] = q[3]


def second(table, rows_in, mask, sums, got, columns):
    rows = mask.shape[0]
    return pl.pallas_call(
        second_kernel,
        out_shape=[shape_of(*lead, 2, 3, 32, columns) for lead in ((), (2,), ())]
        + [shape_of(rows, 256), shape_of(rows, 512)],
        in_specs=[SMEM] + [VMEM] * 7,
        out_specs=[VMEM] * 5,
        scratch_shapes=[pltpu.VMEM((768, rows), jnp.bfloat16)],
        compiler_params=pltpu.CompilerParams(vmem_limit_bytes=24 * 1024 * 1024),
        name="second",
    )(table, *rows_in, mask, sums, got)


def rows_kernel(start, table_ref, *refs):
    hidden, pair, weights = refs[0:3], refs[3:6], refs[6:9]
    columns = weights[0].shape[-1]
    count = hidden[0].shape[0] // 2
    rows = slice(start, start + count)
    step = 512
    copies = []
    if start:
        outs = refs[9:]
        ready = outs
    else:
        got, outs, (ready, sems) = refs[9:11], refs[11:13], refs[13:]
        core = table_ref[8]
        near = pl.multiple_of(core * columns, columns)
        far = pl.ds(pl.multiple_of((1 - core) * columns, columns), columns)
        for i in range(2):
            copies.append(pltpu.make_async_copy(got[i], outs[i].at[:, far], sems.at[i]))
            copies[-1].start()
        ready = [ready.at[i] for i in range(2)]
    for c in range(0, columns, step):
        part = slice(c, c + step)
        layer = 0.0
        grad = 0.0
        for chain in range(CHAINS):
            w = weights[chain]
            down = jnp.concatenate([w[k, 2, :, :, part].reshape(128, step) for k in range(2)], 0)
            layer = layer + matmul(hidden[chain][rows], down)
            for k in range(2):
                both = w[k, 0:2, :, :, part].reshape(256, step)
                grad = grad + matmul(pair[chain][rows, 256 * k : 256 * k + 256], both)
        ready[0][:, part] = layer.astype(jnp.bfloat16)
        ready[1][:, part] = grad.astype(jnp.bfloat16)
        if not start:
            for i in range(2):
                target = outs[i].at[:, pl.ds(near + c, step)]
                sem = sems.at[len(copies)]
                copies.append(pltpu.make_async_copy(ready[i].at[:, part], target, sem))
                copies[-1].start()
    for copy in copies:
        copy.wait()


def rows_out(table, hidden, pair, weights, added, start):
    columns = weights[0].shape[-1]
    rows = hidden[0].shape[0] // 2
    scratch = [pltpu.VMEM((2, rows, columns), jnp.bfloat16), pltpu.SemaphoreType.DMA((6,))]
    return pl.pallas_call(
        functools.partial(rows_kernel, start),
        out_shape=[shape_of(rows, columns if start else 2 * columns)] * 2,
        in_specs=[SMEM] + [VMEM] * (9 + len(added)),
        out_specs=[VMEM if start else pl.BlockSpec(memory_space=pl.ANY)] * 2,
        scratch_shapes=[] if start else scratch,
        compiler_params=pltpu.CompilerParams(vmem_limit_bytes=24 * 1024 * 1024),
        name="rows_out",
    )(table, *hidden, *pair, *weights, *added)


def merge_kernel(table_ref, kept, came, passed, own, one, rest, total):
    spot = spots(table_ref[8])
    total[...] = jnp.zeros_like(total)
    for index, block in enumerate((kept, came.at[0], passed.at[0], passed.at[1])):
        for k in range(2):
            e = table_ref[2 * index + k]
            for p in range(4):
                total[p, :, e] += block[k, :, p].astype(jnp.float32)
    own[...] = total[0].astype(jnp.bfloat16)
    one[...] = total[spot[1]].astype(jnp.bfloat16)
    rest[0] = total[spot[2]].astype(jnp.bfloat16)
    rest[1] = total[3].astype(jnp.bfloat16)


def merge(table, came, experts):
    columns = came[0].shape[-1]
    return pl.pallas_call(
        merge_kernel,
        out_shape=[shape_of(*lead, 3, experts, 8, columns) for lead in ((), (), (2,))],
        in_specs=[SMEM] + [VMEM] * 3,
        out_specs=[VMEM] * 3,
        scratch_shapes=[pltpu.VMEM((4, 3, experts, 8, columns), jnp.float32)],
        compiler_params=LIMIT,
        name="merge",
    )(table, *[c.reshape(*c.shape[:-2], 4, 8, columns) for c in came])


def shards(tokens, cotangent, row_slot, placement, master, first_moment, second_moment):
    group = lax.axis_index("group")
    core = lax.axis_index("local")
    experts = master.shape[0]
    columns = master.shape[3]
    rows = tokens.shape[0]

    steps = np.array(
        [[[step[c] << SHIFTS[axes[2]] for step in STEPS] for axes in AXES] for c in range(2)], np.int32
    ).reshape(2, -1)
    there = group ^ jnp.where(core == 0, jnp.asarray(steps[0]), jnp.asarray(steps[1]))
    seen = there[:, None] == jnp.arange(SIDE**3)[None]
    pairs = jnp.sum(jnp.where(seen[:, :, None], placement[None], 0), 1)
    pairs = pairs.reshape(CHAINS, 2 * SIDE)
    table = jnp.concatenate([pairs, jnp.full((CHAINS, 1), core)], 1)

    near = [axes[0] for axes in AXES]
    mid = [axes[1] for axes in AXES]
    last = [axes[2] for axes in AXES]
    each = range(CHAINS)
    blocks = split(master.transpose(1, 2, 0, 3))
    ones = [hop(blocks[c], near[c], ONE) for c in each]
    both = [jnp.stack([blocks[c], ones[c]], 0) for c in each]
    rests = [hop(both[c], near[c], BACK) for c in each]
    lines = [weave(table[c], blocks[c], ones[c], rests[c]) for c in each]

    def other_rows(*rows):
        far = (1 - core) * columns
        return [lax.dynamic_slice_in_dim(v, far, columns, 1) for v in rows]

    lines[2], tokens, cotangent, row_slot = lax.optimization_barrier(
        (lines[2], tokens, cotangent, row_slot)
    )
    far_tokens, far_cotangent = other_rows(tokens, cotangent)
    rows_in = [tokens, swap(far_tokens), cotangent, swap(far_cotangent)]
    slots = jnp.concatenate([row_slot, swap(row_slot)], 0)
    chosen = jnp.broadcast_to((slots == 0)[:, None], (2 * rows, 128)).astype(jnp.float32)

    ones = [hop(lines[c], mid[c], ONE) for c in each]
    both = [jnp.stack([lines[c], ones[c]], 0) for c in each]
    rests = [hop(both[c], mid[c], BACK) for c in each]
    rests[0], rows_in, chosen = lax.optimization_barrier((rests[0], rows_in, chosen))
    packed = [pick(table[c], lines[c], ones[c], rests[c]) for c in each]

    def exchange(packed, also=None):
        came = [hop(packed[c][1], last[c], ONE) for c in each]
        if also is not None:
            came[2], _ = lax.optimization_barrier((came[2], also))
        both = [jnp.stack([packed[c][2], came[c][1]], 0) for c in each]
        return [(packed[c][0], came[c], hop(both[c], last[c], BACK)) for c in each]

    arrived = exchange(packed)
    blocks = [[a.reshape(*a.shape[:-3], 32, columns) for a in arrived[c]] for c in each]
    firsts = [first(table[c], rows_in, chosen, blocks[c]) for c in each]
    got = [swap(f[0]) for f in firsts]
    seconds = [
        second(table[c], rows_in, chosen, firsts[c][0], got[c], columns)
        for c in each
    ]
    weights = [f[1] for f in firsts]
    hidden = [v[3] for v in seconds]
    pair = [v[4] for v in seconds]
    far_rows = rows_out(table[0], hidden, pair, weights, [], rows)
    sent = exchange(seconds, far_rows)
    merged = [merge(table[c], sent[c], experts) for c in each]

    def add(one, came):
        return (one.astype(jnp.float32) + came[1].astype(jnp.float32)).astype(jnp.bfloat16)

    def scatter(parts, axes):
        came = [hop(parts[c][2], axes[c], BACK) for c in each]
        ones = [add(parts[c][1], came[c]) for c in each]
        return [(parts[c][0], came[c], hop(ones[c], axes[c], ONE)) for c in each]

    layer_out, input_grad = rows_out(
        table[0], hidden, pair, weights, [swap(r) for r in far_rows], 0
    )
    merged = scatter(merged, mid)
    sums = [unweave(table[c], *merged[c]) for c in each]
    parts = [
        own + came[0].astype(jnp.float32) + one.astype(jnp.float32)
        for own, came, one in scatter(sums, near)
    ]

    grads = jnp.concatenate(parts, 1).transpose(2, 0, 1, 3)
    scaled = grads / loss_scale
    new_first = beta_first * first_moment + (1.0 - beta_first) * scaled
    new_second = beta_second * second_moment + (1.0 - beta_second) * scaled * scaled
    new_master = master - learn_rate * (new_first / bias_first) / (
        jnp.sqrt(new_second / bias_second) + adam_epsilon
    )

    return layer_out, input_grad, new_master, new_first, new_second


def solution(mesh):
    state = P(None, None, "group", "local")
    rows = P(("group", "local"), None)
    return jax.shard_map(
        shards,
        mesh=mesh,
        in_specs=(rows, rows, P(("group", "local")), P(), state, state, state),
        out_specs=(rows, rows, state, state, state),
        check_vma=False,
    )
```

```python
import functools
import jax
import jax.numpy as jnp
import numpy as np
from jax import lax
from jax.experimental import pallas as pl
from jax.experimental.pallas import tpu as pltpu
from jax.sharding import PartitionSpec as P

loss_scale = 4.0
beta_first = 0.9
beta_second = 0.95
learn_rate = 0.001
adam_epsilon = 1e-08
bias_first = 1.0 - 0.9**10
bias_second = 1.0 - 0.95**10

SIDE = 4
CHAINS = 3
BOTH = ("group", "local")
SHIFTS = (4, 2, 0)
AXES = ((2, 1, 0), (0, 2, 1), (1, 0, 2))


def place(coords, core):
    return ((coords[0] * SIDE + coords[1]) * SIDE + coords[2]) * 2 + core


def step_pairs(axis, offsets):
    pairs = []
    for group in range(SIDE**3):
        for core in range(2):
            coords = [group // 16, group // 4 % 4, group % 4]
            here = place(coords, core)
            coords[axis] ^= offsets[core]
            pairs.append((here, place(coords, core)))
    return pairs


CORE_PAIRS = [(i, i ^ 1) for i in range(2 * SIDE**3)]
ONE, BACK, ACROSS = (1, 3), (3, 1), (2, 2)
STEPS = ((0, 0), ONE, BACK, ACROSS)


def hop(value, axis, offsets):
    return lax.ppermute(value, BOTH, step_pairs(axis, offsets))


def swap(value):
    return lax.ppermute(value, BOTH, CORE_PAIRS)


def contract_last(left, right):
    return lax.dot_general(
        left, right, (((1,), (1,)), ((), ())), preferred_element_type=jnp.float32
    )


def contract_first(left, right):
    return lax.dot_general(
        left, right, (((0,), (0,)), ((), ())), preferred_element_type=jnp.float32
    )


def matmul(left, right):
    return jnp.dot(left, right, preferred_element_type=jnp.float32)


VMEM = pl.BlockSpec(memory_space=pltpu.VMEM)
SMEM = pl.BlockSpec(memory_space=pltpu.SMEM)
LIMIT = pltpu.CompilerParams(vmem_limit_bytes=16 * 1024 * 1024)


def shape_of(*dims):
    return jax.ShapeDtypeStruct(dims, jnp.bfloat16)


def spots(core):
    return (0, 1 + core, 2 - core, 3)


def weave_kernel(table_ref, own, one, rest, out, turned):
    first = table_ref[8] == 0
    for m in range(3):
        for r in range(2):
            near = one[m, r].astype(jnp.float32)
            back = rest[0, m, r].astype(jnp.float32)
            turned[m, :, r] = own[m, r].astype(jnp.float32)
            turned[m, :, 2 + r] = jnp.where(first, near, back)
            turned[m, :, 4 + r] = jnp.where(first, back, near)
            turned[m, :, 6 + r] = rest[1, m, r].astype(jnp.float32)
    out[...] = turned[...].astype(jnp.bfloat16)


def weave(table, own, one, rest):
    _, _, experts, columns = own.shape
    return pl.pallas_call(
        weave_kernel,
        out_shape=shape_of(3, experts, 8, columns),
        in_specs=[SMEM] + [VMEM] * 3,
        out_specs=VMEM,
        scratch_shapes=[pltpu.VMEM((3, experts, 8, columns), jnp.float32)],
        compiler_params=LIMIT,
        name="weave",
    )(table, own, one, rest)


def unweave_kernel(table_ref, own, came, last, out, one, rest):
    first = table_ref[8] == 0
    for m in range(3):
        total = own[m].astype(jnp.float32) + came[0, m].astype(jnp.float32)
        turned = jnp.swapaxes(total + last[m].astype(jnp.float32), 0, 1)
        left = turned[2:4]
        right = turned[4:6]
        out[m] = turned[0:2]
        one[m] = jnp.where(first, left, right).astype(jnp.bfloat16)
        rest[0, m] = jnp.where(first, right, left).astype(jnp.bfloat16)
        rest[1, m] = turned[6:8].astype(jnp.bfloat16)


def unweave(table, own, came, last):
    _, experts, _, columns = own.shape
    return pl.pallas_call(
        unweave_kernel,
        out_shape=[
            jax.ShapeDtypeStruct((3, 2, experts, columns), jnp.float32),
            shape_of(3, 2, experts, columns),
            shape_of(2, 3, 2, experts, columns),
        ],
        in_specs=[SMEM] + [VMEM] * 3,
        out_specs=[VMEM] * 3,
        compiler_params=LIMIT,
        name="unweave",
    )(table, own, came, last)


def split_kernel(master, *outs):
    for c, out in enumerate(outs):
        out[...] = master[:, 2 * c : 2 * c + 2].astype(jnp.bfloat16)


def split(master):
    parts, _, experts, columns = master.shape
    return pl.pallas_call(
        split_kernel,
        out_shape=[shape_of(parts, 2, experts, columns)] * CHAINS,
        in_specs=[VMEM],
        out_specs=[VMEM] * CHAINS,
        compiler_params=LIMIT,
        name="split",
    )(master)


def pick_kernel(table_ref, kept, one, rest, own, ahead, back):
    spot = spots(table_ref[8])
    for index, out in enumerate((own, ahead.at[0], back, ahead.at[1])):
        for k in range(2):
            e = table_ref[2 * index + k]
            for b, p in enumerate((kept, one, rest.at[0], rest.at[1])):
                out[k, :, spot[b]] = p[:, e]


def pick(table, *plane):
    columns = plane[0].shape[-1]
    return pl.pallas_call(
        pick_kernel,
        out_shape=[shape_of(*lead, 2, 3, 4, 8, columns) for lead in ((), (2,), ())],
        in_specs=[SMEM] + [VMEM] * 3,
        out_specs=[VMEM] * 3,
        compiler_params=LIMIT,
        name="pick",
    )(table, *plane)


def first_kernel(table_ref, tok0, tok1, cot0, cot1, mask, own, came, rest, sums, weights):
    core = table_ref[8]
    columns = own.shape[-1]
    rows = tok0.shape[0]
    for spot, a in zip(spots(core), (own, came.at[0], rest.at[0], rest.at[1])):
        weights[:, :, spot] = a[...]
    half = pl.ds(pl.multiple_of(core * columns, columns), columns)
    w_pair = jnp.concatenate([weights[k, 0:2].reshape(256, columns) for k in range(2)], 0)
    w_down = jnp.concatenate([weights[k, 2].reshape(128, columns) for k in range(2)], 0)
    parts = ((tok0[:, half], cot0[:, half]), (tok1[...], cot1[...]))
    for b, (tok, cot) in enumerate(parts):
        here = slice(rows * b, rows * b + rows)
        chosen = mask[here] > 0.0
        pre = contract_last(tok, w_pair)
        d_hidden = contract_last(cot, w_down)
        sums[0, here] = jnp.where(chosen, pre[:, :128], pre[:, 256:384])
        sums[1, here] = jnp.where(chosen, pre[:, 128:256], pre[:, 384:])
        sums[2, here] = jnp.where(chosen, d_hidden[:, :128], d_hidden[:, 128:])


def first(table, rows_in, mask, arrived):
    columns = arrived[0].shape[-1]
    rows = mask.shape[0]
    return pl.pallas_call(
        first_kernel,
        out_shape=[
            jax.ShapeDtypeStruct((3, rows, 128), jnp.float32),
            shape_of(2, 3, 4, 32, columns),
        ],
        in_specs=[SMEM] + [VMEM] * 8,
        out_specs=[VMEM] * 2,
        compiler_params=pltpu.CompilerParams(vmem_limit_bytes=24 * 1024 * 1024),
        name="first",
    )(table, *rows_in, mask, *arrived)


def second_kernel(
    table_ref, tok0, tok1, cot0, cot1, mask, sums, got, own, ahead, back, hidden, pair, turned
):
    core = table_ref[8]
    columns = own.shape[-1]
    rows = tok0.shape[0]
    step = 256
    for r in range(0, 2 * rows, step):
        here = slice(r, r + step)
        there = slice((r + rows) % (2 * rows), (r + rows) % (2 * rows) + step)
        gate_pre = sums[0, here] + got[0, there]
        up_pre = sums[1, here] + got[1, there]
        d_hidden = sums[2, here] + got[2, there]
        sigmoid_gate = jax.nn.sigmoid(gate_pre)
        act = gate_pre * sigmoid_gate
        d_gate = d_hidden * up_pre * sigmoid_gate * (1.0 + gate_pre * (1.0 - sigmoid_gate))
        three = (d_gate, d_hidden * act, act * up_pre)
        chosen = mask[here] > 0.0
        for k in range(2):
            for m in range(3):
                part = jnp.where(chosen, three[m], 0.0) if k == 0 else jnp.where(chosen, 0.0, three[m])
                part = part.astype(jnp.bfloat16)
                if m < 2:
                    pair[here, 256 * k + 128 * m : 256 * k + 128 * m + 128] = part
                else:
                    hidden[here, 128 * k : 128 * k + 128] = part
                line = 256 * k + 128 * m if m < 2 else 512 + 128 * k
                turned[line : line + 128, here] = part.T
    start = pl.multiple_of(core * columns, columns)
    swapped = core == 1
    for c in range(0, columns, step):
        cols = pl.ds(start + c, step)
        out_cols = slice(c, c + step)
        both = matmul(turned[:512, :rows], tok0[:, cols]) + matmul(
            turned[:512, rows:], tok1[:, out_cols]
        )
        down = matmul(turned[512:, :rows], cot0[:, cols]) + matmul(
            turned[512:, rows:], cot1[:, out_cols]
        )
        for k in range(2):
            for m in range(3):
                line = both[256 * k + 128 * m :][:128] if m < 2 else down[128 * k :][:128]
                line = line.astype(jnp.bfloat16)
                q = [line[32 * i : 32 * i + 32] for i in range(4)]
                own[k, m, :, out_cols] = q[0]
                ahead[0, k, m, :, out_cols] = jnp.where(swapped, q[2], q[1])
                back[k, m, :, out_cols] = jnp.where(swapped, q[1], q[2])
                ahead[1, k, m, :, out_cols] = q[3]


def second(table, rows_in, mask, sums, got, columns):
    rows = mask.shape[0]
    return pl.pallas_call(
        second_kernel,
        out_shape=[shape_of(*lead, 2, 3, 32, columns) for lead in ((), (2,), ())]
        + [shape_of(rows, 256), shape_of(rows, 512)],
        in_specs=[SMEM] + [VMEM] * 7,
        out_specs=[VMEM] * 5,
        scratch_shapes=[pltpu.VMEM((768, rows), jnp.bfloat16)],
        compiler_params=pltpu.CompilerParams(vmem_limit_bytes=24 * 1024 * 1024),
        name="second",
    )(table, *rows_in, mask, sums, got)


def rows_kernel(start, table_ref, *refs):
    hidden, pair, weights = refs[0:3], refs[3:6], refs[6:9]
    columns = weights[0].shape[-1]
    count = hidden[0].shape[0] // 2
    rows = slice(start, start + count)
    step = 512
    copies = []
    if start:
        outs = refs[9:]
        ready = outs
    else:
        got, outs, (ready, sems) = refs[9:11], refs[11:13], refs[13:]
        core = table_ref[8]
        near = pl.multiple_of(core * columns, columns)
        far = pl.ds(pl.multiple_of((1 - core) * columns, columns), columns)
        for i in range(2):
            copies.append(pltpu.make_async_copy(got[i], outs[i].at[:, far], sems.at[i]))
            copies[-1].start()
        ready = [ready.at[i] for i in range(2)]
    for c in range(0, columns, step):
        part = slice(c, c + step)
        layer = 0.0
        grad = 0.0
        for chain in range(CHAINS):
            w = weights[chain]
            down = jnp.concatenate([w[k, 2, :, :, part].reshape(128, step) for k in range(2)], 0)
            layer = layer + matmul(hidden[chain][rows], down)
            for k in range(2):
                both = w[k, 0:2, :, :, part].reshape(256, step)
                grad = grad + matmul(pair[chain][rows, 256 * k : 256 * k + 256], both)
        ready[0][:, part] = layer.astype(jnp.bfloat16)
        ready[1][:, part] = grad.astype(jnp.bfloat16)
        if not start:
            for i in range(2):
                target = outs[i].at[:, pl.ds(near + c, step)]
                sem = sems.at[len(copies)]
                copies.append(pltpu.make_async_copy(ready[i].at[:, part], target, sem))
                copies[-1].start()
    for copy in copies:
        copy.wait()


def rows_out(table, hidden, pair, weights, added, start):
    columns = weights[0].shape[-1]
    rows = hidden[0].shape[0] // 2
    scratch = [pltpu.VMEM((2, rows, columns), jnp.bfloat16), pltpu.SemaphoreType.DMA((6,))]
    return pl.pallas_call(
        functools.partial(rows_kernel, start),
        out_shape=[shape_of(rows, columns if start else 2 * columns)] * 2,
        in_specs=[SMEM] + [VMEM] * (9 + len(added)),
        out_specs=[VMEM if start else pl.BlockSpec(memory_space=pl.ANY)] * 2,
        scratch_shapes=[] if start else scratch,
        compiler_params=pltpu.CompilerParams(vmem_limit_bytes=24 * 1024 * 1024),
        name="rows_out",
    )(table, *hidden, *pair, *weights, *added)


def merge_kernel(table_ref, kept, came, passed, own, one, rest, total):
    spot = spots(table_ref[8])
    total[...] = jnp.zeros_like(total)
    for index, block in enumerate((kept, came.at[0], passed.at[0], passed.at[1])):
        for k in range(2):
            e = table_ref[2 * index + k]
            for p in range(4):
                total[p, :, e] += block[k, :, p].astype(jnp.float32)
    own[...] = total[0].astype(jnp.bfloat16)
    one[...] = total[spot[1]].astype(jnp.bfloat16)
    rest[0] = total[spot[2]].astype(jnp.bfloat16)
    rest[1] = total[3].astype(jnp.bfloat16)


def merge(table, came, experts):
    columns = came[0].shape[-1]
    return pl.pallas_call(
        merge_kernel,
        out_shape=[shape_of(*lead, 3, experts, 8, columns) for lead in ((), (), (2,))],
        in_specs=[SMEM] + [VMEM] * 3,
        out_specs=[VMEM] * 3,
        scratch_shapes=[pltpu.VMEM((4, 3, experts, 8, columns), jnp.float32)],
        compiler_params=LIMIT,
        name="merge",
    )(table, *[c.reshape(*c.shape[:-2], 4, 8, columns) for c in came])


def shards(tokens, cotangent, row_slot, placement, master, first_moment, second_moment):
    group = lax.axis_index("group")
    core = lax.axis_index("local")
    experts = master.shape[0]
    columns = master.shape[3]
    rows = tokens.shape[0]

    steps = np.array(
        [[[step[c] << SHIFTS[axes[2]] for step in STEPS] for axes in AXES] for c in range(2)], np.int32
    ).reshape(2, -1)
    there = group ^ jnp.where(core == 0, jnp.asarray(steps[0]), jnp.asarray(steps[1]))
    seen = there[:, None] == jnp.arange(SIDE**3)[None]
    pairs = jnp.sum(jnp.where(seen[:, :, None], placement[None], 0), 1)
    pairs = pairs.reshape(CHAINS, 2 * SIDE)
    table = jnp.concatenate([pairs, jnp.full((CHAINS, 1), core)], 1)

    near = [axes[0] for axes in AXES]
    mid = [axes[1] for axes in AXES]
    last = [axes[2] for axes in AXES]
    each = range(CHAINS)
    blocks = split(master.transpose(1, 2, 0, 3))
    ones = [hop(blocks[c], near[c], ONE) for c in each]
    both = [jnp.stack([blocks[c], ones[c]], 0) for c in each]
    rests = [hop(both[c], near[c], BACK) for c in each]
    lines = [weave(table[c], blocks[c], ones[c], rests[c]) for c in each]

    def other_rows(*rows):
        far = (1 - core) * columns
        return [lax.dynamic_slice_in_dim(v, far, columns, 1) for v in rows]

    lines[2], tokens, cotangent, row_slot = lax.optimization_barrier(
        (lines[2], tokens, cotangent, row_slot)
    )
    far_tokens, far_cotangent = other_rows(tokens, cotangent)
    rows_in = [tokens, swap(far_tokens), cotangent, swap(far_cotangent)]
    slots = jnp.concatenate([row_slot, swap(row_slot)], 0)
    chosen = jnp.broadcast_to((slots == 0)[:, None], (2 * rows, 128)).astype(jnp.float32)

    ones = [hop(lines[c], mid[c], ONE) for c in each]
    both = [jnp.stack([lines[c], ones[c]], 0) for c in each]
    rests = [hop(both[c], mid[c], BACK) for c in each]
    rests[0], rows_in, chosen = lax.optimization_barrier((rests[0], rows_in, chosen))
    packed = [pick(table[c], lines[c], ones[c], rests[c]) for c in each]

    def exchange(packed, also=None):
        came = [hop(packed[c][1], last[c], ONE) for c in each]
        if also is not None:
            came[2], _ = lax.optimization_barrier((came[2], also))
        both = [jnp.stack([packed[c][2], came[c][1]], 0) for c in each]
        return [(packed[c][0], came[c], hop(both[c], last[c], BACK)) for c in each]

    arrived = exchange(packed)
    blocks = [[a.reshape(*a.shape[:-3], 32, columns) for a in arrived[c]] for c in each]
    firsts = [first(table[c], rows_in, chosen, blocks[c]) for c in each]
    got = [swap(f[0]) for f in firsts]
    seconds = [
        second(table[c], rows_in, chosen, firsts[c][0], got[c], columns)
        for c in each
    ]
    weights = [f[1] for f in firsts]
    hidden = [v[3] for v in seconds]
    pair = [v[4] for v in seconds]
    far_rows = rows_out(table[0], hidden, pair, weights, [], rows)
    sent = exchange(seconds, far_rows)
    merged = [merge(table[c], sent[c], experts) for c in each]

    def add(one, came):
        return (one.astype(jnp.float32) + came[1].astype(jnp.float32)).astype(jnp.bfloat16)

    def scatter(parts, axes, *also):
        came = [hop(parts[c][2], axes[c], BACK) for c in each]
        if also:
            came[2], *also = lax.optimization_barrier((came[2], *also))
        ones = [add(parts[c][1], came[c]) for c in each]
        return [(parts[c][0], came[c], hop(ones[c], axes[c], ONE)) for c in each]

    layer_out, input_grad = rows_out(
        table[0], hidden, pair, weights, [swap(r) for r in far_rows], 0
    )
    merged = scatter(merged, mid, layer_out, input_grad)
    sums = [unweave(table[c], *merged[c]) for c in each]
    parts = [
        own + came[0].astype(jnp.float32) + one.astype(jnp.float32)
        for own, came, one in scatter(sums, near)
    ]

    grads = jnp.concatenate(parts, 1).transpose(2, 0, 1, 3)
    scaled = grads / loss_scale
    new_first = beta_first * first_moment + (1.0 - beta_first) * scaled
    new_second = beta_second * second_moment + (1.0 - beta_second) * scaled * scaled
    new_master = master - learn_rate * (new_first / bias_first) / (
        jnp.sqrt(new_second / bias_second) + adam_epsilon
    )

    return layer_out, input_grad, new_master, new_first, new_second


def solution(mesh):
    state = P(None, None, "group", "local")
    rows = P(("group", "local"), None)
    return jax.shard_map(
        shards,
        mesh=mesh,
        in_specs=(rows, rows, P(("group", "local")), P(), state, state, state),
        out_specs=(rows, rows, state, state, state),
        check_vma=False,
    )
```
